32 devices in a mesh: leaf: 8 (over z, y), rows: 4 (over x, core).
Axes of the slice: x: 2, y: 2, z: 4, core: 2. Of those that a mesh axis runs over, the one named last changes fastest.
Arguments:
- mixing: bfloat16 [24, 1024, 1024], P('leaf'), may hold values from 0.04 to 2048
- emission: bfloat16 [24, 256, 1024], P('leaf'), may hold values from 0.099609375 to 10
- prior: float32 [1024], replicated, may hold values from 0.1 to 10
- parent: int32 [24], P('leaf'), may hold values from -1 to 23, as said below
- observed: int32 [24, 512], P('leaf', 'rows'), may hold values from 0 to 255
Outputs:
- pair_counts: bfloat16 [24, 1024, 1024], P('leaf', 'rows')
- emit_counts: bfloat16 [24, 256, 1024], P('leaf', None, 'rows')
The draws below stay inside these ranges and needn't reach their ends.
Inputs may be any that keep to these rules, and one draw needn't show every extreme that they name: Nodes are numbered 3 to an index of leaf, in order. Every parent has a smaller number than its child. A node that is not the first of its index of leaf has its parent among the nodes of the same index. The first node of index d > 0 has as parent the first node of index d with its lowest set binary digit cleared. Node 0 is the root.
All inputs are finite; a program needn't handle non-finite values.
Results may differ from the reference program's by a relative error of at most 0.009.
Values may be sent and summed in bfloat16 or wider, within the bound.
No kernel may reach another device: no remote copies, remote signals or barrier semaphores. Data moves between devices by JAX's collectives and lax.ppermute only.
A program may use at most 128 MiB of HBM per device.

```python
import math
import jax
import jax.numpy as jnp
from jax import lax

K = 1024
V = 256
NODE_DEV = 3
NODES = 24
SAMPLES = 512


def draw_mixing(key, part):
    keys = jax.random.split(jax.random.fold_in(key, 11), NODES)

    def single(node_key):
        first, second = jax.random.split(node_key)
        spread = jnp.exp(jax.random.uniform(first, (K, K), jnp.float32, math.log(0.05), 0.0))
        share = jax.random.uniform(second, (K,), jnp.float32, 0.25, 1.0)
        bump = jnp.sum(spread, axis=1) * share
        return spread + jnp.eye(K, dtype=jnp.float32) * bump[:, None]
    return lax.map(single, keys).astype(jnp.bfloat16)


def draw_parent(key, part):
    index = jnp.arange(NODES, dtype=jnp.int32)
    holder = index // NODE_DEV
    local = index % NODE_DEV
    pick = jax.random.randint(jax.random.fold_in(key, 7), (NODES,), 0, jnp.maximum(local, 1), dtype=jnp.int32)
    inside = holder * NODE_DEV + pick
    upper = jnp.bitwise_and(holder, holder - 1) * NODE_DEV
    return jnp.where(local > 0, inside, jnp.where(holder > 0, upper, -1)).astype(jnp.int32)


def touch_ends(entries, rng, low, largest):
    extent = entries.shape
    spot = [jax.random.randint(jax.random.fold_in(rng, axis), (), 0, extent[axis]) for axis in range(len(extent))]
    entries = entries.at[tuple(spot)].set(low)
    longest = extent.index(max(extent))
    spot[longest] = (spot[longest] + 1) % extent[longest]
    return entries.at[tuple(spot)].set(largest)


def shard_levels(rng, dims, cuts, least, largest):
    def one(position, parts):
        draws = jax.random.uniform(jax.random.fold_in(jax.random.fold_in(rng, 6), position), (parts,), jnp.float32, least / len(cuts), largest / len(cuts))
        return jnp.repeat(jnp.exp(draws), dims[position] // parts).reshape((-1,) + (1,) * (len(dims) - position - 1))

    gain = one(*cuts[0])
    for cut in cuts[1:]:
        gain = gain * one(*cut)
    return gain


def setup_inputs(seed: int = 0) -> dict:
    streams_of = jax.random.split(jax.random.key(seed), 6)
    mixing = draw_mixing(jax.random.fold_in(streams_of[5], 71), 0)
    emission = jnp.clip(jnp.exp(math.log(10.0) - 4.609084 * jax.random.uniform(streams_of[1], (NODES, V, K), jnp.float32) ** shard_levels(streams_of[1], (NODES, V, K), ((0, 8),), -0.2, 0.2)), 0.099609375, 10.0).astype(jnp.bfloat16)
    prior = jnp.clip(jnp.exp(jax.random.uniform(streams_of[2], (K,), jnp.float32, math.log(0.1), math.log(10.0))), 0.1, 10.0)
    parent = draw_parent(jax.random.fold_in(streams_of[5], 71), 0)
    observed = touch_ends(jax.random.randint(streams_of[4], (NODES, SAMPLES), 0, V), jax.random.fold_in(streams_of[4], 1), 0, V - 1).astype(jnp.int32)
    return dict(mixing=mixing, emission=emission, prior=prior, parent=parent, observed=observed)


def node_weights(raw_rows):
    wide = raw_rows.astype(jnp.float32)
    return (wide / jnp.sum(wide, axis=1, keepdims=True)).astype(jnp.bfloat16)


def node_table(raw_table):
    wide = raw_table.astype(jnp.float32)
    return (wide / jnp.sum(wide, axis=0, keepdims=True)).astype(jnp.bfloat16)


def one_hot_rows(values):
    return (values[:, None] == jnp.arange(V, dtype=jnp.int32)[None, :]).astype(jnp.bfloat16)


def outgoing(lam, weight):
    return lax.dot_general(lam, weight, (((1,), (1,)), ((), ())), preferred_element_type=jnp.float32)


def reference(mixing, emission, prior, parent, observed):
    prods = jnp.ones((NODES, SAMPLES, K), jnp.float32)
    lams = jnp.zeros((NODES, SAMPLES, K), jnp.bfloat16)
    root_msg = jnp.ones((SAMPLES, K), jnp.float32)

    def up_step(i, state):
        prods, lams, root_msg = state
        node = (NODES - 1 - i).astype(jnp.int32)
        weight = node_weights(mixing[node])
        hot = one_hot_rows(observed[node])
        emit = jnp.dot(hot, node_table(emission[node]), preferred_element_type=jnp.float32)
        raw = emit * prods[node]
        scale = jnp.mean(raw, axis=1, keepdims=True)
        lam = (raw / scale).astype(jnp.bfloat16)
        msg = outgoing(lam, weight)
        above = parent[node]
        target = jnp.maximum(above, 0).astype(jnp.int32)
        updated = jnp.where(above >= 0, prods[target] * msg, prods[target])
        prods = prods.at[target].set(updated)
        root_msg = jnp.where(above < 0, msg, root_msg)
        lams = lams.at[node].set(lam)
        return prods, lams, root_msg

    prods, lams, root_msg = lax.fori_loop(jnp.int32(0), jnp.int32(NODES), up_step, (prods, lams, root_msg))
    prior_share = prior / jnp.sum(prior)
    weighted = prior_share[None, :] * root_msg
    root_post = weighted / jnp.sum(weighted, axis=1, keepdims=True)
    pair = jnp.zeros((NODES, K, K), jnp.bfloat16)
    emit_c = jnp.zeros((NODES, V, K), jnp.bfloat16)
    pair_scale = K * K / SAMPLES
    emit_scale = V * K / SAMPLES

    def down_step(node, state):
        posts, pair, emit_c = state
        weight = node_weights(mixing[node])
        lam = lams[node]
        msg = outgoing(lam, weight)
        above = parent[node]
        source = jnp.maximum(above, 0).astype(jnp.int32)
        q_par = jnp.where(above >= 0, posts[source], root_post)
        ratio = (q_par / msg).astype(jnp.bfloat16)
        post = lam.astype(jnp.float32) * jnp.dot(ratio, weight, preferred_element_type=jnp.float32)
        posts = posts.at[node].set(post)
        flow = lax.dot_general(ratio, lam, (((0,), (0,)), ((), ())), preferred_element_type=jnp.float32)
        pair = pair.at[node].set((weight.astype(jnp.float32) * flow * pair_scale).astype(jnp.bfloat16))
        hot = one_hot_rows(observed[node])
        tally = lax.dot_general(hot, post.astype(jnp.bfloat16), (((0,), (0,)), ((), ())), preferred_element_type=jnp.float32)
        emit_c = emit_c.at[node].set((tally * emit_scale).astype(jnp.bfloat16))
        return posts, pair, emit_c

    posts, pair, emit_c = lax.fori_loop(jnp.int32(0), jnp.int32(NODES), down_step, (prods, pair, emit_c))
    return pair, emit_c
```

```python
import functools
import jax
import jax.numpy as jnp
from jax import lax
from jax.experimental import pallas as pl
from jax.experimental.pallas import tpu as pltpu
from jax.sharding import PartitionSpec as P

F32 = jnp.float32
BF16 = jnp.bfloat16
ONES = 16
LIMIT = 40 * 2**20
VM = pl.BlockSpec(memory_space=pltpu.VMEM)
SM = pl.BlockSpec(memory_space=pltpu.SMEM)
ANY = pl.BlockSpec(memory_space=pl.ANY)


def vmem(shape, dtype):
    return pltpu.VMEM(shape, dtype)


def run(body, name, ins, specs, outs, scratch=()):
    return pl.pallas_call(
        body,
        name=name,
        in_specs=specs,
        out_specs=tuple(VM for _ in outs),
        out_shape=tuple(outs),
        scratch_shapes=list(scratch),
        compiler_params=pltpu.CompilerParams(vmem_limit_bytes=LIMIT),
    )(*ins)


def scaled(raw):
    return (raw * (1.0 / jnp.mean(raw, axis=1, keepdims=True))).astype(BF16)


def upward(lam, weight):
    rows = lam.shape[0]
    stacked = jnp.concatenate([lam, jnp.ones((ONES, lam.shape[1]), BF16)], axis=0)
    both = lax.dot_general(stacked, weight, (((1,), (1,)), ((), ())), preferred_element_type=F32)
    return both[:rows], both[rows : rows + 1]


def downward(q_par, raw_msg, lam, weight):
    ratio = (q_par / raw_msg).astype(BF16)
    post = lam.astype(F32) * jnp.dot(ratio, weight, preferred_element_type=F32)
    return ratio, post


def prep_body(nodes, slot_ref, obs_ref, emission_hbm, mixing_hbm, w_ref, u_ref, msg_ref, send_ref, lam_refs, prods, tables, sems):
    copies_w = [pltpu.make_async_copy(mixing_hbm.at[n], w_ref.at[n], sems.at[0, n]) for n in range(nodes)]
    copies_e = [pltpu.make_async_copy(emission_hbm.at[n], tables.at[n], sems.at[1, n]) for n in range(nodes)]
    for n in reversed(range(nodes)):
        copies_e[n].start()
    for n in reversed(range(nodes)):
        copies_w[n].start()
    values = tables.shape[1]
    rows = obs_ref.shape[1]
    for n in reversed(range(nodes)):
        copies_e[n].wait()
        hot = (lax.broadcasted_iota(jnp.int32, (values, rows), 0) == obs_ref[n : n + 1, :]).astype(F32).astype(BF16)
        table = tables[n]
        picked = lax.dot_general(hot, table, (((0,), (0,)), ((), ())), preferred_element_type=F32)
        total = jnp.dot(jnp.ones((ONES, values), BF16), table, preferred_element_type=F32)[:1]
        prods[n] = (picked * (1.0 / total)).astype(BF16).astype(F32)
    for n in reversed(range(nodes)):
        copies_w[n].wait()
        raw = prods[n]
        lam = scaled(raw)
        raw_msg, sums = upward(lam, w_ref[n])
        msg = raw_msg * (1.0 / sums)
        if n > 0:
            lam_refs[n - 1][...] = lam
            msg_ref[n - 1] = raw_msg
            slot = slot_ref[n]
            prods[slot] = prods[slot] * msg
        else:
            u_ref[...] = raw
            send_ref[...] = msg.astype(BF16)


def lift_body(level, flag_ref, u_ref, recv_ref, w_ref, u_out, send_ref):
    factor = jnp.where(flag_ref[level] > 0, recv_ref[...].astype(F32), 1.0)
    raw = u_ref[...] * factor
    u_out[...] = raw
    raw_msg, sums = upward(scaled(raw), w_ref[0])
    send_ref[...] = (raw_msg * (1.0 / sums)).astype(BF16)


def root_body(level, flag_ref, u_ref, recv_ref, w_ref, prior_ref, lam_ref, msg_ref, ratio_ref, post_ref):
    factor = jnp.where(flag_ref[level] > 0, recv_ref[...].astype(F32), 1.0)
    lam = scaled(u_ref[...] * factor)
    raw_msg, sums = upward(lam, w_ref[0])
    lam_ref[...] = lam
    msg_ref[...] = raw_msg
    prior = prior_ref[...]
    weighted = (prior / jnp.sum(prior)) * (raw_msg * (1.0 / sums))
    share = weighted / jnp.sum(weighted, axis=1, keepdims=True)
    ratio, post = downward(share, raw_msg, lam, w_ref[0])
    ratio_ref[...] = ratio
    post_ref[...] = post.astype(BF16)


def settle_body(spot, flag_ref, recv_ref, lam_ref, msg_ref, w_ref, ratio_in, post_in, ratio_ref, post_ref):
    got = flag_ref[spot] > 0

    @pl.when(got)
    def _():
        ratio, post = downward(recv_ref[...].astype(F32), msg_ref[...], lam_ref[...], w_ref[0])
        ratio_ref[...] = ratio
        post_ref[...] = post.astype(BF16)

    @pl.when(jnp.logical_not(got))
    def _():
        ratio_ref[...] = ratio_in[...]
        post_ref[...] = post_in[...]


def last_body(nodes, groups, spot, slot_ref, flag_ref, recv_ref, lam_ref, msg_ref, w_ref, ratio_in, post_in, lams_ref, msgs_ref, pack_ref, posts):
    got = flag_ref[spot] > 0
    share = lam_ref.shape[1] // groups

    def pack(item, value):
        for g in range(groups):
            pack_ref[g, item] = value[:, g * share : (g + 1) * share]

    @pl.when(got)
    def _():
        ratio, post = downward(recv_ref[...].astype(F32), msg_ref[...], lam_ref[...], w_ref[0])
        pack(nodes, ratio)
        posts[0] = post.astype(BF16)

    @pl.when(jnp.logical_not(got))
    def _():
        pack(nodes, ratio_in[...])
        posts[0] = post_in[...]

    pack(0, posts[0])
    for n in range(1, nodes):
        q_par = posts[slot_ref[n]].astype(F32)
        _, post = downward(q_par, msgs_ref[n - 1], lams_ref[n - 1][...], w_ref[n])
        posts[n] = post.astype(BF16)
        pack(n, posts[n])


def counts_body(nodes, groups, pair_scale, emit_scale, slot_ref, own_ref, obs_ref, w_ref, lam_refs, own_post_ref, pair_ref, emit_ref):
    share = pair_ref.shape[1]
    values = emit_ref.shape[1]
    start = pl.multiple_of(own_ref[0] * share, share)
    for n in range(nodes):
        weight = w_ref[n, pl.ds(start, share), :]
        lam = lam_refs[n][...]
        if n == 0:
            ratio = jnp.concatenate([own_post_ref[g, nodes] for g in range(groups)], axis=0)
        else:
            raw_msg = lax.dot_general(lam, weight, (((1,), (1,)), ((), ())), preferred_element_type=F32)
            slot = slot_ref[n]
            q_par = jnp.concatenate([own_post_ref[g, slot] for g in range(groups)], axis=0)
            ratio = (q_par.astype(F32) / raw_msg).astype(BF16)
        flow = lax.dot_general(ratio, lam, (((0,), (0,)), ((), ())), preferred_element_type=F32)
        pair_ref[n] = (weight.astype(F32) * flow * pair_scale).astype(BF16)
        rows = obs_ref.shape[2]
        hot = jnp.concatenate(
            [
                (lax.broadcasted_iota(jnp.int32, (values, rows), 0) == obs_ref[g, n : n + 1, :]).astype(F32).astype(BF16)
                for g in range(groups)
            ],
            axis=1,
        )
        post = jnp.concatenate([own_post_ref[g, n] for g in range(groups)], axis=0)
        emit_ref[n] = (jnp.dot(hot, post, preferred_element_type=F32) * emit_scale).astype(BF16)


def per_device(mixing, emission, prior, parent, observed):
    nodes, states = mixing.shape[:2]
    rows = observed.shape[1]
    values = emission.shape[1]
    leaves = lax.axis_size("leaf")
    groups = lax.axis_size("rows")
    levels = leaves.bit_length() - 1
    share = states // groups
    samples = rows * groups
    place = lax.axis_index("leaf")
    slots = jnp.maximum(parent - place * nodes, 0)
    low = [jnp.bitwise_and(place, (2 << level) - 1) for level in range(levels)]
    flags = jnp.stack(
        [low[level] == 0 for level in range(levels)] + [low[level] == (1 << level) for level in range(levels)]
    ).astype(jnp.int32)
    own = lax.axis_index("rows").reshape(1)
    obs_all = lax.all_gather(observed, "rows", axis=0)

    wide = functools.partial(vmem, (rows, states))
    lam_shape = tuple(wide(BF16) for _ in range(nodes - 1))

    def prep(slot_ref, obs_ref, em, mix, w_ref, u_ref, msg_ref, send_ref, *rest):
        prep_body(nodes, slot_ref, obs_ref, em, mix, w_ref, u_ref, msg_ref, send_ref, rest[: nodes - 1], *rest[nodes - 1 :])

    outs = run(
        prep,
        "prep",
        (slots, observed, emission, mixing),
        [SM, VM, ANY, ANY],
        (vmem(mixing.shape, BF16), wide(F32), vmem((nodes - 1, rows, states), F32), wide(BF16)) + lam_shape,
        (
            pltpu.VMEM((nodes, rows, states), F32),
            pltpu.VMEM(emission.shape, BF16),
            pltpu.SemaphoreType.DMA((2, nodes)),
        ),
    )
    weights, raw, msgs, send = outs[:4]
    lams = outs[4:]
    gathered = [lax.all_gather(lam, "rows", axis=0, tiled=True) for lam in lams]

    for level in range(levels):
        step = 1 << level
        pairs = [(s, s - step) for s in range(leaves) if s % (2 * step) == step]
        recv = lax.ppermute(send, "leaf", pairs)
        if level < levels - 1:
            raw, send = run(
                functools.partial(lift_body, level),
                "lift",
                (flags, raw, recv, weights),
                [SM, VM, VM, VM],
                (wide(F32), wide(BF16)),
            )
    lam_top, msg_top, ratio, post = run(
        functools.partial(root_body, levels - 1),
        "root",
        (flags, raw, recv, weights, prior.reshape(1, states)),
        [SM, VM, VM, VM, VM],
        (wide(BF16), wide(F32), wide(BF16), wide(BF16)),
    )
    gathered_top = lax.all_gather(lam_top, "rows", axis=0, tiled=True)
    for level in reversed(range(levels)):
        step = 1 << level
        pairs = [(s - step, s) for s in range(leaves) if s % (2 * step) == step]
        recv = lax.ppermute(post, "leaf", pairs)
        if level > 0:
            ratio, post = run(
                functools.partial(settle_body, levels + level),
                "settle",
                (flags, recv, lam_top, msg_top, weights, ratio, post),
                [SM, VM, VM, VM, VM, VM, VM],
                (wide(BF16), wide(BF16)),
            )

    def last(slot_ref, flag_ref, recv_ref, lam_ref, msg_ref, w_ref, ratio_in, post_in, msgs_ref, *rest):
        last_body(
            nodes, groups, levels, slot_ref, flag_ref, recv_ref, lam_ref, msg_ref, w_ref, ratio_in, post_in,
            rest[: nodes - 1], msgs_ref, *rest[nodes - 1 :],
        )

    (packed,) = run(
        last,
        "last",
        (slots, flags, recv, lam_top, msg_top, weights, ratio, post, msgs) + tuple(lams),
        [SM, SM] + [VM] * (7 + nodes - 1),
        (vmem((groups, nodes + 1, rows, share), BF16),),
        (pltpu.VMEM((nodes, rows, states), BF16),),
    )
    own_posts = lax.all_to_all(packed, "rows", split_axis=0, concat_axis=0, tiled=True)

    def counts(slot_ref, own_ref, obs_ref, w_ref, *rest):
        counts_body(
            nodes, groups, states * states / samples, values * states / samples,
            slot_ref, own_ref, obs_ref, w_ref, rest[:nodes], *rest[nodes:],
        )

    return run(
        counts,
        "counts",
        (slots, own, obs_all, weights, gathered_top) + tuple(gathered) + (own_posts,),
        [SM, SM] + [VM] * (3 + nodes),
        (
            jax.ShapeDtypeStruct((nodes, share, states), BF16),
            jax.ShapeDtypeStruct((nodes, values, share), BF16),
        ),
    )


def solution(mesh):
    placed = (P("leaf", None, None), P("leaf", None, None), P(), P("leaf"), P("leaf", "rows"))
    return jax.shard_map(
        per_device,
        mesh=mesh,
        in_specs=placed,
        out_specs=(P("leaf", "rows", None), P("leaf", None, "rows")),
        check_vma=False,
    )
```

```python
import functools
import jax
import jax.numpy as jnp
from jax import lax
from jax.experimental import pallas as pl
from jax.experimental.pallas import tpu as pltpu
from jax.sharding import PartitionSpec as P

F32 = jnp.float32
BF16 = jnp.bfloat16
PAD = 16
CHUNKS = 2
LIMIT = 24 * 2**20
VM = pl.BlockSpec(memory_space=pltpu.VMEM)
SM = pl.BlockSpec(memory_space=pltpu.SMEM)
ANY = pl.BlockSpec(memory_space=pl.ANY)


def run(body, name, ins, outs, scratch=(), specs=None):
    return pl.pallas_call(
        body,
        name=name,
        in_specs=specs or [VM] * len(ins),
        out_specs=tuple(VM for _ in outs),
        out_shape=tuple(outs),
        scratch_shapes=list(scratch),
        compiler_params=pltpu.CompilerParams(vmem_limit_bytes=LIMIT),
    )(*ins)


def scaled(raw):
    return (raw * (1.0 / jnp.mean(raw, axis=1, keepdims=True))).astype(BF16)


def upward(lam, weight):
    rows = lam.shape[0]
    stacked = jnp.concatenate([lam, jnp.ones((PAD, lam.shape[1]), BF16)], axis=0)
    both = lax.dot_general(stacked, weight, (((1,), (1,)), ((), ())), preferred_element_type=F32)
    return both[:rows], both[rows : rows + 1]


def downward(q_par, raw_msg, lam, weight):
    ratio = (q_par / raw_msg).astype(BF16)
    post = lam.astype(F32) * jnp.dot(ratio, weight, preferred_element_type=F32)
    return ratio, post.astype(BF16)


def one_hot(row, values):
    return (lax.broadcasted_iota(jnp.int32, (values, row.shape[1]), 0) == row).astype(F32).astype(BF16)


def local_slot(parent_ref, node, nodes):
    return jnp.clip(parent_ref[node] - lax.axis_index("leaf") * nodes, 0, node - 1)


def receives_up(level):
    return jnp.bitwise_and(lax.axis_index("leaf"), (2 << level) - 1) == 0


def receives_down(level):
    return jnp.bitwise_and(lax.axis_index("leaf"), (2 << level) - 1) == (1 << level)


def prep_body(nodes, parent_ref, obs_hbm, emission_hbm, mixing_hbm, *refs):
    w_ref, lam_ref, msg_ref = refs[:3]
    u_refs, send_refs = refs[3 : 3 + CHUNKS], refs[3 + CHUNKS : 3 + 2 * CHUNKS]
    prods, tables, obs, sems = refs[3 + 2 * CHUNKS :]
    copy_obs = pltpu.make_async_copy(obs_hbm, obs, sems.at[2, 0])
    copies_w = [pltpu.make_async_copy(mixing_hbm.at[n], w_ref.at[n], sems.at[0, n]) for n in range(nodes)]
    copies_e = [pltpu.make_async_copy(emission_hbm.at[n], tables.at[n], sems.at[1, n]) for n in range(nodes)]
    copy_obs.start()
    for n in reversed(range(nodes)):
        copies_e[n].start()
    for n in reversed(range(nodes)):
        copies_w[n].start()
    values = tables.shape[1]
    rows = obs.shape[1]
    part = rows // CHUNKS
    copy_obs.wait()
    index = lax.broadcasted_iota(jnp.int32, (PAD, rows), 0)
    listed = jnp.zeros((PAD, rows), jnp.int32)
    for n in range(nodes):
        listed = jnp.where(index == n, obs[n : n + 1, :], listed)
    base = (nodes - 1) * rows
    lam_ref[base : base + PAD, :] = jnp.zeros((PAD, lam_ref.shape[1]), BF16)
    lam_ref[base : base + PAD, :rows] = listed.astype(F32).astype(BF16)
    for n in reversed(range(nodes)):
        copies_e[n].wait()
        hot = one_hot(obs[n : n + 1, :], values)
        table = tables[n]
        picked = lax.dot_general(hot, table, (((0,), (0,)), ((), ())), preferred_element_type=F32)
        total = jnp.dot(jnp.ones((PAD, values), BF16), table, preferred_element_type=F32)[:1]
        prods[n] = (picked * (1.0 / total)).astype(BF16).astype(F32)
    for n in reversed(range(nodes)):
        copies_w[n].wait()
        raw = prods[n]
        lam = scaled(raw)
        raw_msg, sums = upward(lam, w_ref[n])
        msg = raw_msg * (1.0 / sums)
        if n > 0:
            lam_ref[(n - 1) * rows : n * rows, :] = lam
            msg_ref[n - 1] = raw_msg
            slot = local_slot(parent_ref, n, nodes)
            prods[slot] = prods[slot] * msg
        else:
            for c in range(CHUNKS):
                u_refs[c][...] = raw[c * part : (c + 1) * part]
                send_refs[c][...] = msg[c * part : (c + 1) * part].astype(BF16)


def lift_body(level, u_ref, recv_ref, w_ref, u_out, send_ref):
    raw = u_ref[...] * jnp.where(receives_up(level), recv_ref[...].astype(F32), 1.0)
    u_out[...] = raw
    raw_msg, sums = upward(scaled(raw), w_ref[0])
    send_ref[...] = (raw_msg * (1.0 / sums)).astype(BF16)


def root_body(level, u_ref, recv_ref, w_ref, prior_ref, *refs):
    lam_ref, msg_ref, ratio_ref, post_ref = refs[-5:-1] if len(refs) > 4 else refs
    lam = scaled(u_ref[...] * jnp.where(receives_up(level), recv_ref[...].astype(F32), 1.0))
    raw_msg, sums = upward(lam, w_ref[0])
    lam_ref[...] = lam
    if len(refs) > 4:
        for c, block in enumerate([item[...] for item in refs[:-5]] + [lam]):
            refs[-1][c * lam.shape[0] : (c + 1) * lam.shape[0], :] = block
    msg_ref[...] = raw_msg
    prior = prior_ref[...]
    weighted = (prior / jnp.sum(prior)) * (raw_msg * (1.0 / sums))
    share = weighted / jnp.sum(weighted, axis=1, keepdims=True)
    ratio, post = downward(share, raw_msg, lam, w_ref[0])
    ratio_ref[...] = ratio
    post_ref[...] = post


def settle_body(level, recv_ref, lam_ref, msg_ref, w_ref, ratio_in, post_in, ratio_ref, post_ref):
    got = receives_down(level)

    @pl.when(got)
    def _():
        ratio, post = downward(recv_ref[...].astype(F32), msg_ref[...], lam_ref[...], w_ref[0])
        ratio_ref[...] = ratio
        post_ref[...] = post

    @pl.when(jnp.logical_not(got))
    def _():
        ratio_ref[...] = ratio_in[...]
        post_ref[...] = post_in[...]


def last_body(nodes, groups, chunk, parent_ref, recv_ref, lam_ref, msg_ref, w_ref, ratio_in, post_in, lams_ref, msgs_ref, *refs):
    packs, posts = refs[:groups], refs[groups]
    rows, part = msgs_ref.shape[1], lam_ref.shape[0]
    share = lam_ref.shape[1] // groups
    got = receives_down(0)

    @pl.when(got)
    def _():
        ratio, post = downward(recv_ref[...].astype(F32), msg_ref[...], lam_ref[...], w_ref[0])
        posts[nodes] = ratio
        posts[0] = post

    @pl.when(jnp.logical_not(got))
    def _():
        posts[nodes] = ratio_in[...]
        posts[0] = post_in[...]

    for n in range(1, nodes):
        q_par = posts[local_slot(parent_ref, n, nodes)].astype(F32)
        low = (n - 1) * rows + chunk * part
        raw_msg = msgs_ref[n - 1, chunk * part : (chunk + 1) * part, :]
        _, posts[n] = downward(q_par, raw_msg, lams_ref[low : low + part, :], w_ref[n])
    own = lax.axis_index("rows")
    for mask in range(groups):
        start = pl.multiple_of(jnp.bitwise_xor(own, mask) * share, share)
        packs[mask][...] = posts[:, :, pl.ds(start, share)]


def ready_body(nodes, groups, w_ref, *refs):
    lams, (raw_ref, hot_ref) = refs[:groups], refs[groups:]
    chunks, merged, share = raw_ref.shape[1:]
    part = merged // groups
    rows = part * chunks
    values = hot_ref.shape[2]
    base = (nodes - 1) * rows
    start = pl.multiple_of(lax.axis_index("rows") * share, share)
    for n in range(nodes):
        observed = [lam[base : base + PAD, :rows].astype(F32).astype(jnp.int32)[n : n + 1] for lam in lams]
        for c in range(chunks):
            row = jnp.concatenate([item[:, c * part : (c + 1) * part] for item in observed], axis=1)
            hot_ref[n, c] = one_hot(row, values)
        if n > 0:
            weight = w_ref[n, pl.ds(start, share), :]
            for c in range(chunks):
                low = (n - 1) * rows + c * part
                lam = jnp.concatenate([item[low : low + part, :] for item in lams], axis=0)
                raw_ref[n - 1, c] = lax.dot_general(lam, weight, (((1,), (1,)), ((), ())), preferred_element_type=F32)


def counts_body(nodes, groups, chunk, parent_ref, raw_ref, hot_ref, *refs):
    lams, tops, posts = refs[:groups], refs[groups : 2 * groups], refs[2 * groups : 3 * groups]
    refs = refs[3 * groups :]
    chunks = raw_ref.shape[1]
    part = raw_ref.shape[2] // groups
    rows = part * chunks
    before = refs[:2] if chunk > 0 else None
    refs = refs[2:] if chunk > 0 else refs
    final = chunk == chunks - 1
    if final:
        w_ref, refs = refs[0], refs[1:]
        share = refs[0].shape[1]
        samples = rows * groups
        start = pl.multiple_of(lax.axis_index("rows") * share, share)
    for n in range(nodes):
        low = (n - 1) * rows + chunk * part if n > 0 else chunk * part
        lam = jnp.concatenate([item[low : low + part, :] for item in (lams if n > 0 else tops)], axis=0)
        if n == 0:
            ratio = jnp.concatenate([item[nodes] for item in posts], axis=0)
        else:
            slot = local_slot(parent_ref, n, nodes)
            q_par = jnp.concatenate([item[slot] for item in posts], axis=0)
            ratio = (q_par.astype(F32) / raw_ref[n - 1, chunk]).astype(BF16)
        flow = lax.dot_general(ratio, lam, (((0,), (0,)), ((), ())), preferred_element_type=F32)
        post = jnp.concatenate([item[n] for item in posts], axis=0)
        tally = jnp.dot(hot_ref[n, chunk], post, preferred_element_type=F32)
        if before is not None:
            flow += before[0][n]
            tally += before[1][n]
        if final:
            states, values = flow.shape[1], tally.shape[0]
            weight = w_ref[n, pl.ds(start, share), :].astype(F32)
            flow = weight * flow * (states * states / samples)
            tally = tally * (values * states / samples)
        refs[0][n] = flow.astype(refs[0].dtype)
        refs[1][n] = tally.astype(refs[1].dtype)


def swap(value, mask):
    return lax.ppermute(value, "rows", [(s, s ^ mask) for s in range(lax.axis_size("rows"))])


def gather(value):
    blocks = {0: value}
    for bit in reversed(range(lax.axis_size("rows").bit_length() - 1)):
        blocks.update({place | (1 << bit): swap(block, 1 << bit) for place, block in blocks.items()})
    return [blocks[place] for place in range(len(blocks))]


def per_device(mixing, emission, prior, parent, observed):
    nodes, states = mixing.shape[:2]
    rows = observed.shape[1]
    values = emission.shape[1]
    leaves = lax.axis_size("leaf")
    groups = lax.axis_size("rows")
    levels = leaves.bit_length() - 1
    share = states // groups
    part = rows // CHUNKS
    every = range(CHUNKS)
    half = functools.partial(pltpu.VMEM, (part, states))

    outs = run(
        functools.partial(prep_body, nodes),
        "prep",
        (parent,) + tuple(pltpu.with_memory_space_constraint(x, pltpu.HBM) for x in (observed, emission, mixing)),
        (
            pltpu.VMEM(mixing.shape, BF16),
            pltpu.VMEM(((nodes - 1) * rows + PAD, states), BF16),
            pltpu.VMEM((nodes - 1, rows, states), F32),
        )
        + (half(F32),) * CHUNKS
        + (half(BF16),) * CHUNKS,
        (
            pltpu.VMEM((nodes, rows, states), F32),
            pltpu.VMEM(emission.shape, BF16),
            pltpu.VMEM(observed.shape, jnp.int32),
            pltpu.SemaphoreType.DMA((3, nodes)),
        ),
        [SM, ANY, ANY, ANY],
    )
    weights, lams, msgs = outs[:3]
    raw, send = list(outs[3 : 3 + CHUNKS]), list(outs[3 + CHUNKS :])

    def up_pairs(level):
        step = 1 << level
        return [(s, s - step) for s in range(leaves) if s % (2 * step) == step]

    def down_pairs(level):
        return [(b, a) for a, b in up_pairs(level)]

    for level in range(levels - 1):
        for c in every:
            recv = lax.ppermute(send[c], "leaf", up_pairs(level))
            raw[c], send[c] = run(
                functools.partial(lift_body, level), "lift", (raw[c], recv, weights), (half(F32), half(BF16))
            )
        if level == 0:
            all_lams = gather(lams)
    top_lam, top_msg, ratio, post = ([None] * CHUNKS for _ in range(4))
    for c in every:
        recv = lax.ppermute(send[c], "leaf", up_pairs(levels - 1))
        final = c == CHUNKS - 1
        top_lam[c], top_msg[c], ratio[c], post[c], *merged = run(
            functools.partial(root_body, levels - 1),
            "root",
            (raw[c], recv, weights, prior.reshape(1, states)) + (tuple(top_lam[:c]) if final else ()),
            (half(BF16), half(F32), half(BF16), half(BF16)) + ((pltpu.VMEM((rows, states), BF16),) if final else ()),
        )
    all_tops = gather(merged[0])
    for level in reversed(range(1, levels)):
        for c in every:
            recv = lax.ppermute(post[c], "leaf", down_pairs(level))
            ratio[c], post[c] = run(
                functools.partial(settle_body, level),
                "settle",
                (recv, top_lam[c], top_msg[c], weights, ratio[c], post[c]),
                (half(BF16), half(BF16)),
            )
    raw_own, hots = run(
        functools.partial(ready_body, nodes, groups),
        "ready",
        (weights, *all_lams),
        (
            pltpu.VMEM((nodes - 1, CHUNKS, groups * part, share), F32),
            pltpu.VMEM((nodes, CHUNKS, values, groups * part), BF16),
        ),
    )
    own_posts = []
    for c in every:
        recv = lax.ppermute(post[c], "leaf", down_pairs(0))
        packs = run(
            functools.partial(last_body, nodes, groups, c),
            "last",
            (parent, recv, top_lam[c], top_msg[c], weights, ratio[c], post[c], lams, msgs),
            (pltpu.VMEM((nodes + 1, part, share), BF16),) * groups,
            (pltpu.VMEM((nodes + 1, part, states), BF16),),
            [SM] + [VM] * 8,
        )
        order = sorted(range(1, groups), reverse=True)
        moved = {mask: swap(packs[mask], mask) for mask in order}
        own_posts.append([packs[0]] + [moved[mask] for mask in range(1, groups)])
    sums = ()
    for c in every:
        final = c == CHUNKS - 1
        kinds = (
            (jax.ShapeDtypeStruct, BF16) if final else (pltpu.VMEM, F32)
        )
        ins = (parent, raw_own, hots, *all_lams, *all_tops, *own_posts[c])
        ins += tuple(sums) + ((weights,) if final else ())
        sums = run(
            functools.partial(counts_body, nodes, groups, c),
            "counts",
            ins,
            (kinds[0]((nodes, share, states), kinds[1]), kinds[0]((nodes, values, share), kinds[1])),
            (),
            [SM] + [VM] * (len(ins) - 1),
        )
    return tuple(sums)


def solution(mesh):
    placed = (P("leaf", None, None), P("leaf", None, None), P(), P("leaf"), P("leaf", "rows"))
    return jax.shard_map(
        per_device,
        mesh=mesh,
        in_specs=placed,
        out_specs=(P("leaf", "rows", None), P("leaf", None, "rows")),
        check_vma=False,
    )
```

```python
import functools
import jax
import jax.numpy as jnp
from jax import lax
from jax.experimental import pallas as pl
from jax.experimental.pallas import tpu as pltpu
from jax.sharding import PartitionSpec as P

F32 = jnp.float32
BF16 = jnp.bfloat16
PAD = 16
CHUNKS = 2
LIMIT = 24 * 2**20
VM = pl.BlockSpec(memory_space=pltpu.VMEM)
SM = pl.BlockSpec(memory_space=pltpu.SMEM)
ANY = pl.BlockSpec(memory_space=pl.ANY)


def run(body, name, ins, outs, scratch=(), specs=None, out_specs=None, same=None):
    return pl.pallas_call(
        body,
        name=name,
        in_specs=specs or [VM] * len(ins),
        out_specs=out_specs or tuple(VM for _ in outs),
        out_shape=tuple(outs),
        input_output_aliases=same or {},
        scratch_shapes=list(scratch),
        compiler_params=pltpu.CompilerParams(vmem_limit_bytes=LIMIT),
    )(*ins)


def scaled(raw):
    return (raw * (1.0 / jnp.mean(raw, axis=1, keepdims=True))).astype(BF16)


def upward(lam, weight):
    rows = lam.shape[0]
    stacked = jnp.concatenate([lam, jnp.ones((PAD, lam.shape[1]), BF16)], axis=0)
    both = lax.dot_general(stacked, weight, (((1,), (1,)), ((), ())), preferred_element_type=F32)
    return both[:rows], both[rows : rows + 1]


def downward(q_par, raw_msg, lam, weight):
    ratio = (q_par / raw_msg).astype(BF16)
    post = lam.astype(F32) * jnp.dot(ratio, weight, preferred_element_type=F32)
    return ratio, post.astype(BF16)


def one_hot(row, values):
    return (lax.broadcasted_iota(jnp.int32, (values, row.shape[1]), 0) == row).astype(F32).astype(BF16)


def local_slot(parent_ref, node, nodes):
    return jnp.clip(parent_ref[node] - lax.axis_index("leaf") * nodes, 0, node - 1)


def is_upper(level):
    return jnp.bitwise_and(lax.axis_index("leaf"), (2 << level) - 1) == 0


def is_lower(level):
    return jnp.bitwise_and(lax.axis_index("leaf"), (2 << level) - 1) == (1 << level)


def prep_body(nodes, parent_hbm, obs_hbm, emission_hbm, mixing_hbm, *refs):
    w_ref, lam_ref, msg_ref = refs[:3]
    u_refs = refs[3 : 3 + CHUNKS]
    prods, tables, obs, parent_ref, sems = refs[3 + CHUNKS :]
    copy_obs = pltpu.make_async_copy(obs_hbm, obs, sems.at[2, 0])
    copy_parent = pltpu.make_async_copy(parent_hbm, parent_ref, sems.at[2, 1])
    copies_w = [pltpu.make_async_copy(mixing_hbm.at[n], w_ref.at[n], sems.at[0, n]) for n in range(nodes)]
    copies_e = [pltpu.make_async_copy(emission_hbm.at[n], tables.at[n], sems.at[1, n]) for n in range(nodes)]
    copy_obs.start()
    copy_parent.start()
    for n in reversed(range(nodes)):
        copies_e[n].start()
        copies_w[n].start()
    values = tables.shape[1]
    rows = obs.shape[1]
    part = rows // CHUNKS
    for n in range(nodes - 1):
        prods[n] = jnp.ones(prods.shape[1:], F32)
    copy_obs.wait()
    index = lax.broadcasted_iota(jnp.int32, (PAD, rows), 0)
    listed = jnp.zeros((PAD, rows), jnp.int32)
    for n in range(nodes):
        listed = jnp.where(index == n, obs[n : n + 1, :], listed)
    base = (nodes - 1) * rows
    lam_ref[base : base + PAD, :] = jnp.zeros((PAD, lam_ref.shape[1]), BF16)
    lam_ref[base : base + PAD, :rows] = listed.astype(F32).astype(BF16)
    copy_parent.wait()
    for n in reversed(range(nodes)):
        copies_e[n].wait()
        hot = one_hot(obs[n : n + 1, :], values)
        table = tables[n]
        picked = lax.dot_general(hot, table, (((0,), (0,)), ((), ())), preferred_element_type=F32)
        total = jnp.dot(jnp.ones((PAD, values), BF16), table, preferred_element_type=F32)[:1]
        raw = (picked * (1.0 / total)).astype(BF16).astype(F32)
        if n < nodes - 1:
            raw = raw * prods[n]
        if n > 0:
            lam = scaled(raw)
            copies_w[n].wait()
            raw_msg, sums = upward(lam, w_ref[n])
            lam_ref[(n - 1) * rows : n * rows, :] = lam
            msg_ref[n - 1] = raw_msg
            slot = local_slot(parent_ref, n, nodes)
            prods[slot] = prods[slot] * (raw_msg * (1.0 / sums))
        else:
            for c in range(CHUNKS):
                u_refs[c][...] = raw[c * part : (c + 1) * part]
    copies_w[0].wait()


def send_up(level, raw_ref, w_ref, send_ref):
    @pl.when(is_lower(level))
    def _():
        raw_msg, sums = upward(scaled(raw_ref[...]), w_ref[0])
        send_ref[...] = (raw_msg * (1.0 / sums)).astype(BF16)


def first_body(u_ref, w_ref, *refs):
    send_up(0, u_ref, w_ref, refs[-1])


def lift_body(level, u_ref, recv_ref, w_ref, *refs):
    u_out, send_ref = refs[-3:-1] if len(refs) > 2 else refs

    @pl.when(is_upper(level))
    def _():
        u_out[...] = u_ref[...] * recv_ref[...].astype(F32)

    send_up(level + 1, u_out, w_ref, send_ref)


def root_body(level, u_ref, recv_ref, w_ref, prior_ref, *refs):
    lam_ref, msg_ref, ratio_ref, post_ref = refs[-5:-1] if len(refs) > 4 else refs
    lam = scaled(u_ref[...] * jnp.where(is_upper(level), recv_ref[...].astype(F32), 1.0))
    raw_msg, sums = upward(lam, w_ref[0])
    lam_ref[...] = lam
    msg_ref[...] = raw_msg
    if len(refs) > 4:
        for c, block in enumerate([item[...] for item in refs[:-5]] + [lam]):
            refs[-1][c * lam.shape[0] : (c + 1) * lam.shape[0], :] = block

    @pl.when(lax.axis_index("leaf") == 0)
    def _():
        prior = prior_ref[...]
        weighted = (prior / jnp.sum(prior)) * (raw_msg * (1.0 / sums))
        share = weighted / jnp.sum(weighted, axis=1, keepdims=True)
        ratio, post = downward(share, raw_msg, lam, w_ref[0])
        ratio_ref[...] = ratio
        post_ref[...] = post


def settle_body(level, recv_ref, lam_ref, msg_ref, w_ref, ratio_in, post_in, ratio_ref, post_ref):
    got = is_lower(level)

    @pl.when(got)
    def _():
        ratio, post = downward(recv_ref[...].astype(F32), msg_ref[...], lam_ref[...], w_ref[0])
        ratio_ref[...] = ratio
        post_ref[...] = post

    @pl.when(jnp.logical_not(got))
    def _():
        ratio_ref[...] = ratio_in[...]
        post_ref[...] = post_in[...]


def last_body(nodes, groups, chunk, parent_ref, recv_ref, lam_ref, msg_ref, w_ref, ratio_in, post_in, lams_ref, msgs_ref, _, *refs):
    packs, posts = refs[:groups], refs[groups]
    rows, part = msgs_ref.shape[1], lam_ref.shape[0]
    share = lam_ref.shape[1] // groups
    got = is_lower(0)

    @pl.when(got)
    def _():
        ratio, post = downward(recv_ref[...].astype(F32), msg_ref[...], lam_ref[...], w_ref[0])
        posts[nodes] = ratio
        posts[0] = post

    @pl.when(jnp.logical_not(got))
    def _():
        posts[nodes] = ratio_in[...]
        posts[0] = post_in[...]

    for n in range(1, nodes):
        q_par = posts[local_slot(parent_ref, n, nodes)].astype(F32)
        low = (n - 1) * rows + chunk * part
        raw_msg = msgs_ref[n - 1, chunk * part : (chunk + 1) * part, :]
        _, posts[n] = downward(q_par, raw_msg, lams_ref[low : low + part, :], w_ref[n])
    own = lax.axis_index("rows")
    for mask in range(groups):
        start = pl.multiple_of(jnp.bitwise_xor(own, mask) * share, share)
        packs[mask][...] = posts[:, :, pl.ds(start, share)]


def ready_body(nodes, groups, w_ref, *refs):
    lams, (raw_ref, hot_ref) = refs[:groups], refs[groups:]
    chunks, merged, share = raw_ref.shape[1:]
    part = merged // groups
    rows = part * chunks
    values = hot_ref.shape[2]
    base = (nodes - 1) * rows
    start = pl.multiple_of(lax.axis_index("rows") * share, share)
    for n in range(nodes):
        observed = [lam[base : base + PAD, :rows].astype(F32).astype(jnp.int32)[n : n + 1] for lam in lams]
        for c in range(chunks):
            row = jnp.concatenate([item[:, c * part : (c + 1) * part] for item in observed], axis=1)
            hot_ref[n, c] = one_hot(row, values)
        if n > 0:
            weight = w_ref[n, pl.ds(start, share), :]
            for c in range(chunks):
                low = (n - 1) * rows + c * part
                lam = jnp.concatenate([item[low : low + part, :] for item in lams], axis=0)
                raw_ref[n - 1, c] = lax.dot_general(lam, weight, (((1,), (1,)), ((), ())), preferred_element_type=F32)


def counts_body(nodes, groups, chunk, parent_ref, raw_ref, hot_ref, *refs):
    lams, tops, posts = refs[:groups], refs[groups : 2 * groups], refs[2 * groups : 3 * groups]
    refs = refs[3 * groups :]
    chunks = raw_ref.shape[1]
    part = raw_ref.shape[2] // groups
    rows = part * chunks
    before = refs[:2] if chunk > 0 else None
    refs = refs[2:] if chunk > 0 else refs
    final = chunk == chunks - 1
    copies = []
    if final:
        w_ref, homes, refs, sems = refs[0], refs[1:3], refs[3:5], refs[5]
        share = refs[0].shape[1]
        samples = rows * groups
        start = pl.multiple_of(lax.axis_index("rows") * share, share)
    for n in range(nodes):
        low = (n - 1) * rows + chunk * part if n > 0 else chunk * part
        lam = jnp.concatenate([item[low : low + part, :] for item in (lams if n > 0 else tops)], axis=0)
        if n == 0:
            ratio = jnp.concatenate([item[nodes] for item in posts], axis=0)
        else:
            slot = local_slot(parent_ref, n, nodes)
            q_par = jnp.concatenate([item[slot] for item in posts], axis=0)
            ratio = (q_par.astype(F32) / raw_ref[n - 1, chunk]).astype(BF16)
        flow = lax.dot_general(ratio, lam, (((0,), (0,)), ((), ())), preferred_element_type=F32)
        post = jnp.concatenate([item[n] for item in posts], axis=0)
        tally = jnp.dot(hot_ref[n, chunk], post, preferred_element_type=F32)
        if before is not None:
            flow += before[0][n]
            tally += before[1][n]
        if final:
            states, values = flow.shape[1], tally.shape[0]
            weight = w_ref[n, pl.ds(start, share), :].astype(F32)
            flow = weight * flow * (states * states / samples)
            tally = tally * (values * states / samples)
        for k, value in enumerate((flow, tally)):
            refs[k][n] = value.astype(refs[k].dtype)
            if final:
                copies.append(pltpu.make_async_copy(refs[k].at[n], homes[k].at[n], sems.at[k, n]))
                copies[-1].start()
    for copy in copies:
        copy.wait()


def swap(value, mask):
    return lax.ppermute(value, "rows", [(s, s ^ mask) for s in range(lax.axis_size("rows"))])


def gather(value):
    blocks = {0: value}
    for bit in reversed(range(lax.axis_size("rows").bit_length() - 1)):
        blocks.update({place | (1 << bit): swap(block, 1 << bit) for place, block in blocks.items()})
    return [blocks[place] for place in range(len(blocks))]


def per_device(mixing, emission, prior, parent, observed):
    nodes, states = mixing.shape[:2]
    rows = observed.shape[1]
    values = emission.shape[1]
    leaves = lax.axis_size("leaf")
    groups = lax.axis_size("rows")
    levels = leaves.bit_length() - 1
    share = states // groups
    part = rows // CHUNKS
    every = range(CHUNKS)
    half = functools.partial(pltpu.VMEM, (part, states))

    outs = run(
        functools.partial(prep_body, nodes),
        "prep",
        tuple(pltpu.with_memory_space_constraint(x, pltpu.HBM) for x in (parent, observed, emission, mixing)),
        (
            pltpu.VMEM(mixing.shape, BF16),
            pltpu.VMEM(((nodes - 1) * rows + PAD, states), BF16),
            pltpu.VMEM((nodes - 1, rows, states), F32),
        )
        + (half(F32),) * CHUNKS,
        (
            pltpu.VMEM((nodes - 1, rows, states), F32),
            pltpu.VMEM(emission.shape, BF16),
            pltpu.VMEM(observed.shape, jnp.int32),
            pltpu.SMEM(parent.shape, jnp.int32),
            pltpu.SemaphoreType.DMA((3, max(nodes, 2))),
        ),
        [ANY] * 4,
    )
    weights, lams, msgs = outs[:3]
    raw, send = list(outs[3:]), []
    for c in every:
        (block,) = run(first_body, "first", (raw[c], weights, *send[-1:]), (half(BF16),))
        send.append(block)

    def up_pairs(level):
        step = 1 << level
        return [(s, s - step) for s in range(leaves) if s % (2 * step) == step]

    def down_pairs(level):
        return [(b, a) for a, b in up_pairs(level)]

    for level in range(levels - 1):
        for c in every:
            recv = lax.ppermute(send[c], "leaf", up_pairs(level))
            tie = level == 0 and c == CHUNKS - 1
            raw[c], send[c], *passed = run(
                functools.partial(lift_body, level),
                "lift",
                (raw[c], recv, weights) + ((lams,) if tie else ()),
                (half(F32), half(BF16)) + ((pltpu.VMEM(lams.shape, BF16),) if tie else ()),
                same={0: 0, 3: 2} if tie else {0: 0},
            )
            lams = passed[0] if tie else lams
        if level == 0:
            all_lams = gather(lams)
    top_lam, top_msg, ratio, post = ([None] * CHUNKS for _ in range(4))
    for c in every:
        recv = lax.ppermute(send[c], "leaf", up_pairs(levels - 1))
        final = c == CHUNKS - 1
        top_lam[c], top_msg[c], ratio[c], post[c], *merged = run(
            functools.partial(root_body, levels - 1),
            "root",
            (raw[c], recv, weights, prior.reshape(1, states)) + (tuple(top_lam[:c]) if final else ()),
            (half(BF16), half(F32), half(BF16), half(BF16)) + ((pltpu.VMEM((rows, states), BF16),) if final else ()),
        )
    all_tops = gather(merged[0])
    for level in reversed(range(1, levels)):
        for c in every:
            recv = lax.ppermute(post[c], "leaf", down_pairs(level))
            ratio[c], post[c] = run(
                functools.partial(settle_body, level),
                "settle",
                (recv, top_lam[c], top_msg[c], weights, ratio[c], post[c]),
                (half(BF16), half(BF16)),
            )
    raw_own, hots = run(
        functools.partial(ready_body, nodes, groups),
        "ready",
        (weights, *all_lams),
        (
            pltpu.VMEM((nodes - 1, CHUNKS, groups * part, share), F32),
            pltpu.VMEM((nodes, CHUNKS, values, groups * part), BF16),
        ),
    )
    own_posts = []
    for c in every:
        recv = lax.ppermute(post[c], "leaf", down_pairs(0))
        packs = run(
            functools.partial(last_body, nodes, groups, c),
            "last",
            (parent, recv, top_lam[c], top_msg[c], weights, ratio[c], post[c], lams, msgs, raw_own),
            (pltpu.VMEM((nodes + 1, part, share), BF16),) * groups,
            (pltpu.VMEM((nodes + 1, part, states), BF16),),
            [SM] + [VM] * 9,
        )
        order = sorted(range(1, groups), reverse=True)
        moved = {mask: swap(packs[mask], mask) for mask in order}
        own_posts.append([packs[0]] + [moved[mask] for mask in range(1, groups)])
    sums = ()
    for c in every:
        final = c == CHUNKS - 1
        ins = (parent, raw_own, hots, *all_lams, *all_tops, *own_posts[c], *sums) + ((weights,) if final else ())
        shapes = ((nodes, share, states), (nodes, values, share))
        sums = run(
            functools.partial(counts_body, nodes, groups, c),
            "counts",
            ins,
            tuple(jax.ShapeDtypeStruct(x, BF16) if final else pltpu.VMEM(x, F32) for x in shapes),
            tuple(pltpu.VMEM(x, BF16) for x in shapes) + (pltpu.SemaphoreType.DMA((2, nodes)),) if final else (),
            [SM] + [VM] * (len(ins) - 1),
            (ANY, ANY) if final else None,
        )
    return tuple(sums)


def solution(mesh):
    placed = (P("leaf", None, None), P("leaf", None, None), P(), P("leaf"), P("leaf", "rows"))
    return jax.shard_map(
        per_device,
        mesh=mesh,
        in_specs=placed,
        out_specs=(P("leaf", "rows", None), P("leaf", None, "rows")),
        check_vma=False,
    )
```

```python
import functools
import jax
import jax.numpy as jnp
from jax import lax
from jax.experimental import pallas as pl
from jax.experimental.pallas import tpu as pltpu
from jax.sharding import PartitionSpec as P

F32 = jnp.float32
BF16 = jnp.bfloat16
PAD = 16
CHUNKS = 2
LIMIT = 24 * 2**20
VM = pl.BlockSpec(memory_space=pltpu.VMEM)
SM = pl.BlockSpec(memory_space=pltpu.SMEM)
ANY = pl.BlockSpec(memory_space=pl.ANY)


def run(body, name, ins, outs, scratch=(), specs=None, out_specs=None, same=None, after=()):
    count, idle = len(ins), len(ins) + len(after)
    return pl.pallas_call(
        lambda *refs: body(*refs[:count], *refs[idle:]),
        name=name,
        in_specs=(specs or [VM] * count) + [VM] * len(after),
        out_specs=out_specs or tuple(VM for _ in outs),
        out_shape=tuple(outs),
        input_output_aliases=same or {},
        scratch_shapes=list(scratch),
        compiler_params=pltpu.CompilerParams(vmem_limit_bytes=LIMIT),
    )(*ins, *after)


def scaled(raw):
    return (raw * (1.0 / jnp.mean(raw, axis=1, keepdims=True))).astype(BF16)


def upward(lam, weight):
    rows = lam.shape[0]
    stacked = jnp.concatenate([lam, jnp.ones((PAD, lam.shape[1]), BF16)], axis=0)
    both = lax.dot_general(stacked, weight, (((1,), (1,)), ((), ())), preferred_element_type=F32)
    return both[:rows], both[rows : rows + 1]


def downward(q_par, raw_msg, lam, weight):
    ratio = (q_par / raw_msg).astype(BF16)
    post = lam.astype(F32) * jnp.dot(ratio, weight, preferred_element_type=F32)
    return ratio, post.astype(BF16)


def one_hot(row, values):
    return (lax.broadcasted_iota(jnp.int32, (values, row.shape[1]), 0) == row).astype(F32).astype(BF16)


def local_slot(parent_ref, node, nodes):
    return jnp.clip(parent_ref[node] - lax.axis_index("leaf") * nodes, 0, node - 1)


def is_upper(level):
    return jnp.bitwise_and(lax.axis_index("leaf"), (2 << level) - 1) == 0


def is_lower(level):
    return jnp.bitwise_and(lax.axis_index("leaf"), (2 << level) - 1) == (1 << level)


def prep_body(nodes, parent_hbm, obs_hbm, emission_hbm, mixing_hbm, *refs):
    w_ref, lam_ref, msg_ref = refs[:3]
    u_refs = refs[3 : 3 + CHUNKS]
    prods, tables, obs, parent_ref, sems = refs[3 + CHUNKS :]
    copy_obs = pltpu.make_async_copy(obs_hbm, obs, sems.at[2, 0])
    copy_parent = pltpu.make_async_copy(parent_hbm, parent_ref, sems.at[2, 1])
    copies_w = [pltpu.make_async_copy(mixing_hbm.at[n], w_ref.at[n], sems.at[0, n]) for n in range(nodes)]
    copies_e = [pltpu.make_async_copy(emission_hbm.at[n], tables.at[n], sems.at[1, n]) for n in range(nodes)]
    copy_obs.start()
    copy_parent.start()
    for n in reversed(range(nodes)):
        copies_e[n].start()
        copies_w[n].start()
    values = tables.shape[1]
    rows = obs.shape[1]
    part = rows // CHUNKS
    for n in range(nodes - 1):
        prods[n] = jnp.ones(prods.shape[1:], F32)
    copy_obs.wait()
    index = lax.broadcasted_iota(jnp.int32, (PAD, rows), 0)
    listed = jnp.zeros((PAD, rows), jnp.int32)
    for n in range(nodes):
        listed = jnp.where(index == n, obs[n : n + 1, :], listed)
    base = (nodes - 1) * rows
    lam_ref[base : base + PAD, :] = jnp.zeros((PAD, lam_ref.shape[1]), BF16)
    lam_ref[base : base + PAD, :rows] = listed.astype(F32).astype(BF16)
    copy_parent.wait()
    for n in reversed(range(nodes)):
        copies_e[n].wait()
        hot = one_hot(obs[n : n + 1, :], values)
        table = tables[n]
        picked = lax.dot_general(hot, table, (((0,), (0,)), ((), ())), preferred_element_type=F32)
        total = jnp.dot(jnp.ones((PAD, values), BF16), table, preferred_element_type=F32)[:1]
        raw = (picked * (1.0 / total)).astype(BF16).astype(F32)
        if n < nodes - 1:
            raw = raw * prods[n]
        if n > 0:
            lam = scaled(raw)
            copies_w[n].wait()
            raw_msg, sums = upward(lam, w_ref[n])
            lam_ref[(n - 1) * rows : n * rows, :] = lam
            msg_ref[n - 1] = raw_msg
            slot = local_slot(parent_ref, n, nodes)
            prods[slot] = prods[slot] * (raw_msg * (1.0 / sums))
        else:
            for c in range(CHUNKS):
                u_refs[c][...] = raw[c * part : (c + 1) * part]
    copies_w[0].wait()


def send_up(level, raw_ref, w_ref, send_ref):
    @pl.when(is_lower(level))
    def _():
        raw_msg, sums = upward(scaled(raw_ref[...]), w_ref[0])
        send_ref[...] = (raw_msg * (1.0 / sums)).astype(BF16)


def first_body(u_ref, w_ref, send_ref):
    send_up(0, u_ref, w_ref, send_ref)


def lift_body(level, u_ref, recv_ref, w_ref, u_out, send_ref):
    @pl.when(is_upper(level))
    def _():
        u_out[...] = u_ref[...] * recv_ref[...].astype(F32)

    send_up(level + 1, u_out, w_ref, send_ref)


def root_body(level, u_ref, recv_ref, w_ref, prior_ref, *refs):
    lam_ref, msg_ref, ratio_ref, post_ref = refs[-5:-1] if len(refs) > 4 else refs
    lam = scaled(u_ref[...] * jnp.where(is_upper(level), recv_ref[...].astype(F32), 1.0))
    raw_msg, sums = upward(lam, w_ref[0])
    lam_ref[...] = lam
    msg_ref[...] = raw_msg
    if len(refs) > 4:
        for c, block in enumerate([item[...] for item in refs[:-5]] + [lam]):
            refs[-1][c * lam.shape[0] : (c + 1) * lam.shape[0], :] = block

    @pl.when(lax.axis_index("leaf") == 0)
    def _():
        prior = prior_ref[...]
        weighted = (prior / jnp.sum(prior)) * (raw_msg * (1.0 / sums))
        share = weighted / jnp.sum(weighted, axis=1, keepdims=True)
        ratio, post = downward(share, raw_msg, lam, w_ref[0])
        ratio_ref[...] = ratio
        post_ref[...] = post


def settle_body(level, recv_ref, lam_ref, msg_ref, w_ref, ratio_in, post_in, ratio_ref, post_ref):
    got = is_lower(level)

    @pl.when(got)
    def _():
        ratio, post = downward(recv_ref[...].astype(F32), msg_ref[...], lam_ref[...], w_ref[0])
        ratio_ref[...] = ratio
        post_ref[...] = post

    @pl.when(jnp.logical_not(got))
    def _():
        ratio_ref[...] = ratio_in[...]
        post_ref[...] = post_in[...]


def last_body(nodes, groups, chunk, parent_ref, recv_ref, lam_ref, msg_ref, w_ref, ratio_in, post_in, lams_ref, msgs_ref, *refs):
    packs, posts = refs[:groups], refs[groups]
    rows, part = msgs_ref.shape[1], lam_ref.shape[0]
    share = lam_ref.shape[1] // groups
    got = is_lower(0)

    @pl.when(got)
    def _():
        ratio, post = downward(recv_ref[...].astype(F32), msg_ref[...], lam_ref[...], w_ref[0])
        posts[nodes] = ratio
        posts[0] = post

    @pl.when(jnp.logical_not(got))
    def _():
        posts[nodes] = ratio_in[...]
        posts[0] = post_in[...]

    for n in range(1, nodes):
        q_par = posts[local_slot(parent_ref, n, nodes)].astype(F32)
        low = (n - 1) * rows + chunk * part
        raw_msg = msgs_ref[n - 1, chunk * part : (chunk + 1) * part, :]
        _, posts[n] = downward(q_par, raw_msg, lams_ref[low : low + part, :], w_ref[n])
    own = lax.axis_index("rows")
    for mask in range(groups):
        start = pl.multiple_of(jnp.bitwise_xor(own, mask) * share, share)
        packs[mask][...] = posts[:, :, pl.ds(start, share)]


def ready_body(nodes, groups, w_ref, *refs):
    lams, (raw_ref, hot_ref) = refs[:groups], refs[groups:]
    chunks, merged, share = raw_ref.shape[1:]
    part = merged // groups
    rows = part * chunks
    values = hot_ref.shape[2]
    base = (nodes - 1) * rows
    start = pl.multiple_of(lax.axis_index("rows") * share, share)
    for n in range(nodes):
        observed = [lam[base : base + PAD, :rows].astype(F32).astype(jnp.int32)[n : n + 1] for lam in lams]
        for c in range(chunks):
            row = jnp.concatenate([item[:, c * part : (c + 1) * part] for item in observed], axis=1)
            hot_ref[n, c] = one_hot(row, values)
        if n > 0:
            weight = w_ref[n, pl.ds(start, share), :]
            for c in range(chunks):
                low = (n - 1) * rows + c * part
                lam = jnp.concatenate([item[low : low + part, :] for item in lams], axis=0)
                raw_ref[n - 1, c] = lax.dot_general(lam, weight, (((1,), (1,)), ((), ())), preferred_element_type=F32)


def counts_body(nodes, groups, chunk, parent_ref, raw_ref, hot_ref, *refs):
    lams, tops, posts = refs[:groups], refs[groups : 2 * groups], refs[2 * groups : 3 * groups]
    refs = refs[3 * groups :]
    chunks = raw_ref.shape[1]
    part = raw_ref.shape[2] // groups
    rows = part * chunks
    before = refs[:2] if chunk > 0 else None
    refs = refs[2:] if chunk > 0 else refs
    final = chunk == chunks - 1
    copies = []
    if final:
        w_ref, homes, refs, sems = refs[0], refs[1:3], refs[3:5], refs[5]
        share = refs[0].shape[1]
        samples = rows * groups
        start = pl.multiple_of(lax.axis_index("rows") * share, share)
    for n in range(nodes):
        low = (n - 1) * rows + chunk * part if n > 0 else chunk * part
        lam = jnp.concatenate([item[low : low + part, :] for item in (lams if n > 0 else tops)], axis=0)
        if n == 0:
            ratio = jnp.concatenate([item[nodes] for item in posts], axis=0)
        else:
            slot = local_slot(parent_ref, n, nodes)
            q_par = jnp.concatenate([item[slot] for item in posts], axis=0)
            ratio = (q_par.astype(F32) / raw_ref[n - 1, chunk]).astype(BF16)
        flow = lax.dot_general(ratio, lam, (((0,), (0,)), ((), ())), preferred_element_type=F32)
        post = jnp.concatenate([item[n] for item in posts], axis=0)
        tally = jnp.dot(hot_ref[n, chunk], post, preferred_element_type=F32)
        if before is not None:
            flow += before[0][n]
            tally += before[1][n]
        if final:
            states, values = flow.shape[1], tally.shape[0]
            weight = w_ref[n, pl.ds(start, share), :].astype(F32)
            flow = weight * flow * (states * states / samples)
            tally = tally * (values * states / samples)
        for k, value in enumerate((flow, tally)):
            refs[k][n] = value.astype(refs[k].dtype)
            if final:
                copies.append(pltpu.make_async_copy(refs[k].at[n], homes[k].at[n], sems.at[k, n]))
                copies[-1].start()
    for copy in copies:
        copy.wait()


def swap(value, mask):
    return lax.ppermute(value, "rows", [(s, s ^ mask) for s in range(lax.axis_size("rows"))])


def gather(value):
    blocks = {0: value}
    for bit in reversed(range(lax.axis_size("rows").bit_length() - 1)):
        blocks.update({place | (1 << bit): swap(block, 1 << bit) for place, block in blocks.items()})
    return [blocks[place] for place in range(len(blocks))]


def per_device(mixing, emission, prior, parent, observed):
    nodes, states = mixing.shape[:2]
    rows = observed.shape[1]
    values = emission.shape[1]
    leaves = lax.axis_size("leaf")
    groups = lax.axis_size("rows")
    levels = leaves.bit_length() - 1
    share = states // groups
    part = rows // CHUNKS
    every = range(CHUNKS)
    half = functools.partial(pltpu.VMEM, (part, states))

    outs = run(
        functools.partial(prep_body, nodes),
        "prep",
        tuple(pltpu.with_memory_space_constraint(x, pltpu.HBM) for x in (parent, observed, emission, mixing)),
        (
            pltpu.VMEM(mixing.shape, BF16),
            pltpu.VMEM(((nodes - 1) * rows + PAD, states), BF16),
            pltpu.VMEM((nodes - 1, rows, states), F32),
        )
        + (half(F32),) * CHUNKS,
        (
            pltpu.VMEM((nodes - 1, rows, states), F32),
            pltpu.VMEM(emission.shape, BF16),
            pltpu.VMEM(observed.shape, jnp.int32),
            pltpu.SMEM(parent.shape, jnp.int32),
            pltpu.SemaphoreType.DMA((3, max(nodes, 2))),
        ),
        [ANY] * 4,
    )
    weights, lams, msgs = outs[:3]
    raw, send = list(outs[3:]), []
    for c in every:
        (block,) = run(first_body, "first", (raw[c], weights), (half(BF16),), after=[lams] if c > 0 else ())
        send.append(block)
        if c == 0:
            (lams,) = run(
                lambda *refs: None, "pass", (lams,), (pltpu.VMEM(lams.shape, BF16),), same={0: 0}, after=(block,)
            )

    def up_pairs(level):
        step = 1 << level
        return [(s, s - step) for s in range(leaves) if s % (2 * step) == step]

    def down_pairs(level):
        return [(b, a) for a, b in up_pairs(level)]

    for level in range(levels - 1):
        for c in every:
            recv = lax.ppermute(send[c], "leaf", up_pairs(level))
            raw[c], send[c] = run(
                functools.partial(lift_body, level),
                "lift",
                (raw[c], recv, weights),
                (half(F32), half(BF16)),
                same={0: 0},
                after=send[:c][-1:],
            )
        if level == 0:
            all_lams = gather(lams)
    top_lam, top_msg, ratio, post = ([None] * CHUNKS for _ in range(4))
    for c in every:
        recv = lax.ppermute(send[c], "leaf", up_pairs(levels - 1))
        final = c == CHUNKS - 1
        top_lam[c], top_msg[c], ratio[c], post[c], *merged = run(
            functools.partial(root_body, levels - 1),
            "root",
            (raw[c], recv, weights, prior.reshape(1, states)) + (tuple(top_lam[:c]) if final else ()),
            (half(BF16), half(F32), half(BF16), half(BF16)) + ((pltpu.VMEM((rows, states), BF16),) if final else ()),
        )
    all_tops = gather(merged[0])
    for level in reversed(range(1, levels)):
        for c in every:
            recv = lax.ppermute(post[c], "leaf", down_pairs(level))
            ratio[c], post[c] = run(
                functools.partial(settle_body, level),
                "settle",
                (recv, top_lam[c], top_msg[c], weights, ratio[c], post[c]),
                (half(BF16), half(BF16)),
                after=post[:c][-1:],
            )
    raw_own, hots = run(
        functools.partial(ready_body, nodes, groups),
        "ready",
        (weights, *all_lams),
        (
            pltpu.VMEM((nodes - 1, CHUNKS, groups * part, share), F32),
            pltpu.VMEM((nodes, CHUNKS, values, groups * part), BF16),
        ),
    )
    own_posts = []
    for c in every:
        recv = lax.ppermute(post[c], "leaf", down_pairs(0))
        packs = run(
            functools.partial(last_body, nodes, groups, c),
            "last",
            (parent, recv, top_lam[c], top_msg[c], weights, ratio[c], post[c], lams, msgs),
            (pltpu.VMEM((nodes + 1, part, share), BF16),) * groups,
            (pltpu.VMEM((nodes + 1, part, states), BF16),),
            [SM] + [VM] * 8,
            after=own_posts[-1][:1] if c > 0 else (),
        )
        order = sorted(range(1, groups), reverse=True)
        moved = {mask: swap(packs[mask], mask) for mask in order}
        own_posts.append([packs[0]] + [moved[mask] for mask in range(1, groups)])
    sums = ()
    for c in every:
        final = c == CHUNKS - 1
        ins = (parent, raw_own, hots, *all_lams, *all_tops, *own_posts[c], *sums) + ((weights,) if final else ())
        shapes = ((nodes, share, states), (nodes, values, share))
        sums = run(
            functools.partial(counts_body, nodes, groups, c),
            "counts",
            ins,
            tuple(jax.ShapeDtypeStruct(x, BF16) if final else pltpu.VMEM(x, F32) for x in shapes),
            tuple(pltpu.VMEM(x, BF16) for x in shapes) + (pltpu.SemaphoreType.DMA((2, nodes)),) if final else (),
            [SM] + [VM] * (len(ins) - 1),
            (ANY, ANY) if final else None,
        )
    return tuple(sums)


def solution(mesh):
    placed = (P("leaf", None, None), P("leaf", None, None), P(), P("leaf"), P("leaf", "rows"))
    return jax.shard_map(
        per_device,
        mesh=mesh,
        in_specs=placed,
        out_specs=(P("leaf", "rows", None), P("leaf", None, "rows")),
        check_vma=False,
    )
```

```python
import functools
import jax
import jax.numpy as jnp
from jax import lax
from jax.experimental import pallas as pl
from jax.experimental.pallas import tpu as pltpu
from jax.sharding import PartitionSpec as P

F32 = jnp.float32
BF16 = jnp.bfloat16
PAD = 16
CHUNKS = 2
WORK = 10*10**8
LIMIT = 24 * 2**20
VM = pl.BlockSpec(memory_space=pltpu.VMEM)
SM = pl.BlockSpec(memory_space=pltpu.SMEM)
ANY = pl.BlockSpec(memory_space=pl.ANY)


def run(body, name, ins, outs, scratch=(), specs=None, out_specs=None, same=None, after=(), work=1.0):
    count, idle = len(ins), len(ins) + len(after)
    return pl.pallas_call(
        lambda *refs: body(*refs[:count], *refs[idle:]),
        name=name,
        in_specs=(specs or [VM] * count) + [VM] * len(after),
        out_specs=out_specs or tuple(VM for _ in outs),
        out_shape=tuple(outs),
        input_output_aliases=same or {},
        scratch_shapes=list(scratch),
        compiler_params=pltpu.CompilerParams(vmem_limit_bytes=LIMIT),
        cost_estimate=pl.CostEstimate(flops=int(work * WORK), bytes_accessed=2**21, transcendentals=0),
    )(*ins, *after)


def scaled(raw):
    return (raw * (1.0 / jnp.mean(raw, axis=1, keepdims=True))).astype(BF16)


def upward(lam, weight):
    rows = lam.shape[0]
    stacked = jnp.concatenate([lam, jnp.ones((PAD, lam.shape[1]), BF16)], axis=0)
    both = lax.dot_general(stacked, weight, (((1,), (1,)), ((), ())), preferred_element_type=F32)
    return both[:rows], both[rows : rows + 1]


def downward(q_par, raw_msg, lam, weight):
    ratio = (q_par / raw_msg).astype(BF16)
    post = lam.astype(F32) * jnp.dot(ratio, weight, preferred_element_type=F32)
    return ratio, post.astype(BF16)


def one_hot(row, values):
    return (lax.broadcasted_iota(jnp.int32, (values, row.shape[1]), 0) == row).astype(F32).astype(BF16)


def local_slot(parent_ref, node, nodes):
    return jnp.clip(parent_ref[node] - lax.axis_index("leaf") * nodes, 0, node - 1)


def is_upper(level):
    return jnp.bitwise_and(lax.axis_index("leaf"), (2 << level) - 1) == 0


def is_lower(level):
    return jnp.bitwise_and(lax.axis_index("leaf"), (2 << level) - 1) == (1 << level)


def prep_body(nodes, parent_hbm, obs_hbm, emission_hbm, mixing_hbm, *refs):
    w_ref, lam_ref, msg_ref = refs[:3]
    u_refs = refs[3 : 3 + CHUNKS]
    prods, tables, obs, parent_ref, sems = refs[3 + CHUNKS :]
    copy_obs = pltpu.make_async_copy(obs_hbm, obs, sems.at[2, 0])
    copy_parent = pltpu.make_async_copy(parent_hbm, parent_ref, sems.at[2, 1])
    copies_w = [pltpu.make_async_copy(mixing_hbm.at[n], w_ref.at[n], sems.at[0, n]) for n in range(nodes)]
    copies_e = [pltpu.make_async_copy(emission_hbm.at[n], tables.at[n], sems.at[1, n]) for n in range(nodes)]
    copy_obs.start()
    copy_parent.start()
    for n in reversed(range(nodes)):
        copies_e[n].start()
        copies_w[n].start()
    values = tables.shape[1]
    rows = obs.shape[1]
    part = rows // CHUNKS
    for n in range(nodes - 1):
        prods[n] = jnp.ones(prods.shape[1:], F32)
    copy_obs.wait()
    index = lax.broadcasted_iota(jnp.int32, (PAD, rows), 0)
    listed = jnp.zeros((PAD, rows), jnp.int32)
    for n in range(nodes):
        listed = jnp.where(index == n, obs[n : n + 1, :], listed)
    base = (nodes - 1) * rows
    lam_ref[base : base + PAD, :] = jnp.zeros((PAD, lam_ref.shape[1]), BF16)
    lam_ref[base : base + PAD, :rows] = listed.astype(F32).astype(BF16)
    copy_parent.wait()
    for n in reversed(range(nodes)):
        copies_e[n].wait()
        hot = one_hot(obs[n : n + 1, :], values)
        table = tables[n]
        picked = lax.dot_general(hot, table, (((0,), (0,)), ((), ())), preferred_element_type=F32)
        total = jnp.dot(jnp.ones((PAD, values), BF16), table, preferred_element_type=F32)[:1]
        raw = (picked * (1.0 / total)).astype(BF16).astype(F32)
        if n < nodes - 1:
            raw = raw * prods[n]
        if n > 0:
            lam = scaled(raw)
            copies_w[n].wait()
            raw_msg, sums = upward(lam, w_ref[n])
            lam_ref[(n - 1) * rows : n * rows, :] = lam
            msg_ref[n - 1] = raw_msg
            slot = local_slot(parent_ref, n, nodes)
            prods[slot] = prods[slot] * (raw_msg * (1.0 / sums))
        else:
            for c in range(CHUNKS):
                u_refs[c][...] = raw[c * part : (c + 1) * part]
    copies_w[0].wait()


def send_up(level, raw_ref, w_ref, send_ref):
    @pl.when(is_lower(level))
    def _():
        raw_msg, sums = upward(scaled(raw_ref[...]), w_ref[0])
        send_ref[...] = (raw_msg * (1.0 / sums)).astype(BF16)


def first_body(u_ref, w_ref, send_ref):
    send_up(0, u_ref, w_ref, send_ref)


def lift_body(level, u_ref, recv_ref, w_ref, u_out, send_ref):
    @pl.when(is_upper(level))
    def _():
        u_out[...] = u_ref[...] * recv_ref[...].astype(F32)

    send_up(level + 1, u_out, w_ref, send_ref)


def root_body(level, u_ref, recv_ref, w_ref, prior_ref, *refs):
    lam_ref, msg_ref, ratio_ref, post_ref = refs[-5:-1] if len(refs) > 4 else refs
    lam = scaled(u_ref[...] * jnp.where(is_upper(level), recv_ref[...].astype(F32), 1.0))
    raw_msg, sums = upward(lam, w_ref[0])
    lam_ref[...] = lam
    msg_ref[...] = raw_msg
    if len(refs) > 4:
        for c, block in enumerate([item[...] for item in refs[:-5]] + [lam]):
            refs[-1][c * lam.shape[0] : (c + 1) * lam.shape[0], :] = block

    @pl.when(lax.axis_index("leaf") == 0)
    def _():
        prior = prior_ref[...]
        weighted = (prior / jnp.sum(prior)) * (raw_msg * (1.0 / sums))
        share = weighted / jnp.sum(weighted, axis=1, keepdims=True)
        ratio, post = downward(share, raw_msg, lam, w_ref[0])
        ratio_ref[...] = ratio
        post_ref[...] = post


def settle_body(level, recv_ref, lam_ref, msg_ref, w_ref, ratio_in, post_in, ratio_ref, post_ref):
    got = is_lower(level)

    @pl.when(got)
    def _():
        ratio, post = downward(recv_ref[...].astype(F32), msg_ref[...], lam_ref[...], w_ref[0])
        ratio_ref[...] = ratio
        post_ref[...] = post

    @pl.when(jnp.logical_not(got))
    def _():
        ratio_ref[...] = ratio_in[...]
        post_ref[...] = post_in[...]


def last_body(nodes, groups, chunk, parent_ref, recv_ref, lam_ref, msg_ref, w_ref, ratio_in, post_in, lams_ref, msgs_ref, *refs):
    packs, posts = refs[:groups], refs[groups]
    rows, part = msgs_ref.shape[1], lam_ref.shape[0]
    share = lam_ref.shape[1] // groups
    got = is_lower(0)

    @pl.when(got)
    def _():
        ratio, post = downward(recv_ref[...].astype(F32), msg_ref[...], lam_ref[...], w_ref[0])
        posts[nodes] = ratio
        posts[0] = post

    @pl.when(jnp.logical_not(got))
    def _():
        posts[nodes] = ratio_in[...]
        posts[0] = post_in[...]

    for n in range(1, nodes):
        q_par = posts[local_slot(parent_ref, n, nodes)].astype(F32)
        low = (n - 1) * rows + chunk * part
        raw_msg = msgs_ref[n - 1, chunk * part : (chunk + 1) * part, :]
        _, posts[n] = downward(q_par, raw_msg, lams_ref[low : low + part, :], w_ref[n])
    own = lax.axis_index("rows")
    for mask in range(groups):
        start = pl.multiple_of(jnp.bitwise_xor(own, mask) * share, share)
        packs[mask][...] = posts[:, :, pl.ds(start, share)]


def ready_body(nodes, groups, w_ref, *refs):
    lams, (raw_ref, hot_ref) = refs[:groups], refs[groups:]
    chunks, merged, share = raw_ref.shape[1:]
    part = merged // groups
    rows = part * chunks
    values = hot_ref.shape[2]
    base = (nodes - 1) * rows
    start = pl.multiple_of(lax.axis_index("rows") * share, share)
    for n in range(nodes):
        observed = [lam[base : base + PAD, :rows].astype(F32).astype(jnp.int32)[n : n + 1] for lam in lams]
        for c in range(chunks):
            row = jnp.concatenate([item[:, c * part : (c + 1) * part] for item in observed], axis=1)
            hot_ref[n, c] = one_hot(row, values)
        if n > 0:
            weight = w_ref[n, pl.ds(start, share), :]
            for c in range(chunks):
                low = (n - 1) * rows + c * part
                lam = jnp.concatenate([item[low : low + part, :] for item in lams], axis=0)
                raw_ref[n - 1, c] = lax.dot_general(lam, weight, (((1,), (1,)), ((), ())), preferred_element_type=F32)


def counts_body(nodes, groups, chunk, parent_ref, raw_ref, hot_ref, *refs):
    lams, tops, posts = refs[:groups], refs[groups : 2 * groups], refs[2 * groups : 3 * groups]
    refs = refs[3 * groups :]
    chunks = raw_ref.shape[1]
    part = raw_ref.shape[2] // groups
    rows = part * chunks
    before = refs[:2] if chunk > 0 else None
    refs = refs[2:] if chunk > 0 else refs
    final = chunk == chunks - 1
    copies = []
    if final:
        w_ref, homes, refs, sems = refs[0], refs[1:3], refs[3:5], refs[5]
        share = refs[0].shape[1]
        samples = rows * groups
        start = pl.multiple_of(lax.axis_index("rows") * share, share)
    for n in range(nodes):
        low = (n - 1) * rows + chunk * part if n > 0 else chunk * part
        lam = jnp.concatenate([item[low : low + part, :] for item in (lams if n > 0 else tops)], axis=0)
        if n == 0:
            ratio = jnp.concatenate([item[nodes] for item in posts], axis=0)
        else:
            slot = local_slot(parent_ref, n, nodes)
            q_par = jnp.concatenate([item[slot] for item in posts], axis=0)
            ratio = (q_par.astype(F32) / raw_ref[n - 1, chunk]).astype(BF16)
        flow = lax.dot_general(ratio, lam, (((0,), (0,)), ((), ())), preferred_element_type=F32)
        post = jnp.concatenate([item[n] for item in posts], axis=0)
        tally = jnp.dot(hot_ref[n, chunk], post, preferred_element_type=F32)
        if before is not None:
            flow += before[0][n]
            tally += before[1][n]
        if final:
            states, values = flow.shape[1], tally.shape[0]
            weight = w_ref[n, pl.ds(start, share), :].astype(F32)
            flow = weight * flow * (states * states / samples)
            tally = tally * (values * states / samples)
        for k, value in enumerate((flow, tally)):
            refs[k][n] = value.astype(refs[k].dtype)
            if final:
                copies.append(pltpu.make_async_copy(refs[k].at[n], homes[k].at[n], sems.at[k, n]))
                copies[-1].start()
    for copy in copies:
        copy.wait()


def swap(value, mask):
    return lax.ppermute(value, "rows", [(s, s ^ mask) for s in range(lax.axis_size("rows"))])


def gather(value):
    blocks = {0: value}
    for bit in reversed(range(lax.axis_size("rows").bit_length() - 1)):
        blocks.update({place | (1 << bit): swap(block, 1 << bit) for place, block in blocks.items()})
    return [blocks[place] for place in range(len(blocks))]


def per_device(mixing, emission, prior, parent, observed):
    nodes, states = mixing.shape[:2]
    rows = observed.shape[1]
    values = emission.shape[1]
    leaves = lax.axis_size("leaf")
    groups = lax.axis_size("rows")
    levels = leaves.bit_length() - 1
    share = states // groups
    part = rows // CHUNKS
    every = range(CHUNKS)
    half = functools.partial(pltpu.VMEM, (part, states))

    outs = run(
        functools.partial(prep_body, nodes),
        "prep",
        tuple(pltpu.with_memory_space_constraint(x, pltpu.HBM) for x in (parent, observed, emission, mixing)),
        (
            pltpu.VMEM(mixing.shape, BF16),
            pltpu.VMEM(((nodes - 1) * rows + PAD, states), BF16),
            pltpu.VMEM((nodes - 1, rows, states), F32),
        )
        + (half(F32),) * CHUNKS,
        (
            pltpu.VMEM((nodes - 1, rows, states), F32),
            pltpu.VMEM(emission.shape, BF16),
            pltpu.VMEM(observed.shape, jnp.int32),
            pltpu.SMEM(parent.shape, jnp.int32),
            pltpu.SemaphoreType.DMA((3, max(nodes, 2))),
        ),
        [ANY] * 4,
    )
    weights, lams, msgs = outs[:3]
    raw, send = list(outs[3:]), []
    for c in every:
        (block,) = run(first_body, "first", (raw[c], weights), (half(BF16),), after=[lams] if c > 0 else ())
        send.append(block)
        if c == 0:
            (lams,) = run(
                lambda *refs: None, "pass", (lams,), (pltpu.VMEM(lams.shape, BF16),), same={0: 0}, after=(block,)
            )

    def up_pairs(level):
        step = 1 << level
        return [(s, s - step) for s in range(leaves) if s % (2 * step) == step]

    def down_pairs(level):
        return [(b, a) for a, b in up_pairs(level)]

    for level in range(levels - 1):
        for c in every:
            recv = lax.ppermute(send[c], "leaf", up_pairs(level))
            raw[c], send[c] = run(
                functools.partial(lift_body, level),
                "lift",
                (raw[c], recv, weights),
                (half(F32), half(BF16)),
                same={0: 0},
                after=send[:c][-1:],
            )
        if level == 0:
            all_lams = gather(lams)
    top_lam, top_msg, ratio, post = ([None] * CHUNKS for _ in range(4))
    for c in every:
        recv = lax.ppermute(send[c], "leaf", up_pairs(levels - 1))
        final = c == CHUNKS - 1
        top_lam[c], top_msg[c], ratio[c], post[c], *merged = run(
            functools.partial(root_body, levels - 1),
            "root",
            (raw[c], recv, weights, prior.reshape(1, states)) + (tuple(top_lam[:c]) if final else ()),
            (half(BF16), half(F32), half(BF16), half(BF16)) + ((pltpu.VMEM((rows, states), BF16),) if final else ()),
        )
    all_tops = gather(merged[0])
    raw_own, hots = run(
        functools.partial(ready_body, nodes, groups),
        "ready",
        (weights, *all_lams),
        (
            pltpu.VMEM((nodes - 1, CHUNKS, groups * part, share), F32),
            pltpu.VMEM((nodes, CHUNKS, values, groups * part), BF16),
        ),

    )
    for level in reversed(range(1, levels)):
        for c in every:
            recv = lax.ppermute(post[c], "leaf", down_pairs(level))
            ratio[c], post[c] = run(
                functools.partial(settle_body, level),
                "settle",
                (recv, top_lam[c], top_msg[c], weights, ratio[c], post[c]),
                (half(BF16), half(BF16)),
                after=post[:c][-1:] if c != 1 or level > 1 else (raw_own, *post[:c][-1:]),
            )
    own_posts = []
    for c in every:
        recv = lax.ppermute(post[c], "leaf", down_pairs(0))
        packs = run(
            functools.partial(last_body, nodes, groups, c),
            "last",
            (parent, recv, top_lam[c], top_msg[c], weights, ratio[c], post[c], lams, msgs),
            (pltpu.VMEM((nodes + 1, part, share), BF16),) * groups,
            (pltpu.VMEM((nodes + 1, part, states), BF16),),
            [SM] + [VM] * 8,
            after=own_posts[-1][:1] if c > 0 else tuple(all_tops),
        )
        order = sorted(range(1, groups), reverse=True)
        moved = {mask: swap(packs[mask], mask) for mask in order}
        own_posts.append([packs[0]] + [moved[mask] for mask in range(1, groups)])
    sums = ()
    for c in every:
        final = c == CHUNKS - 1
        ins = (parent, raw_own, hots, *all_lams, *all_tops, *own_posts[c], *sums) + ((weights,) if final else ())
        shapes = ((nodes, share, states), (nodes, values, share))
        sums = run(
            functools.partial(counts_body, nodes, groups, c),
            "counts",
            ins,
            tuple(jax.ShapeDtypeStruct(x, BF16) if final else pltpu.VMEM(x, F32) for x in shapes),
            tuple(pltpu.VMEM(x, BF16) for x in shapes) + (pltpu.SemaphoreType.DMA((2, nodes)),) if final else (),
            [SM] + [VM] * (len(ins) - 1),
            (ANY, ANY) if final else None,
        )
    return tuple(sums)


def solution(mesh):
    placed = (P("leaf", None, None), P("leaf", None, None), P(), P("leaf"), P("leaf", "rows"))
    return jax.shard_map(
        per_device,
        mesh=mesh,
        in_specs=placed,
        out_specs=(P("leaf", "rows", None), P("leaf", None, "rows")),
        check_vma=False,
    )
```

```python
import functools
import jax
import jax.numpy as jnp
from jax import lax
from jax.experimental import pallas as pl
from jax.experimental.pallas import tpu as pltpu
from jax.sharding import PartitionSpec as P

F32 = jnp.float32
BF16 = jnp.bfloat16
PAD = 16
CHUNKS = 2
WORK = 10*10**8
LIMIT = 24 * 2**20
VM = pl.BlockSpec(memory_space=pltpu.VMEM)
SM = pl.BlockSpec(memory_space=pltpu.SMEM)
ANY = pl.BlockSpec(memory_space=pl.ANY)


def run(body, name, ins, outs, scratch=(), specs=None, out_specs=None, same=None, after=(), work=1.0):
    count, idle = len(ins), len(ins) + len(after)
    return pl.pallas_call(
        lambda *refs: body(*refs[:count], *refs[idle:]),
        name=name,
        in_specs=(specs or [VM] * count) + [VM] * len(after),
        out_specs=out_specs or tuple(VM for _ in outs),
        out_shape=tuple(outs),
        input_output_aliases=same or {},
        scratch_shapes=list(scratch),
        compiler_params=pltpu.CompilerParams(vmem_limit_bytes=LIMIT),
        cost_estimate=pl.CostEstimate(flops=int(work * WORK), bytes_accessed=2**21, transcendentals=0),
    )(*ins, *after)


def scaled(raw):
    return (raw * (1.0 / jnp.mean(raw, axis=1, keepdims=True))).astype(BF16)


def upward(lam, weight):
    rows = lam.shape[0]
    stacked = jnp.concatenate([lam, jnp.ones((PAD, lam.shape[1]), BF16)], axis=0)
    both = lax.dot_general(stacked, weight, (((1,), (1,)), ((), ())), preferred_element_type=F32)
    return both[:rows], both[rows : rows + 1]


def downward(q_par, raw_msg, lam, weight):
    ratio = (q_par / raw_msg).astype(BF16)
    post = lam.astype(F32) * jnp.dot(ratio, weight, preferred_element_type=F32)
    return ratio, post.astype(BF16)


def one_hot(row, values):
    return (lax.broadcasted_iota(jnp.int32, (values, row.shape[1]), 0) == row).astype(F32).astype(BF16)


def local_slot(parent_ref, node, nodes):
    return jnp.clip(parent_ref[node] - lax.axis_index("leaf") * nodes, 0, node - 1)


def is_upper(level):
    return jnp.bitwise_and(lax.axis_index("leaf"), (2 << level) - 1) == 0


def is_lower(level):
    return jnp.bitwise_and(lax.axis_index("leaf"), (2 << level) - 1) == (1 << level)


def prep_body(nodes, parent_hbm, obs_hbm, emission_hbm, mixing_hbm, *refs):
    w_ref, lam_ref, msg_ref = refs[:3]
    u_refs = refs[3 : 3 + CHUNKS]
    prods, tables, obs, parent_ref, sems = refs[3 + CHUNKS :]
    copy_obs = pltpu.make_async_copy(obs_hbm, obs, sems.at[2, 0])
    copy_parent = pltpu.make_async_copy(parent_hbm, parent_ref, sems.at[2, 1])
    copies_w = [pltpu.make_async_copy(mixing_hbm.at[n], w_ref.at[n], sems.at[0, n]) for n in range(nodes)]
    copies_e = [pltpu.make_async_copy(emission_hbm.at[n], tables.at[n], sems.at[1, n]) for n in range(nodes)]
    copy_obs.start()
    copy_parent.start()
    for n in reversed(range(nodes)):
        copies_e[n].start()
        copies_w[n].start()
    values = tables.shape[1]
    rows = obs.shape[1]
    part = rows // CHUNKS
    for n in range(nodes - 1):
        prods[n] = jnp.ones(prods.shape[1:], F32)
    copy_obs.wait()
    index = lax.broadcasted_iota(jnp.int32, (PAD, rows), 0)
    listed = jnp.zeros((PAD, rows), jnp.int32)
    for n in range(nodes):
        listed = jnp.where(index == n, obs[n : n + 1, :], listed)
    base = (nodes - 1) * rows
    lam_ref[base : base + PAD, :] = jnp.zeros((PAD, lam_ref.shape[1]), BF16)
    lam_ref[base : base + PAD, :rows] = listed.astype(F32).astype(BF16)
    copy_parent.wait()
    for n in reversed(range(nodes)):
        copies_e[n].wait()
        hot = one_hot(obs[n : n + 1, :], values)
        table = tables[n]
        picked = lax.dot_general(hot, table, (((0,), (0,)), ((), ())), preferred_element_type=F32)
        total = jnp.dot(jnp.ones((PAD, values), BF16), table, preferred_element_type=F32)[:1]
        raw = (picked * (1.0 / total)).astype(BF16).astype(F32)
        if n < nodes - 1:
            raw = raw * prods[n]
        if n > 0:
            lam = scaled(raw)
            copies_w[n].wait()
            raw_msg, sums = upward(lam, w_ref[n])
            lam_ref[(n - 1) * rows : n * rows, :] = lam
            msg_ref[n - 1] = raw_msg
            slot = local_slot(parent_ref, n, nodes)
            prods[slot] = prods[slot] * (raw_msg * (1.0 / sums))
        else:
            for c in range(CHUNKS):
                u_refs[c][...] = raw[c * part : (c + 1) * part]
    copies_w[0].wait()


def send_up(level, raw_ref, w_ref, send_ref):
    @pl.when(is_lower(level))
    def _():
        raw_msg, sums = upward(scaled(raw_ref[...]), w_ref[0])
        send_ref[...] = (raw_msg * (1.0 / sums)).astype(BF16)


def first_body(u_ref, w_ref, send_ref):
    send_up(0, u_ref, w_ref, send_ref)


def lift_body(level, u_ref, recv_ref, w_ref, u_out, send_ref):
    @pl.when(is_upper(level))
    def _():
        u_out[...] = u_ref[...] * recv_ref[...].astype(F32)

    send_up(level + 1, u_out, w_ref, send_ref)


def root_body(level, u_ref, recv_ref, w_ref, prior_ref, *refs):
    lam_ref, msg_ref, ratio_ref, post_ref = refs[-5:-1] if len(refs) > 4 else refs
    lam = scaled(u_ref[...] * jnp.where(is_upper(level), recv_ref[...].astype(F32), 1.0))
    raw_msg, sums = upward(lam, w_ref[0])
    lam_ref[...] = lam
    msg_ref[...] = raw_msg
    if len(refs) > 4:
        for c, block in enumerate([item[...] for item in refs[:-5]] + [lam]):
            refs[-1][c * lam.shape[0] : (c + 1) * lam.shape[0], :] = block

    @pl.when(lax.axis_index("leaf") == 0)
    def _():
        prior = prior_ref[...]
        weighted = (prior / jnp.sum(prior)) * (raw_msg * (1.0 / sums))
        share = weighted / jnp.sum(weighted, axis=1, keepdims=True)
        ratio, post = downward(share, raw_msg, lam, w_ref[0])
        ratio_ref[...] = ratio
        post_ref[...] = post


def settle_body(level, recv_ref, lam_ref, msg_ref, w_ref, ratio_in, post_in, ratio_ref, post_ref):
    got = is_lower(level)

    @pl.when(got)
    def _():
        ratio, post = downward(recv_ref[...].astype(F32), msg_ref[...], lam_ref[...], w_ref[0])
        ratio_ref[...] = ratio
        post_ref[...] = post

    @pl.when(jnp.logical_not(got))
    def _():
        ratio_ref[...] = ratio_in[...]
        post_ref[...] = post_in[...]


def last_body(nodes, groups, chunk, parent_ref, recv_ref, lam_ref, msg_ref, w_ref, ratio_in, post_in, lams_ref, msgs_ref, *refs):
    packs, posts = refs[:groups], refs[groups]
    rows, part = msgs_ref.shape[1], lam_ref.shape[0]
    share = lam_ref.shape[1] // groups
    got = is_lower(0)

    @pl.when(got)
    def _():
        ratio, post = downward(recv_ref[...].astype(F32), msg_ref[...], lam_ref[...], w_ref[0])
        posts[nodes] = ratio
        posts[0] = post

    @pl.when(jnp.logical_not(got))
    def _():
        posts[nodes] = ratio_in[...]
        posts[0] = post_in[...]

    for n in range(1, nodes):
        q_par = posts[local_slot(parent_ref, n, nodes)].astype(F32)
        low = (n - 1) * rows + chunk * part
        raw_msg = msgs_ref[n - 1, chunk * part : (chunk + 1) * part, :]
        _, posts[n] = downward(q_par, raw_msg, lams_ref[low : low + part, :], w_ref[n])
    own = lax.axis_index("rows")
    for mask in range(groups):
        start = pl.multiple_of(jnp.bitwise_xor(own, mask) * share, share)
        packs[mask][...] = posts[:, :, pl.ds(start, share)]


def ready_body(nodes, groups, w_ref, *refs):
    lams, (raw_ref, hot_ref) = refs[:groups], refs[groups:]
    chunks, merged, share = raw_ref.shape[1:]
    part = merged // groups
    rows = part * chunks
    values = hot_ref.shape[2]
    base = (nodes - 1) * rows
    start = pl.multiple_of(lax.axis_index("rows") * share, share)
    for n in range(nodes):
        observed = [lam[base : base + PAD, :rows].astype(F32).astype(jnp.int32)[n : n + 1] for lam in lams]
        for c in range(chunks):
            row = jnp.concatenate([item[:, c * part : (c + 1) * part] for item in observed], axis=1)
            hot_ref[n, c] = one_hot(row, values)
        if n > 0:
            weight = w_ref[n, pl.ds(start, share), :]
            for c in range(chunks):
                low = (n - 1) * rows + c * part
                lam = jnp.concatenate([item[low : low + part, :] for item in lams], axis=0)
                raw_ref[n - 1, c] = lax.dot_general(lam, weight, (((1,), (1,)), ((), ())), preferred_element_type=F32)


def counts_body(nodes, groups, chunk, parent_ref, raw_ref, hot_ref, *refs):
    lams, tops, posts = refs[:groups], refs[groups : 2 * groups], refs[2 * groups : 3 * groups]
    refs = refs[3 * groups :]
    chunks = raw_ref.shape[1]
    part = raw_ref.shape[2] // groups
    rows = part * chunks
    before = refs[:2] if chunk > 0 else None
    refs = refs[2:] if chunk > 0 else refs
    final = chunk == chunks - 1
    copies = []
    if final:
        w_ref, homes, refs, sems = refs[0], refs[1:3], refs[3:5], refs[5]
        share = refs[0].shape[1]
        samples = rows * groups
        start = pl.multiple_of(lax.axis_index("rows") * share, share)
    for n in range(nodes):
        low = (n - 1) * rows + chunk * part if n > 0 else chunk * part
        lam = jnp.concatenate([item[low : low + part, :] for item in (lams if n > 0 else tops)], axis=0)
        if n == 0:
            ratio = jnp.concatenate([item[nodes] for item in posts], axis=0)
        else:
            slot = local_slot(parent_ref, n, nodes)
            q_par = jnp.concatenate([item[slot] for item in posts], axis=0)
            ratio = (q_par.astype(F32) / raw_ref[n - 1, chunk]).astype(BF16)
        flow = lax.dot_general(ratio, lam, (((0,), (0,)), ((), ())), preferred_element_type=F32)
        post = jnp.concatenate([item[n] for item in posts], axis=0)
        tally = jnp.dot(hot_ref[n, chunk], post, preferred_element_type=F32)
        if before is not None:
            flow += before[0][n]
            tally += before[1][n]
        if final:
            states, values = flow.shape[1], tally.shape[0]
            weight = w_ref[n, pl.ds(start, share), :].astype(F32)
            flow = weight * flow * (states * states / samples)
            tally = tally * (values * states / samples)
        for k, value in enumerate((flow, tally)):
            refs[k][n] = value.astype(refs[k].dtype)
            if final:
                copies.append(pltpu.make_async_copy(refs[k].at[n], homes[k].at[n], sems.at[k, n]))
                copies[-1].start()
    for copy in copies:
        copy.wait()


def swap(value, mask):
    return lax.ppermute(value, "rows", [(s, s ^ mask) for s in range(lax.axis_size("rows"))])


def hold(value, after):
    shape = pltpu.VMEM(value.shape, value.dtype)
    return run(lambda *refs: None, "hold", (value,), (shape,), same={0: 0}, after=after)[0]


def gather(blocks, after=()):
    for bit in reversed(range(lax.axis_size("rows").bit_length() - 1)):
        if 1 << bit in blocks:
            continue
        for place, block in list(blocks.items()):
            blocks[place | (1 << bit)] = swap(hold(block, after) if place and after else block, 1 << bit)
    return [blocks[place] for place in range(len(blocks))]


def far(value):
    half = lax.axis_size("rows") // 2
    return {0: value, half: swap(value, half)} if half else {0: value}


def per_device(mixing, emission, prior, parent, observed):
    nodes, states = mixing.shape[:2]
    rows = observed.shape[1]
    values = emission.shape[1]
    leaves = lax.axis_size("leaf")
    groups = lax.axis_size("rows")
    levels = leaves.bit_length() - 1
    share = states // groups
    part = rows // CHUNKS
    every = range(CHUNKS)
    half = functools.partial(pltpu.VMEM, (part, states))

    outs = run(
        functools.partial(prep_body, nodes),
        "prep",
        tuple(pltpu.with_memory_space_constraint(x, pltpu.HBM) for x in (parent, observed, emission, mixing)),
        (
            pltpu.VMEM(mixing.shape, BF16),
            pltpu.VMEM(((nodes - 1) * rows + PAD, states), BF16),
            pltpu.VMEM((nodes - 1, rows, states), F32),
        )
        + (half(F32),) * CHUNKS,
        (
            pltpu.VMEM((nodes - 1, rows, states), F32),
            pltpu.VMEM(emission.shape, BF16),
            pltpu.VMEM(observed.shape, jnp.int32),
            pltpu.SMEM(parent.shape, jnp.int32),
            pltpu.SemaphoreType.DMA((3, max(nodes, 2))),
        ),
        [ANY] * 4,
    )
    weights, lams, msgs = outs[:3]
    raw, send = list(outs[3:]), []
    for c in every:
        (block,) = run(first_body, "first", (raw[c], weights), (half(BF16),), after=[lams] if c > 0 else ())
        send.append(block)
        if c == 0:
            lams = hold(lams, (block,))

    def up_pairs(level):
        step = 1 << level
        return [(s, s - step) for s in range(leaves) if s % (2 * step) == step]

    def down_pairs(level):
        return [(b, a) for a, b in up_pairs(level)]

    for level in range(levels - 1):
        for c in every:
            recv = lax.ppermute(send[c], "leaf", up_pairs(level))
            raw[c], send[c] = run(
                functools.partial(lift_body, level),
                "lift",
                (raw[c], recv, weights),
                (half(F32), half(BF16)),
                same={0: 0},
                after=send[:c][-1:],
            )
        if level == 0:
            near = far(lams)
    top_lam, top_msg, ratio, post = ([None] * CHUNKS for _ in range(4))
    for c in every:
        recv = lax.ppermute(send[c], "leaf", up_pairs(levels - 1))
        final = c == CHUNKS - 1
        top_lam[c], top_msg[c], ratio[c], post[c], *merged = run(
            functools.partial(root_body, levels - 1),
            "root",
            (raw[c], recv, weights, prior.reshape(1, states)) + (tuple(top_lam[:c]) if final else ()),
            (half(BF16), half(F32), half(BF16), half(BF16)) + ((pltpu.VMEM((rows, states), BF16),) if final else ()),
        )
    all_tops = gather(far(merged[0]))
    all_lams = gather(near, send[-1:])
    raw_own, hots = run(
        functools.partial(ready_body, nodes, groups),
        "ready",
        (weights, *all_lams),
        (
            pltpu.VMEM((nodes - 1, CHUNKS, groups * part, share), F32),
            pltpu.VMEM((nodes, CHUNKS, values, groups * part), BF16),
        ),
        work=0.1,

    )
    for level in reversed(range(1, levels)):
        for c in every:
            recv = lax.ppermute(post[c], "leaf", down_pairs(level))
            ratio[c], post[c] = run(
                functools.partial(settle_body, level),
                "settle",
                (recv, top_lam[c], top_msg[c], weights, ratio[c], post[c]),
                (half(BF16), half(BF16)),
                after=post[:c][-1:] + ([raw_own] if level == 1 and c == 0 else []),
            )
    own_posts = []
    for c in every:
        recv = lax.ppermute(post[c], "leaf", down_pairs(0))
        packs = run(
            functools.partial(last_body, nodes, groups, c),
            "last",
            (parent, recv, top_lam[c], top_msg[c], weights, ratio[c], post[c], lams, msgs),
            (pltpu.VMEM((nodes + 1, part, share), BF16),) * groups,
            (pltpu.VMEM((nodes + 1, part, states), BF16),),
            [SM] + [VM] * 8,
            after=own_posts[-1][:1] + all_tops if c > 0 else (),
        )
        order = range(1, groups)
        moved = {mask: swap(packs[mask], mask) for mask in order}
        own_posts.append([packs[0]] + [moved[mask] for mask in range(1, groups)])
    sums = ()
    for c in every:
        final = c == CHUNKS - 1
        ins = (parent, raw_own, hots, *all_lams, *all_tops, *own_posts[c], *sums) + ((weights,) if final else ())
        shapes = ((nodes, share, states), (nodes, values, share))
        sums = run(
            functools.partial(counts_body, nodes, groups, c),
            "counts",
            ins,
            tuple(jax.ShapeDtypeStruct(x, BF16) if final else pltpu.VMEM(x, F32) for x in shapes),
            tuple(pltpu.VMEM(x, BF16) for x in shapes) + (pltpu.SemaphoreType.DMA((2, nodes)),) if final else (),
            [SM] + [VM] * (len(ins) - 1),
            (ANY, ANY) if final else None,
        )
    return tuple(sums)


def solution(mesh):
    placed = (P("leaf", None, None), P("leaf", None, None), P(), P("leaf"), P("leaf", "rows"))
    return jax.shard_map(
        per_device,
        mesh=mesh,
        in_specs=placed,
        out_specs=(P("leaf", "rows", None), P("leaf", None, "rows")),
        check_vma=False,
    )
```

```python
import functools
import jax
import jax.numpy as jnp
from jax import lax
from jax.experimental import pallas as pl
from jax.experimental.pallas import tpu as pltpu
from jax.sharding import PartitionSpec as P

F32 = jnp.float32
BF16 = jnp.bfloat16
PAD = 16
CHUNKS = 2
WORK = 13*10**8
LIMIT = 24 * 2**20
VM = pl.BlockSpec(memory_space=pltpu.VMEM)
SM = pl.BlockSpec(memory_space=pltpu.SMEM)
ANY = pl.BlockSpec(memory_space=pl.ANY)


def run(body, name, ins, outs, scratch=(), specs=None, out_specs=None, same=None, after=(), work=1.0):
    count, idle = len(ins), len(ins) + len(after)
    return pl.pallas_call(
        lambda *refs: body(*refs[:count], *refs[idle:]),
        name=name,
        in_specs=(specs or [VM] * count) + [VM] * len(after),
        out_specs=out_specs or tuple(VM for _ in outs),
        out_shape=tuple(outs),
        input_output_aliases=same or {},
        scratch_shapes=list(scratch),
        compiler_params=pltpu.CompilerParams(vmem_limit_bytes=LIMIT),
        cost_estimate=pl.CostEstimate(flops=int(work * WORK), bytes_accessed=2**21, transcendentals=0),
    )(*ins, *after)


def scaled(raw):
    return (raw * (1.0 / jnp.mean(raw, axis=1, keepdims=True))).astype(BF16)


def upward(lam, weight):
    rows = lam.shape[0]
    stacked = jnp.concatenate([lam, jnp.ones((PAD, lam.shape[1]), BF16)], axis=0)
    both = lax.dot_general(stacked, weight, (((1,), (1,)), ((), ())), preferred_element_type=F32)
    return both[:rows], both[rows : rows + 1]


def downward(q_par, raw_msg, lam, weight):
    ratio = (q_par / raw_msg).astype(BF16)
    post = lam.astype(F32) * jnp.dot(ratio, weight, preferred_element_type=F32)
    return ratio, post.astype(BF16)


def one_hot(row, values):
    return (lax.broadcasted_iota(jnp.int32, (values, row.shape[1]), 0) == row).astype(F32).astype(BF16)


def local_slot(parent_ref, node, nodes):
    return jnp.clip(parent_ref[node] - lax.axis_index("leaf") * nodes, 0, node - 1)


def is_upper(level):
    return jnp.bitwise_and(lax.axis_index("leaf"), (2 << level) - 1) == 0


def is_lower(level):
    return jnp.bitwise_and(lax.axis_index("leaf"), (2 << level) - 1) == (1 << level)


def prep_body(nodes, parent_hbm, obs_hbm, emission_hbm, mixing_hbm, *refs):
    w_ref, lam_ref, msg_ref = refs[:3]
    u_refs = refs[3 : 3 + CHUNKS]
    prods, tables, obs, parent_ref, sems = refs[3 + CHUNKS :]
    copy_obs = pltpu.make_async_copy(obs_hbm, obs, sems.at[2, 0])
    copy_parent = pltpu.make_async_copy(parent_hbm, parent_ref, sems.at[2, 1])
    copies_w = [pltpu.make_async_copy(mixing_hbm.at[n], w_ref.at[n], sems.at[0, n]) for n in range(nodes)]
    copies_e = [pltpu.make_async_copy(emission_hbm.at[n], tables.at[n], sems.at[1, n]) for n in range(nodes)]
    copy_obs.start()
    copy_parent.start()
    for n in reversed(range(nodes)):
        copies_e[n].start()
        copies_w[n].start()
    values = tables.shape[1]
    rows = obs.shape[1]
    part = rows // CHUNKS
    for n in range(nodes - 1):
        prods[n] = jnp.ones(prods.shape[1:], F32)
    copy_obs.wait()
    index = lax.broadcasted_iota(jnp.int32, (PAD, rows), 0)
    listed = jnp.zeros((PAD, rows), jnp.int32)
    for n in range(nodes):
        listed = jnp.where(index == n, obs[n : n + 1, :], listed)
    base = (nodes - 1) * rows
    lam_ref[base : base + PAD, :] = jnp.zeros((PAD, lam_ref.shape[1]), BF16)
    lam_ref[base : base + PAD, :rows] = listed.astype(F32).astype(BF16)
    copy_parent.wait()
    for n in reversed(range(nodes)):
        copies_e[n].wait()
        hot = one_hot(obs[n : n + 1, :], values)
        table = tables[n]
        picked = lax.dot_general(hot, table, (((0,), (0,)), ((), ())), preferred_element_type=F32)
        total = jnp.dot(jnp.ones((PAD, values), BF16), table, preferred_element_type=F32)[:1]
        raw = (picked * (1.0 / total)).astype(BF16).astype(F32)
        if n < nodes - 1:
            raw = raw * prods[n]
        if n > 0:
            lam = scaled(raw)
            copies_w[n].wait()
            raw_msg, sums = upward(lam, w_ref[n])
            lam_ref[(n - 1) * rows : n * rows, :] = lam
            msg_ref[n - 1] = raw_msg
            slot = local_slot(parent_ref, n, nodes)
            prods[slot] = prods[slot] * (raw_msg * (1.0 / sums))
        else:
            for c in range(CHUNKS):
                u_refs[c][...] = raw[c * part : (c + 1) * part]
    copies_w[0].wait()


def send_up(level, raw_ref, w_ref, send_ref):
    @pl.when(is_lower(level))
    def _():
        raw_msg, sums = upward(scaled(raw_ref[...]), w_ref[0])
        send_ref[...] = (raw_msg * (1.0 / sums)).astype(BF16)


def first_body(u_ref, w_ref, send_ref):
    send_up(0, u_ref, w_ref, send_ref)


def lift_body(level, u_ref, recv_ref, w_ref, u_out, send_ref):
    @pl.when(is_upper(level))
    def _():
        u_out[...] = u_ref[...] * recv_ref[...].astype(F32)

    send_up(level + 1, u_out, w_ref, send_ref)


def root_body(level, u_ref, recv_ref, w_ref, prior_ref, *refs):
    lam_ref, msg_ref, ratio_ref, post_ref = refs[-5:-1] if len(refs) > 4 else refs
    lam = scaled(u_ref[...] * jnp.where(is_upper(level), recv_ref[...].astype(F32), 1.0))
    raw_msg, sums = upward(lam, w_ref[0])
    lam_ref[...] = lam
    msg_ref[...] = raw_msg
    if len(refs) > 4:
        for c, block in enumerate([item[...] for item in refs[:-5]] + [lam]):
            refs[-1][c * lam.shape[0] : (c + 1) * lam.shape[0], :] = block

    @pl.when(lax.axis_index("leaf") == 0)
    def _():
        prior = prior_ref[...]
        weighted = (prior / jnp.sum(prior)) * (raw_msg * (1.0 / sums))
        share = weighted / jnp.sum(weighted, axis=1, keepdims=True)
        ratio, post = downward(share, raw_msg, lam, w_ref[0])
        ratio_ref[...] = ratio
        post_ref[...] = post


def settle_body(level, recv_ref, lam_ref, msg_ref, w_ref, ratio_in, post_in, ratio_ref, post_ref):
    got = is_lower(level)

    @pl.when(got)
    def _():
        ratio, post = downward(recv_ref[...].astype(F32), msg_ref[...], lam_ref[...], w_ref[0])
        ratio_ref[...] = ratio
        post_ref[...] = post

    @pl.when(jnp.logical_not(got))
    def _():
        ratio_ref[...] = ratio_in[...]
        post_ref[...] = post_in[...]


def last_body(nodes, groups, chunk, parent_ref, recv_ref, lam_ref, msg_ref, w_ref, ratio_in, post_in, lams_ref, msgs_ref, *refs):
    packs, posts = refs[:groups], refs[groups]
    rows, part = msgs_ref.shape[1], lam_ref.shape[0]
    share = lam_ref.shape[1] // groups
    got = is_lower(0)

    @pl.when(got)
    def _():
        ratio, post = downward(recv_ref[...].astype(F32), msg_ref[...], lam_ref[...], w_ref[0])
        posts[nodes] = ratio
        posts[0] = post

    @pl.when(jnp.logical_not(got))
    def _():
        posts[nodes] = ratio_in[...]
        posts[0] = post_in[...]

    for n in range(1, nodes):
        q_par = posts[local_slot(parent_ref, n, nodes)].astype(F32)
        low = (n - 1) * rows + chunk * part
        raw_msg = msgs_ref[n - 1, chunk * part : (chunk + 1) * part, :]
        _, posts[n] = downward(q_par, raw_msg, lams_ref[low : low + part, :], w_ref[n])
    own = lax.axis_index("rows")
    for mask in range(groups):
        start = pl.multiple_of(jnp.bitwise_xor(own, mask) * share, share)
        packs[mask][...] = posts[:, :, pl.ds(start, share)]


def ready_body(nodes, groups, w_ref, *refs):
    lams, (raw_ref, hot_ref) = refs[:groups], refs[groups:]
    chunks, merged, share = raw_ref.shape[1:]
    part = merged // groups
    rows = part * chunks
    values = hot_ref.shape[2]
    base = (nodes - 1) * rows
    start = pl.multiple_of(lax.axis_index("rows") * share, share)
    for n in range(nodes):
        observed = [lam[base : base + PAD, :rows].astype(F32).astype(jnp.int32)[n : n + 1] for lam in lams]
        for c in range(chunks):
            row = jnp.concatenate([item[:, c * part : (c + 1) * part] for item in observed], axis=1)
            hot_ref[n, c] = one_hot(row, values)
        if n > 0:
            weight = w_ref[n, pl.ds(start, share), :]
            for c in range(chunks):
                low = (n - 1) * rows + c * part
                lam = jnp.concatenate([item[low : low + part, :] for item in lams], axis=0)
                raw_ref[n - 1, c] = lax.dot_general(lam, weight, (((1,), (1,)), ((), ())), preferred_element_type=F32)


def counts_body(nodes, groups, chunk, parent_ref, raw_ref, hot_ref, *refs):
    lams, tops, posts = refs[:groups], refs[groups : 2 * groups], refs[2 * groups : 3 * groups]
    refs = refs[3 * groups :]
    chunks = raw_ref.shape[1]
    part = raw_ref.shape[2] // groups
    rows = part * chunks
    before = refs[:2] if chunk > 0 else None
    refs = refs[2:] if chunk > 0 else refs
    final = chunk == chunks - 1
    copies = []
    if final:
        w_ref, homes, refs, sems = refs[0], refs[1:3], refs[3:5], refs[5]
        share = refs[0].shape[1]
        samples = rows * groups
        start = pl.multiple_of(lax.axis_index("rows") * share, share)
    for n in range(nodes):
        low = (n - 1) * rows + chunk * part if n > 0 else chunk * part
        lam = jnp.concatenate([item[low : low + part, :] for item in (lams if n > 0 else tops)], axis=0)
        if n == 0:
            ratio = jnp.concatenate([item[nodes] for item in posts], axis=0)
        else:
            slot = local_slot(parent_ref, n, nodes)
            q_par = jnp.concatenate([item[slot] for item in posts], axis=0)
            ratio = (q_par.astype(F32) / raw_ref[n - 1, chunk]).astype(BF16)
        flow = lax.dot_general(ratio, lam, (((0,), (0,)), ((), ())), preferred_element_type=F32)
        post = jnp.concatenate([item[n] for item in posts], axis=0)
        tally = jnp.dot(hot_ref[n, chunk], post, preferred_element_type=F32)
        if before is not None:
            flow += before[0][n]
            tally += before[1][n]
        if final:
            states, values = flow.shape[1], tally.shape[0]
            weight = w_ref[n, pl.ds(start, share), :].astype(F32)
            flow = weight * flow * (states * states / samples)
            tally = tally * (values * states / samples)
        for k, value in enumerate((flow, tally)):
            refs[k][n] = value.astype(refs[k].dtype)
            if final:
                copies.append(pltpu.make_async_copy(refs[k].at[n], homes[k].at[n], sems.at[k, n]))
                copies[-1].start()
    for copy in copies:
        copy.wait()


def swap(value, mask):
    return lax.ppermute(value, "rows", [(s, s ^ mask) for s in range(lax.axis_size("rows"))])


def hold(value, after):
    shape = pltpu.VMEM(value.shape, value.dtype)
    return run(lambda *refs: None, "hold", (value,), (shape,), same={0: 0}, after=after)[0]


def gather(blocks, after=()):
    for bit in reversed(range(lax.axis_size("rows").bit_length() - 1)):
        if 1 << bit in blocks:
            continue
        for place, block in list(blocks.items()):
            blocks[place | (1 << bit)] = swap(hold(block, after) if place and after else block, 1 << bit)
    return [blocks[place] for place in range(len(blocks))]


def far(value):
    half = lax.axis_size("rows") // 2
    return {0: value, half: swap(value, half)} if half else {0: value}


def per_device(mixing, emission, prior, parent, observed):
    nodes, states = mixing.shape[:2]
    rows = observed.shape[1]
    values = emission.shape[1]
    leaves = lax.axis_size("leaf")
    groups = lax.axis_size("rows")
    levels = leaves.bit_length() - 1
    share = states // groups
    part = rows // CHUNKS
    every = range(CHUNKS)
    half = functools.partial(pltpu.VMEM, (part, states))

    outs = run(
        functools.partial(prep_body, nodes),
        "prep",
        tuple(pltpu.with_memory_space_constraint(x, pltpu.HBM) for x in (parent, observed, emission, mixing)),
        (
            pltpu.VMEM(mixing.shape, BF16),
            pltpu.VMEM(((nodes - 1) * rows + PAD, states), BF16),
            pltpu.VMEM((nodes - 1, rows, states), F32),
        )
        + (half(F32),) * CHUNKS,
        (
            pltpu.VMEM((nodes - 1, rows, states), F32),
            pltpu.VMEM(emission.shape, BF16),
            pltpu.VMEM(observed.shape, jnp.int32),
            pltpu.SMEM(parent.shape, jnp.int32),
            pltpu.SemaphoreType.DMA((3, max(nodes, 2))),
        ),
        [ANY] * 4,
    )
    weights, lams, msgs = outs[:3]
    raw, send = list(outs[3:]), []
    for c in every:
        (block,) = run(first_body, "first", (raw[c], weights), (half(BF16),), after=[lams] if c > 0 else ())
        send.append(block)
        if c == 0:
            lams = hold(lams, (block,))

    def up_pairs(level):
        step = 1 << level
        return [(s, s - step) for s in range(leaves) if s % (2 * step) == step]

    def down_pairs(level):
        return [(b, a) for a, b in up_pairs(level)]

    for level in range(levels - 1):
        for c in every:
            recv = lax.ppermute(send[c], "leaf", up_pairs(level))
            raw[c], send[c] = run(
                functools.partial(lift_body, level),
                "lift",
                (raw[c], recv, weights),
                (half(F32), half(BF16)),
                same={0: 0},
                after=send[:c][-1:],
            )
        if level == 0:
            near = far(lams)
    top_lam, top_msg, ratio, post = ([None] * CHUNKS for _ in range(4))
    for c in every:
        recv = lax.ppermute(send[c], "leaf", up_pairs(levels - 1))
        final = c == CHUNKS - 1
        top_lam[c], top_msg[c], ratio[c], post[c], *merged = run(
            functools.partial(root_body, levels - 1),
            "root",
            (raw[c], recv, weights, prior.reshape(1, states)) + (tuple(top_lam[:c]) if final else ()),
            (half(BF16), half(F32), half(BF16), half(BF16)) + ((pltpu.VMEM((rows, states), BF16),) if final else ()),
        )
    all_tops = gather(far(merged[0]))
    all_lams = gather(near, send[-1:])
    raw_own, hots = run(
        functools.partial(ready_body, nodes, groups),
        "ready",
        (weights, *all_lams),
        (
            pltpu.VMEM((nodes - 1, CHUNKS, groups * part, share), F32),
            pltpu.VMEM((nodes, CHUNKS, values, groups * part), BF16),
        ),
        work=0.1,

    )
    for level in reversed(range(1, levels)):
        for c in every:
            recv = lax.ppermute(post[c], "leaf", down_pairs(level))
            ratio[c], post[c] = run(
                functools.partial(settle_body, level),
                "settle",
                (recv, top_lam[c], top_msg[c], weights, ratio[c], post[c]),
                (half(BF16), half(BF16)),
                after=post[:c][-1:] + (all_lams if level == 1 and c == CHUNKS - 1 else []),
            )
    own_posts = []
    for c in every:
        recv = lax.ppermute(post[c], "leaf", down_pairs(0))
        packs = run(
            functools.partial(last_body, nodes, groups, c),
            "last",
            (parent, recv, top_lam[c], top_msg[c], weights, ratio[c], post[c], lams, msgs),
            (pltpu.VMEM((nodes + 1, part, share), BF16),) * groups,
            (pltpu.VMEM((nodes + 1, part, states), BF16),),
            [SM] + [VM] * 8,
            after=[own_posts[-1][0], *all_tops, raw_own] if c > 0 else [],
        )
        order = range(1, groups)
        moved = {mask: swap(packs[mask], mask) for mask in order}
        own_posts.append([packs[0]] + [moved[mask] for mask in range(1, groups)])
    sums = ()
    for c in every:
        final = c == CHUNKS - 1
        ins = (parent, raw_own, hots, *all_lams, *all_tops, *own_posts[c], *sums) + ((weights,) if final else ())
        shapes = ((nodes, share, states), (nodes, values, share))
        sums = run(
            functools.partial(counts_body, nodes, groups, c),
            "counts",
            ins,
            tuple(jax.ShapeDtypeStruct(x, BF16) if final else pltpu.VMEM(x, F32) for x in shapes),
            tuple(pltpu.VMEM(x, BF16) for x in shapes) + (pltpu.SemaphoreType.DMA((2, nodes)),) if final else (),
            [SM] + [VM] * (len(ins) - 1),
            (ANY, ANY) if final else None,
        )
    return tuple(sums)


def solution(mesh):
    placed = (P("leaf", None, None), P("leaf", None, None), P(), P("leaf"), P("leaf", "rows"))
    return jax.shard_map(
        per_device,
        mesh=mesh,
        in_specs=placed,
        out_specs=(P("leaf", "rows", None), P("leaf", None, "rows")),
        check_vma=False,
    )
```

```python
import functools
import jax
import jax.numpy as jnp
from jax import lax
from jax.experimental import pallas as pl
from jax.experimental.pallas import tpu as pltpu
from jax.sharding import PartitionSpec as P

F32 = jnp.float32
BF16 = jnp.bfloat16
PAD = 16
CHUNKS = 2
WORK = 13*10**8
LIMIT = 24 * 2**20
VM = pl.BlockSpec(memory_space=pltpu.VMEM)
SM = pl.BlockSpec(memory_space=pltpu.SMEM)
ANY = pl.BlockSpec(memory_space=pl.ANY)


def run(body, name, ins, outs, scratch=(), specs=None, out_specs=None, same=None, after=(), work=1.0):
    count, idle = len(ins), len(ins) + len(after)
    return pl.pallas_call(
        lambda *refs: body(*refs[:count], *refs[idle:]),
        name=name,
        in_specs=(specs or [VM] * count) + [VM] * len(after),
        out_specs=out_specs or tuple(VM for _ in outs),
        out_shape=tuple(outs),
        input_output_aliases=same or {},
        scratch_shapes=list(scratch),
        compiler_params=pltpu.CompilerParams(vmem_limit_bytes=LIMIT),
        cost_estimate=pl.CostEstimate(flops=int(work * WORK), bytes_accessed=2**21, transcendentals=0),
    )(*ins, *after)


def scaled(raw):
    return (raw * (1.0 / jnp.mean(raw, axis=1, keepdims=True))).astype(BF16)


def upward(lam, weight):
    rows = lam.shape[0]
    stacked = jnp.concatenate([lam, jnp.ones((PAD, lam.shape[1]), BF16)], axis=0)
    both = lax.dot_general(stacked, weight, (((1,), (1,)), ((), ())), preferred_element_type=F32)
    return both[:rows], both[rows : rows + 1]


def downward(q_par, raw_msg, lam, weight):
    ratio = (q_par / raw_msg).astype(BF16)
    post = lam.astype(F32) * jnp.dot(ratio, weight, preferred_element_type=F32)
    return ratio, post.astype(BF16)


def one_hot(row, values):
    return (lax.broadcasted_iota(jnp.int32, (values, row.shape[1]), 0) == row).astype(F32).astype(BF16)


def local_slot(parent_ref, node, nodes):
    return jnp.clip(parent_ref[node] - lax.axis_index("leaf") * nodes, 0, node - 1)


def is_upper(level):
    return jnp.bitwise_and(lax.axis_index("leaf"), (2 << level) - 1) == 0


def is_lower(level):
    return jnp.bitwise_and(lax.axis_index("leaf"), (2 << level) - 1) == (1 << level)


def root_base(w_ref, prior_ref, base_ref):
    states = base_ref.shape[1]
    sums = lax.dot_general(jnp.ones((PAD, states), BF16), w_ref[0], (((1,), (1,)), ((), ())), preferred_element_type=F32)
    prior = prior_ref[...]
    odds = (prior / jnp.sum(prior)) / sums[:1]
    high = odds.astype(BF16).astype(F32)
    index = lax.broadcasted_iota(jnp.int32, (PAD, states), 0)
    stacked = jnp.where(index == 0, high, jnp.where(index == 1, odds - high, 0.0)).astype(BF16)
    both = jnp.dot(stacked, w_ref[0], preferred_element_type=F32)
    base_ref[0:1, :] = both[0:1] + both[1:2]
    base_ref[1:2, :] = odds


def prep_body(nodes, parent_hbm, obs_hbm, emission_hbm, mixing_hbm, prior_hbm, *refs):
    w_ref, lam_ref, msg_ref, base_ref = refs[:4]
    u_refs = refs[4 : 4 + CHUNKS]
    prods, tables, obs, parent_ref, prior_ref, sems = refs[4 + CHUNKS :]
    copy_prior = pltpu.make_async_copy(prior_hbm, prior_ref, sems.at[3, 0])
    copy_obs = pltpu.make_async_copy(obs_hbm, obs, sems.at[2, 0])
    copy_parent = pltpu.make_async_copy(parent_hbm, parent_ref, sems.at[2, 1])
    copies_w = [pltpu.make_async_copy(mixing_hbm.at[n], w_ref.at[n], sems.at[0, n]) for n in range(nodes)]
    copies_e = [pltpu.make_async_copy(emission_hbm.at[n], tables.at[n], sems.at[1, n]) for n in range(nodes)]
    copy_obs.start()
    copy_parent.start()
    for n in reversed(range(nodes)):
        copies_e[n].start()
        copies_w[n].start()
    copy_prior.start()
    values = tables.shape[1]
    rows = obs.shape[1]
    part = rows // CHUNKS
    for n in range(nodes - 1):
        prods[n] = jnp.ones(prods.shape[1:], F32)
    copy_obs.wait()
    index = lax.broadcasted_iota(jnp.int32, (PAD, rows), 0)
    listed = jnp.zeros((PAD, rows), jnp.int32)
    for n in range(nodes):
        listed = jnp.where(index == n, obs[n : n + 1, :], listed)
    base = (nodes - 1) * rows
    lam_ref[base : base + PAD, :] = jnp.zeros((PAD, lam_ref.shape[1]), BF16)
    lam_ref[base : base + PAD, :rows] = listed.astype(F32).astype(BF16)
    copy_parent.wait()
    for n in reversed(range(nodes)):
        copies_e[n].wait()
        hot = one_hot(obs[n : n + 1, :], values)
        table = tables[n]
        picked = lax.dot_general(hot, table, (((0,), (0,)), ((), ())), preferred_element_type=F32)
        total = jnp.dot(jnp.ones((PAD, values), BF16), table, preferred_element_type=F32)[:1]
        raw = (picked * (1.0 / total)).astype(BF16).astype(F32)
        if n < nodes - 1:
            raw = raw * prods[n]
        if n > 0:
            lam = scaled(raw)
            copies_w[n].wait()
            raw_msg, sums = upward(lam, w_ref[n])
            lam_ref[(n - 1) * rows : n * rows, :] = lam
            msg_ref[n - 1] = raw_msg
            slot = local_slot(parent_ref, n, nodes)
            prods[slot] = prods[slot] * (raw_msg * (1.0 / sums))
        else:
            for c in range(CHUNKS):
                u_refs[c][...] = raw[c * part : (c + 1) * part]
    copies_w[0].wait()
    copy_prior.wait()

    @pl.when(lax.axis_index("leaf") == 0)
    def _():
        root_base(w_ref, prior_ref, base_ref)


def send_up(level, raw_ref, w_ref, send_ref):
    @pl.when(is_lower(level))
    def _():
        raw_msg, sums = upward(scaled(raw_ref[...]), w_ref[0])
        send_ref[...] = (raw_msg * (1.0 / sums)).astype(BF16)


def first_body(u_ref, w_ref, send_ref):
    send_up(0, u_ref, w_ref, send_ref)


def lift_body(level, u_ref, recv_ref, w_ref, u_out, send_ref):
    @pl.when(is_upper(level))
    def _():
        u_out[...] = u_ref[...] * recv_ref[...].astype(F32)

    send_up(level + 1, u_out, w_ref, send_ref)


def root_body(level, u_ref, recv_ref, w_ref, base_ref, *refs):
    lam_ref, msg_ref, ratio_ref, post_ref = refs[-5:-1] if len(refs) > 4 else refs
    lam = scaled(u_ref[...] * jnp.where(is_upper(level), recv_ref[...].astype(F32), 1.0))
    lam_ref[...] = lam
    if len(refs) > 4:
        for c, block in enumerate([item[...] for item in refs[:-5]] + [lam]):
            refs[-1][c * lam.shape[0] : (c + 1) * lam.shape[0], :] = block
    top = lax.axis_index("leaf") == 0

    @pl.when(top)
    def _():
        terms = lam.astype(F32) * base_ref[0:1, :]
        inverse = 1.0 / jnp.sum(terms, axis=1, keepdims=True)
        ratio_ref[...] = (base_ref[1:2, :] * inverse).astype(BF16)
        post_ref[...] = (terms * inverse).astype(BF16)

    @pl.when(jnp.logical_not(top))
    def _():
        msg_ref[...] = lax.dot_general(lam, w_ref[0], (((1,), (1,)), ((), ())), preferred_element_type=F32)


def settle_body(level, recv_ref, lam_ref, msg_ref, w_ref, ratio_in, post_in, ratio_ref, post_ref):
    got = is_lower(level)

    @pl.when(got)
    def _():
        ratio, post = downward(recv_ref[...].astype(F32), msg_ref[...], lam_ref[...], w_ref[0])
        ratio_ref[...] = ratio
        post_ref[...] = post

    @pl.when(jnp.logical_not(got))
    def _():
        ratio_ref[...] = ratio_in[...]
        post_ref[...] = post_in[...]


def last_body(nodes, groups, chunk, parent_ref, recv_ref, lam_ref, msg_ref, w_ref, ratio_in, post_in, lams_ref, msgs_ref, *refs):
    packs, posts = refs[:groups], refs[groups]
    rows, part = msgs_ref.shape[1], lam_ref.shape[0]
    share = lam_ref.shape[1] // groups
    got = is_lower(0)

    @pl.when(got)
    def _():
        ratio, post = downward(recv_ref[...].astype(F32), msg_ref[...], lam_ref[...], w_ref[0])
        posts[nodes] = ratio
        posts[0] = post

    @pl.when(jnp.logical_not(got))
    def _():
        posts[nodes] = ratio_in[...]
        posts[0] = post_in[...]

    for n in range(1, nodes):
        q_par = posts[local_slot(parent_ref, n, nodes)].astype(F32)
        low = (n - 1) * rows + chunk * part
        raw_msg = msgs_ref[n - 1, chunk * part : (chunk + 1) * part, :]
        _, posts[n] = downward(q_par, raw_msg, lams_ref[low : low + part, :], w_ref[n])
    own = lax.axis_index("rows")
    for mask in range(groups):
        start = pl.multiple_of(jnp.bitwise_xor(own, mask) * share, share)
        packs[mask][...] = posts[:, :, pl.ds(start, share)]


def ready_body(nodes, groups, w_ref, *refs):
    lams, (raw_ref, hot_ref) = refs[:groups], refs[groups:]
    chunks, merged, share = raw_ref.shape[1:]
    part = merged // groups
    rows = part * chunks
    values = hot_ref.shape[2]
    base = (nodes - 1) * rows
    start = pl.multiple_of(lax.axis_index("rows") * share, share)
    for n in range(nodes):
        observed = [lam[base : base + PAD, :rows].astype(F32).astype(jnp.int32)[n : n + 1] for lam in lams]
        for c in range(chunks):
            row = jnp.concatenate([item[:, c * part : (c + 1) * part] for item in observed], axis=1)
            hot_ref[n, c] = one_hot(row, values)
        if n > 0:
            weight = w_ref[n, pl.ds(start, share), :]
            for c in range(chunks):
                low = (n - 1) * rows + c * part
                lam = jnp.concatenate([item[low : low + part, :] for item in lams], axis=0)
                raw_ref[n - 1, c] = lax.dot_general(lam, weight, (((1,), (1,)), ((), ())), preferred_element_type=F32)


def counts_body(nodes, groups, chunk, parent_ref, raw_ref, hot_ref, *refs):
    lams, tops, posts = refs[:groups], refs[groups : 2 * groups], refs[2 * groups : 3 * groups]
    refs = refs[3 * groups :]
    chunks = raw_ref.shape[1]
    part = raw_ref.shape[2] // groups
    rows = part * chunks
    before = refs[:2] if chunk > 0 else None
    refs = refs[2:] if chunk > 0 else refs
    final = chunk == chunks - 1
    copies = []
    if final:
        w_ref, homes, refs, sems = refs[0], refs[1:3], refs[3:5], refs[5]
        share = refs[0].shape[1]
        samples = rows * groups
        start = pl.multiple_of(lax.axis_index("rows") * share, share)
    for n in range(nodes):
        low = (n - 1) * rows + chunk * part if n > 0 else chunk * part
        lam = jnp.concatenate([item[low : low + part, :] for item in (lams if n > 0 else tops)], axis=0)
        if n == 0:
            ratio = jnp.concatenate([item[nodes] for item in posts], axis=0)
        else:
            slot = local_slot(parent_ref, n, nodes)
            q_par = jnp.concatenate([item[slot] for item in posts], axis=0)
            ratio = (q_par.astype(F32) / raw_ref[n - 1, chunk]).astype(BF16)
        flow = lax.dot_general(ratio, lam, (((0,), (0,)), ((), ())), preferred_element_type=F32)
        post = jnp.concatenate([item[n] for item in posts], axis=0)
        tally = jnp.dot(hot_ref[n, chunk], post, preferred_element_type=F32)
        if before is not None:
            flow += before[0][n]
            tally += before[1][n]
        if final:
            states, values = flow.shape[1], tally.shape[0]
            weight = w_ref[n, pl.ds(start, share), :].astype(F32)
            flow = weight * flow * (states * states / samples)
            tally = tally * (values * states / samples)
        for k, value in enumerate((flow, tally)):
            refs[k][n] = value.astype(refs[k].dtype)
            if final:
                copies.append(pltpu.make_async_copy(refs[k].at[n], homes[k].at[n], sems.at[k, n]))
                copies[-1].start()
    for copy in copies:
        copy.wait()


def swap(value, mask):
    return lax.ppermute(value, "rows", [(s, s ^ mask) for s in range(lax.axis_size("rows"))])


def hold(value, after):
    shape = pltpu.VMEM(value.shape, value.dtype)
    return run(lambda *refs: None, "hold", (value,), (shape,), same={0: 0}, after=after)[0]


def gather(blocks, after=()):
    for bit in reversed(range(lax.axis_size("rows").bit_length() - 1)):
        if 1 << bit in blocks:
            continue
        for place, block in list(blocks.items()):
            blocks[place | (1 << bit)] = swap(hold(block, after) if place and after else block, 1 << bit)
    return [blocks[place] for place in range(len(blocks))]


def far(value):
    half = lax.axis_size("rows") // 2
    return {0: value, half: swap(value, half)} if half else {0: value}


def per_device(mixing, emission, prior, parent, observed):
    nodes, states = mixing.shape[:2]
    rows = observed.shape[1]
    values = emission.shape[1]
    leaves = lax.axis_size("leaf")
    groups = lax.axis_size("rows")
    levels = leaves.bit_length() - 1
    share = states // groups
    part = rows // CHUNKS
    every = range(CHUNKS)
    half = functools.partial(pltpu.VMEM, (part, states))

    outs = run(
        functools.partial(prep_body, nodes),
        "prep",
        tuple(pltpu.with_memory_space_constraint(x, pltpu.HBM) for x in (parent, observed, emission, mixing, prior.reshape(1, states))),
        (
            pltpu.VMEM(mixing.shape, BF16),
            pltpu.VMEM(((nodes - 1) * rows + PAD, states), BF16),
            pltpu.VMEM((nodes - 1, rows, states), F32),
            pltpu.VMEM((8, states), F32),
        )
        + (half(F32),) * CHUNKS,
        (
            pltpu.VMEM((nodes - 1, rows, states), F32),
            pltpu.VMEM(emission.shape, BF16),
            pltpu.VMEM(observed.shape, jnp.int32),
            pltpu.SMEM(parent.shape, jnp.int32),
            pltpu.VMEM((1, states), F32),
            pltpu.SemaphoreType.DMA((4, max(nodes, 2))),
        ),
        [ANY] * 5,
    )
    weights, lams, msgs, base = outs[:4]
    raw, send = list(outs[4:]), []
    for c in every:
        (block,) = run(first_body, "first", (raw[c], weights), (half(BF16),), after=[lams] if c > 0 else ())
        send.append(block)
        if c == 0:
            lams = hold(lams, (block,))

    def up_pairs(level):
        step = 1 << level
        return [(s, s - step) for s in range(leaves) if s % (2 * step) == step]

    def down_pairs(level):
        return [(b, a) for a, b in up_pairs(level)]

    for level in range(levels - 1):
        for c in every:
            recv = lax.ppermute(send[c], "leaf", up_pairs(level))
            raw[c], send[c] = run(
                functools.partial(lift_body, level),
                "lift",
                (raw[c], recv, weights),
                (half(F32), half(BF16)),
                same={0: 0},
                after=send[:c][-1:],
            )
        if level == 0:
            near = far(lams)
    top_lam, top_msg, ratio, post = ([None] * CHUNKS for _ in range(4))
    for c in every:
        recv = lax.ppermute(send[c], "leaf", up_pairs(levels - 1))
        final = c == CHUNKS - 1
        top_lam[c], top_msg[c], ratio[c], post[c], *merged = run(
            functools.partial(root_body, levels - 1),
            "root",
            (raw[c], recv, weights, base) + (tuple(top_lam[:c]) if final else ()),
            (half(BF16), half(F32), half(BF16), half(BF16)) + ((pltpu.VMEM((rows, states), BF16),) if final else ()),
        )
    all_tops = gather(far(merged[0]))
    all_lams = gather(near, send[-1:])
    raw_own, hots = run(
        functools.partial(ready_body, nodes, groups),
        "ready",
        (weights, *all_lams),
        (
            pltpu.VMEM((nodes - 1, CHUNKS, groups * part, share), F32),
            pltpu.VMEM((nodes, CHUNKS, values, groups * part), BF16),
        ),
        work=0.1,

    )
    for level in reversed(range(1, levels)):
        for c in every:
            recv = lax.ppermute(post[c], "leaf", down_pairs(level))
            ratio[c], post[c] = run(
                functools.partial(settle_body, level),
                "settle",
                (recv, top_lam[c], top_msg[c], weights, ratio[c], post[c]),
                (half(BF16), half(BF16)),
                after=post[:c][-1:] + (all_lams if level == 1 and c == CHUNKS - 1 else []),
            )
    own_posts = []
    for c in every:
        recv = lax.ppermute(post[c], "leaf", down_pairs(0))
        packs = run(
            functools.partial(last_body, nodes, groups, c),
            "last",
            (parent, recv, top_lam[c], top_msg[c], weights, ratio[c], post[c], lams, msgs),
            (pltpu.VMEM((nodes + 1, part, share), BF16),) * groups,
            (pltpu.VMEM((nodes + 1, part, states), BF16),),
            [SM] + [VM] * 8,
            after=[own_posts[-1][0], *all_tops, raw_own] if c > 0 else [],
        )
        order = sorted(range(1, groups), reverse=c < CHUNKS - 1)
        moved = {mask: swap(packs[mask], mask) for mask in order}
        own_posts.append([packs[0]] + [moved[mask] for mask in range(1, groups)])
    sums = ()
    for c in every:
        final = c == CHUNKS - 1
        ins = (parent, raw_own, hots, *all_lams, *all_tops, *own_posts[c], *sums) + ((weights,) if final else ())
        shapes = ((nodes, share, states), (nodes, values, share))
        sums = run(
            functools.partial(counts_body, nodes, groups, c),
            "counts",
            ins,
            tuple(jax.ShapeDtypeStruct(x, BF16) if final else pltpu.VMEM(x, F32) for x in shapes),
            tuple(pltpu.VMEM(x, BF16) for x in shapes) + (pltpu.SemaphoreType.DMA((2, nodes)),) if final else (),
            [SM] + [VM] * (len(ins) - 1),
            (ANY, ANY) if final else None,
        )
    return tuple(sums)


def solution(mesh):
    placed = (P("leaf", None, None), P("leaf", None, None), P(), P("leaf"), P("leaf", "rows"))
    return jax.shard_map(
        per_device,
        mesh=mesh,
        in_specs=placed,
        out_specs=(P("leaf", "rows", None), P("leaf", None, "rows")),
        check_vma=False,
    )
```

```python
import functools
import jax
import jax.numpy as jnp
from jax import lax
from jax.experimental import pallas as pl
from jax.experimental.pallas import tpu as pltpu
from jax.sharding import PartitionSpec as P

F32 = jnp.float32
BF16 = jnp.bfloat16
PAD = 16
CHUNKS = 2
WORK = 10**9
LIMIT = 24 * 2**20
VM = pl.BlockSpec(memory_space=pltpu.VMEM)
SM = pl.BlockSpec(memory_space=pltpu.SMEM)
ANY = pl.BlockSpec(memory_space=pl.ANY)


def run(body, name, ins, outs, scratch=(), specs=None, out_specs=None, same=None, after=(), work=1.0):
    count, idle = len(ins), len(ins) + len(after)
    return pl.pallas_call(
        lambda *refs: body(*refs[:count], *refs[idle:]),
        name=name,
        in_specs=(specs or [VM] * count) + [VM] * len(after),
        out_specs=out_specs or tuple(VM for _ in outs),
        out_shape=tuple(outs),
        input_output_aliases=same or {},
        scratch_shapes=list(scratch),
        compiler_params=pltpu.CompilerParams(vmem_limit_bytes=LIMIT),
        cost_estimate=pl.CostEstimate(flops=int(work * WORK), bytes_accessed=2**21, transcendentals=0),
    )(*ins, *after)


def scaled(raw):
    return (raw * (1.0 / jnp.mean(raw, axis=1, keepdims=True))).astype(BF16)


def upward(lam, weight):
    rows = lam.shape[0]
    stacked = jnp.concatenate([lam, jnp.ones((PAD, lam.shape[1]), BF16)], axis=0)
    both = lax.dot_general(stacked, weight, (((1,), (1,)), ((), ())), preferred_element_type=F32)
    return both[:rows], both[rows : rows + 1]


def downward(q_par, raw_msg, lam, weight):
    ratio = (q_par / raw_msg).astype(BF16)
    post = lam.astype(F32) * jnp.dot(ratio, weight, preferred_element_type=F32)
    return ratio, post.astype(BF16)


def one_hot(row, values):
    return (lax.broadcasted_iota(jnp.int32, (values, row.shape[1]), 0) == row).astype(F32).astype(BF16)


def local_slot(parent_ref, node, nodes):
    return jnp.clip(parent_ref[node] - lax.axis_index("leaf") * nodes, 0, node - 1)


def is_upper(level):
    return jnp.bitwise_and(lax.axis_index("leaf"), (2 << level) - 1) == 0


def is_lower(level):
    return jnp.bitwise_and(lax.axis_index("leaf"), (2 << level) - 1) == (1 << level)


def root_base(w_ref, prior_ref, base_ref):
    states = base_ref.shape[1]
    sums = lax.dot_general(jnp.ones((PAD, states), BF16), w_ref[0], (((1,), (1,)), ((), ())), preferred_element_type=F32)
    prior = prior_ref[...]
    odds = (prior / jnp.sum(prior)) / sums[:1]
    high = odds.astype(BF16).astype(F32)
    index = lax.broadcasted_iota(jnp.int32, (PAD, states), 0)
    stacked = jnp.where(index == 0, high, jnp.where(index == 1, odds - high, 0.0)).astype(BF16)
    both = jnp.dot(stacked, w_ref[0], preferred_element_type=F32)
    base_ref[0:1, :] = both[0:1] + both[1:2]
    base_ref[1:2, :] = odds


def prep_body(nodes, parent_hbm, obs_hbm, emission_hbm, mixing_hbm, prior_hbm, *refs):
    w_ref, lam_ref, msg_ref, base_ref = refs[:4]
    u_refs = refs[4 : 4 + CHUNKS]
    prods, tables, obs, parent_ref, prior_ref, sems = refs[4 + CHUNKS :]
    copy_prior = pltpu.make_async_copy(prior_hbm, prior_ref, sems.at[3, 0])
    copy_obs = pltpu.make_async_copy(obs_hbm, obs, sems.at[2, 0])
    copy_parent = pltpu.make_async_copy(parent_hbm, parent_ref, sems.at[2, 1])
    copies_w = [pltpu.make_async_copy(mixing_hbm.at[n], w_ref.at[n], sems.at[0, n]) for n in range(nodes)]
    copies_e = [pltpu.make_async_copy(emission_hbm.at[n], tables.at[n], sems.at[1, n]) for n in range(nodes)]
    copy_obs.start()
    copy_parent.start()
    for n in reversed(range(nodes)):
        copies_e[n].start()
        copies_w[n].start()
    copy_prior.start()
    values = tables.shape[1]
    rows = obs.shape[1]
    part = rows // CHUNKS
    for n in range(nodes - 1):
        prods[n] = jnp.ones(prods.shape[1:], F32)
    copy_obs.wait()
    index = lax.broadcasted_iota(jnp.int32, (PAD, rows), 0)
    listed = jnp.zeros((PAD, rows), jnp.int32)
    for n in range(nodes):
        listed = jnp.where(index == n, obs[n : n + 1, :], listed)
    base = (nodes - 1) * rows
    lam_ref[base : base + PAD, :] = jnp.zeros((PAD, lam_ref.shape[1]), BF16)
    lam_ref[base : base + PAD, :rows] = listed.astype(F32).astype(BF16)
    copy_parent.wait()
    for n in reversed(range(nodes)):
        copies_e[n].wait()
        hot = one_hot(obs[n : n + 1, :], values)
        table = tables[n]
        picked = lax.dot_general(hot, table, (((0,), (0,)), ((), ())), preferred_element_type=F32)
        total = jnp.dot(jnp.ones((PAD, values), BF16), table, preferred_element_type=F32)[:1]
        raw = (picked * (1.0 / total)).astype(BF16).astype(F32)
        if n < nodes - 1:
            raw = raw * prods[n]
        if n > 0:
            lam = scaled(raw)
            copies_w[n].wait()
            raw_msg, sums = upward(lam, w_ref[n])
            lam_ref[(n - 1) * rows : n * rows, :] = lam
            msg_ref[n - 1] = raw_msg
            slot = local_slot(parent_ref, n, nodes)
            prods[slot] = prods[slot] * (raw_msg * (1.0 / sums))
        else:
            for c in range(CHUNKS):
                u_refs[c][...] = raw[c * part : (c + 1) * part]
    copies_w[0].wait()
    copy_prior.wait()

    @pl.when(lax.axis_index("leaf") == 0)
    def _():
        root_base(w_ref, prior_ref, base_ref)


def send_up(level, raw_ref, w_ref, send_ref):
    @pl.when(is_lower(level))
    def _():
        raw_msg, sums = upward(scaled(raw_ref[...]), w_ref[0])
        send_ref[...] = (raw_msg * (1.0 / sums)).astype(BF16)


def first_body(u_ref, w_ref, send_ref):
    send_up(0, u_ref, w_ref, send_ref)


def lift_body(level, u_ref, recv_ref, w_ref, u_out, send_ref):
    @pl.when(is_upper(level))
    def _():
        u_out[...] = u_ref[...] * recv_ref[...].astype(F32)

    send_up(level + 1, u_out, w_ref, send_ref)


def root_body(level, u_ref, recv_ref, base_ref, *refs):
    lam_ref, ratio_ref, post_ref = refs[-4:-1] if len(refs) > 3 else refs
    lam = scaled(u_ref[...] * jnp.where(is_upper(level), recv_ref[...].astype(F32), 1.0))
    lam_ref[...] = lam
    if len(refs) > 3:
        for c, block in enumerate([item[...] for item in refs[:-4]] + [lam]):
            refs[-1][c * lam.shape[0] : (c + 1) * lam.shape[0], :] = block

    @pl.when(lax.axis_index("leaf") == 0)
    def _():
        terms = lam.astype(F32) * base_ref[0:1, :]
        inverse = 1.0 / jnp.sum(terms, axis=1, keepdims=True)
        ratio_ref[...] = (base_ref[1:2, :] * inverse).astype(BF16)
        post_ref[...] = (terms * inverse).astype(BF16)


def top_body(lam_ref, w_ref, msg_ref):
    @pl.when(lax.axis_index("leaf") > 0)
    def _():
        msg_ref[...] = lax.dot_general(lam_ref[...], w_ref[0], (((1,), (1,)), ((), ())), preferred_element_type=F32)


def settle_body(level, recv_ref, lam_ref, msg_ref, w_ref, ratio_in, post_in, ratio_ref, post_ref):
    got = is_lower(level)

    @pl.when(got)
    def _():
        ratio, post = downward(recv_ref[...].astype(F32), msg_ref[...], lam_ref[...], w_ref[0])
        ratio_ref[...] = ratio
        post_ref[...] = post

    @pl.when(jnp.logical_not(got))
    def _():
        ratio_ref[...] = ratio_in[...]
        post_ref[...] = post_in[...]


def last_body(nodes, groups, chunk, parent_ref, recv_ref, lam_ref, msg_ref, w_ref, ratio_in, post_in, lams_ref, msgs_ref, *refs):
    packs, posts = refs[:groups], refs[groups]
    rows, part = msgs_ref.shape[1], lam_ref.shape[0]
    share = lam_ref.shape[1] // groups
    got = is_lower(0)

    @pl.when(got)
    def _():
        ratio, post = downward(recv_ref[...].astype(F32), msg_ref[...], lam_ref[...], w_ref[0])
        posts[nodes] = ratio
        posts[0] = post

    @pl.when(jnp.logical_not(got))
    def _():
        posts[nodes] = ratio_in[...]
        posts[0] = post_in[...]

    for n in range(1, nodes):
        q_par = posts[local_slot(parent_ref, n, nodes)].astype(F32)
        low = (n - 1) * rows + chunk * part
        raw_msg = msgs_ref[n - 1, chunk * part : (chunk + 1) * part, :]
        _, posts[n] = downward(q_par, raw_msg, lams_ref[low : low + part, :], w_ref[n])
    own = lax.axis_index("rows")
    for mask in range(groups):
        start = pl.multiple_of(jnp.bitwise_xor(own, mask) * share, share)
        packs[mask][...] = posts[:, :, pl.ds(start, share)]


def ready_body(nodes, groups, w_ref, *refs):
    lams, (raw_ref, hot_ref) = refs[:groups], refs[groups:]
    chunks, merged, share = raw_ref.shape[1:]
    part = merged // groups
    rows = part * chunks
    values = hot_ref.shape[2]
    base = (nodes - 1) * rows
    start = pl.multiple_of(lax.axis_index("rows") * share, share)
    for n in range(nodes):
        observed = [lam[base : base + PAD, :rows].astype(F32).astype(jnp.int32)[n : n + 1] for lam in lams]
        for c in range(chunks):
            row = jnp.concatenate([item[:, c * part : (c + 1) * part] for item in observed], axis=1)
            hot_ref[n, c] = one_hot(row, values)
        if n > 0:
            weight = w_ref[n, pl.ds(start, share), :]
            for c in range(chunks):
                low = (n - 1) * rows + c * part
                lam = jnp.concatenate([item[low : low + part, :] for item in lams], axis=0)
                raw_ref[n - 1, c] = lax.dot_general(lam, weight, (((1,), (1,)), ((), ())), preferred_element_type=F32)


def counts_body(nodes, groups, chunk, parent_ref, raw_ref, hot_ref, *refs):
    lams, tops, posts = refs[:groups], refs[groups : 2 * groups], refs[2 * groups : 3 * groups]
    refs = refs[3 * groups :]
    chunks = raw_ref.shape[1]
    part = raw_ref.shape[2] // groups
    rows = part * chunks
    before = refs[:2] if chunk > 0 else None
    refs = refs[2:] if chunk > 0 else refs
    final = chunk == chunks - 1
    copies = []
    if final:
        w_ref, homes, refs, sems = refs[0], refs[1:3], refs[3:5], refs[5]
        share = refs[0].shape[1]
        samples = rows * groups
        start = pl.multiple_of(lax.axis_index("rows") * share, share)
    for n in range(nodes):
        low = (n - 1) * rows + chunk * part if n > 0 else chunk * part
        lam = jnp.concatenate([item[low : low + part, :] for item in (lams if n > 0 else tops)], axis=0)
        if n == 0:
            ratio = jnp.concatenate([item[nodes] for item in posts], axis=0)
        else:
            slot = local_slot(parent_ref, n, nodes)
            q_par = jnp.concatenate([item[slot] for item in posts], axis=0)
            ratio = (q_par.astype(F32) / raw_ref[n - 1, chunk]).astype(BF16)
        flow = lax.dot_general(ratio, lam, (((0,), (0,)), ((), ())), preferred_element_type=F32)
        post = jnp.concatenate([item[n] for item in posts], axis=0)
        tally = jnp.dot(hot_ref[n, chunk], post, preferred_element_type=F32)
        if before is not None:
            flow += before[0][n]
            tally += before[1][n]
        if final:
            states, values = flow.shape[1], tally.shape[0]
            weight = w_ref[n, pl.ds(start, share), :].astype(F32)
            flow = weight * flow * (states * states / samples)
            tally = tally * (values * states / samples)
        for k, value in enumerate((flow, tally)):
            refs[k][n] = value.astype(refs[k].dtype)
            if final:
                copies.append(pltpu.make_async_copy(refs[k].at[n], homes[k].at[n], sems.at[k, n]))
                copies[-1].start()
    for copy in copies:
        copy.wait()


def swap(value, mask):
    return lax.ppermute(value, "rows", [(s, s ^ mask) for s in range(lax.axis_size("rows"))])


def hold(value, after):
    shape = pltpu.VMEM(value.shape, value.dtype)
    return run(lambda *refs: None, "hold", (value,), (shape,), same={0: 0}, after=after)[0]


def gather(blocks, after=()):
    for bit in reversed(range(lax.axis_size("rows").bit_length() - 1)):
        if 1 << bit in blocks:
            continue
        for place, block in list(blocks.items()):
            blocks[place | (1 << bit)] = swap(hold(block, after) if place and after else block, 1 << bit)
    return [blocks[place] for place in range(len(blocks))]


def far(value):
    half = lax.axis_size("rows") // 2
    return {0: value, half: swap(value, half)} if half else {0: value}


def per_device(mixing, emission, prior, parent, observed):
    nodes, states = mixing.shape[:2]
    rows = observed.shape[1]
    values = emission.shape[1]
    leaves = lax.axis_size("leaf")
    groups = lax.axis_size("rows")
    levels = leaves.bit_length() - 1
    share = states // groups
    part = rows // CHUNKS
    every = range(CHUNKS)
    half = functools.partial(pltpu.VMEM, (part, states))

    outs = run(
        functools.partial(prep_body, nodes),
        "prep",
        tuple(pltpu.with_memory_space_constraint(x, pltpu.HBM) for x in (parent, observed, emission, mixing, prior.reshape(1, states))),
        (
            pltpu.VMEM(mixing.shape, BF16),
            pltpu.VMEM(((nodes - 1) * rows + PAD, states), BF16),
            pltpu.VMEM((nodes - 1, rows, states), F32),
            pltpu.VMEM((8, states), F32),
        )
        + (half(F32),) * CHUNKS,
        (
            pltpu.VMEM((nodes - 1, rows, states), F32),
            pltpu.VMEM(emission.shape, BF16),
            pltpu.VMEM(observed.shape, jnp.int32),
            pltpu.SMEM(parent.shape, jnp.int32),
            pltpu.VMEM((1, states), F32),
            pltpu.SemaphoreType.DMA((4, max(nodes, 2))),
        ),
        [ANY] * 5,
    )
    weights, lams, msgs, base = outs[:4]
    raw, send = list(outs[4:]), []
    for c in every:
        (block,) = run(first_body, "first", (raw[c], weights), (half(BF16),), after=[lams] if c > 0 else ())
        send.append(block)
        if c == 0:
            lams = hold(lams, (block,))

    def up_pairs(level):
        step = 1 << level
        return [(s, s - step) for s in range(leaves) if s % (2 * step) == step]

    def down_pairs(level):
        return [(b, a) for a, b in up_pairs(level)]

    for level in range(levels - 1):
        for c in every:
            recv = lax.ppermute(send[c], "leaf", up_pairs(level))
            raw[c], send[c] = run(
                functools.partial(lift_body, level),
                "lift",
                (raw[c], recv, weights),
                (half(F32), half(BF16)),
                same={0: 0},
                after=send[:c][-1:],
            )
        if level == 0:
            near = far(lams)
    top_lam, top_msg, ratio, post = ([None] * CHUNKS for _ in range(4))
    for c in every:
        recv = lax.ppermute(send[c], "leaf", up_pairs(levels - 1))
        final = c == CHUNKS - 1
        top_lam[c], ratio[c], post[c], *merged = run(
            functools.partial(root_body, levels - 1),
            "root",
            (raw[c], recv, base) + (tuple(top_lam[:c]) if final else ()),
            (half(BF16), half(BF16), half(BF16)) + ((pltpu.VMEM((rows, states), BF16),) if final else ()),
        )
        (top_msg[c],) = run(top_body, "top", (top_lam[c], weights), (half(F32),), work=1.0)
    all_tops = gather(far(merged[0]))
    all_lams = gather(near, send[-1:])
    raw_own, hots = run(
        functools.partial(ready_body, nodes, groups),
        "ready",
        (weights, *all_lams),
        (
            pltpu.VMEM((nodes - 1, CHUNKS, groups * part, share), F32),
            pltpu.VMEM((nodes, CHUNKS, values, groups * part), BF16),
        ),
        after=(),
        work=1.0,
    )
    for level in reversed(range(1, levels)):
        for c in every:
            recv = lax.ppermute(post[c], "leaf", down_pairs(level))
            ratio[c], post[c] = run(
                functools.partial(settle_body, level),
                "settle",
                (recv, top_lam[c], top_msg[c], weights, ratio[c], post[c]),
                (half(BF16), half(BF16)),
                after=post[:c][-1:] + (all_lams if level == 1 and c == CHUNKS - 1 else []),
            )
    own_posts = []
    for c in every:
        recv = lax.ppermute(post[c], "leaf", down_pairs(0))
        packs = run(
            functools.partial(last_body, nodes, groups, c),
            "last",
            (parent, recv, top_lam[c], top_msg[c], weights, ratio[c], post[c], lams, msgs),
            (pltpu.VMEM((nodes + 1, part, share), BF16),) * groups,
            (pltpu.VMEM((nodes + 1, part, states), BF16),),
            [SM] + [VM] * 8,
            after=[own_posts[-1][0], *all_tops, raw_own] if c > 0 else [],
        )
        order = sorted(range(1, groups), reverse=c < CHUNKS - 1)
        moved = {mask: swap(packs[mask], mask) for mask in order}
        own_posts.append([packs[0]] + [moved[mask] for mask in range(1, groups)])
    sums = ()
    for c in every:
        final = c == CHUNKS - 1
        ins = (parent, raw_own, hots, *all_lams, *all_tops, *own_posts[c], *sums) + ((weights,) if final else ())
        shapes = ((nodes, share, states), (nodes, values, share))
        sums = run(
            functools.partial(counts_body, nodes, groups, c),
            "counts",
            ins,
            tuple(jax.ShapeDtypeStruct(x, BF16) if final else pltpu.VMEM(x, F32) for x in shapes),
            tuple(pltpu.VMEM(x, BF16) for x in shapes) + (pltpu.SemaphoreType.DMA((2, nodes)),) if final else (),
            [SM] + [VM] * (len(ins) - 1),
            (ANY, ANY) if final else None,
        )
    return tuple(sums)


def solution(mesh):
    placed = (P("leaf", None, None), P("leaf", None, None), P(), P("leaf"), P("leaf", "rows"))
    return jax.shard_map(
        per_device,
        mesh=mesh,
        in_specs=placed,
        out_specs=(P("leaf", "rows", None), P("leaf", None, "rows")),
        check_vma=False,
    )
```

```python
import functools
import jax
import jax.numpy as jnp
from jax import lax
from jax.experimental import pallas as pl
from jax.experimental.pallas import tpu as pltpu
from jax.sharding import PartitionSpec as P

F32 = jnp.float32
BF16 = jnp.bfloat16
PAD = 16
CHUNKS = 2
WORK = 8*10**8
LIMIT = 24 * 2**20
VM = pl.BlockSpec(memory_space=pltpu.VMEM)
SM = pl.BlockSpec(memory_space=pltpu.SMEM)
ANY = pl.BlockSpec(memory_space=pl.ANY)


def run(body, name, ins, outs, scratch=(), specs=None, out_specs=None, same=None, after=(), work=1.0):
    count, idle = len(ins), len(ins) + len(after)
    return pl.pallas_call(
        lambda *refs: body(*refs[:count], *refs[idle:]),
        name=name,
        in_specs=(specs or [VM] * count) + [VM] * len(after),
        out_specs=out_specs or tuple(VM for _ in outs),
        out_shape=tuple(outs),
        input_output_aliases=same or {},
        scratch_shapes=list(scratch),
        compiler_params=pltpu.CompilerParams(vmem_limit_bytes=LIMIT),
        cost_estimate=pl.CostEstimate(flops=int(work * WORK), bytes_accessed=2**21, transcendentals=0),
    )(*ins, *after)


def scaled(raw):
    return (raw * (1.0 / jnp.mean(raw, axis=1, keepdims=True))).astype(BF16)


def upward(lam, weight):
    rows = lam.shape[0]
    stacked = jnp.concatenate([lam, jnp.ones((PAD, lam.shape[1]), BF16)], axis=0)
    both = lax.dot_general(stacked, weight, (((1,), (1,)), ((), ())), preferred_element_type=F32)
    return both[:rows], both[rows : rows + 1]


def downward(q_par, raw_msg, lam, weight):
    ratio = (q_par / raw_msg).astype(BF16)
    post = lam.astype(F32) * jnp.dot(ratio, weight, preferred_element_type=F32)
    return ratio, post.astype(BF16)


def one_hot(row, values):
    return (lax.broadcasted_iota(jnp.int32, (values, row.shape[1]), 0) == row).astype(F32).astype(BF16)


def local_slot(parent_ref, node, nodes):
    return jnp.clip(parent_ref[node] - lax.axis_index("leaf") * nodes, 0, node - 1)


def is_upper(level):
    return jnp.bitwise_and(lax.axis_index("leaf"), (2 << level) - 1) == 0


def is_lower(level):
    return jnp.bitwise_and(lax.axis_index("leaf"), (2 << level) - 1) == (1 << level)


def root_base(w_ref, prior_ref, base_ref):
    states = base_ref.shape[1]
    sums = lax.dot_general(jnp.ones((PAD, states), BF16), w_ref[0], (((1,), (1,)), ((), ())), preferred_element_type=F32)
    prior = prior_ref[...]
    odds = (prior / jnp.sum(prior)) / sums[:1]
    high = odds.astype(BF16).astype(F32)
    index = lax.broadcasted_iota(jnp.int32, (PAD, states), 0)
    stacked = jnp.where(index == 0, high, jnp.where(index == 1, odds - high, 0.0)).astype(BF16)
    both = jnp.dot(stacked, w_ref[0], preferred_element_type=F32)
    base_ref[0:1, :] = both[0:1] + both[1:2]
    base_ref[1:2, :] = odds


def prep_body(nodes, parent_hbm, obs_hbm, emission_hbm, mixing_hbm, prior_hbm, *refs):
    w_ref, lam_ref, msg_ref, base_ref = refs[:4]
    u_refs = refs[4 : 4 + CHUNKS]
    prods, tables, obs, parent_ref, prior_ref, sems = refs[4 + CHUNKS :]
    copy_prior = pltpu.make_async_copy(prior_hbm, prior_ref, sems.at[3, 0])
    copy_obs = pltpu.make_async_copy(obs_hbm, obs, sems.at[2, 0])
    copy_parent = pltpu.make_async_copy(parent_hbm, parent_ref, sems.at[2, 1])
    copies_w = [pltpu.make_async_copy(mixing_hbm.at[n], w_ref.at[n], sems.at[0, n]) for n in range(nodes)]
    copies_e = [pltpu.make_async_copy(emission_hbm.at[n], tables.at[n], sems.at[1, n]) for n in range(nodes)]
    copy_obs.start()
    copy_parent.start()
    for n in reversed(range(nodes)):
        copies_e[n].start()
        copies_w[n].start()
    copy_prior.start()
    values = tables.shape[1]
    rows = obs.shape[1]
    part = rows // CHUNKS
    for n in range(nodes - 1):
        prods[n] = jnp.ones(prods.shape[1:], F32)
    copy_obs.wait()
    index = lax.broadcasted_iota(jnp.int32, (PAD, rows), 0)
    listed = jnp.zeros((PAD, rows), jnp.int32)
    for n in range(nodes):
        listed = jnp.where(index == n, obs[n : n + 1, :], listed)
    base = (nodes - 1) * rows
    lam_ref[base : base + PAD, :] = jnp.zeros((PAD, lam_ref.shape[1]), BF16)
    lam_ref[base : base + PAD, :rows] = listed.astype(F32).astype(BF16)
    copy_parent.wait()
    for n in reversed(range(nodes)):
        copies_e[n].wait()
        hot = one_hot(obs[n : n + 1, :], values)
        table = tables[n]
        picked = lax.dot_general(hot, table, (((0,), (0,)), ((), ())), preferred_element_type=F32)
        total = jnp.dot(jnp.ones((PAD, values), BF16), table, preferred_element_type=F32)[:1]
        raw = (picked * (1.0 / total)).astype(BF16).astype(F32)
        if n < nodes - 1:
            raw = raw * prods[n]
        if n > 0:
            lam = scaled(raw)
            copies_w[n].wait()
            raw_msg, sums = upward(lam, w_ref[n])
            lam_ref[(n - 1) * rows : n * rows, :] = lam
            msg_ref[n - 1] = raw_msg
            slot = local_slot(parent_ref, n, nodes)
            prods[slot] = prods[slot] * (raw_msg * (1.0 / sums))
        else:
            for c in range(CHUNKS):
                u_refs[c][...] = raw[c * part : (c + 1) * part]
    copies_w[0].wait()
    copy_prior.wait()

    @pl.when(lax.axis_index("leaf") == 0)
    def _():
        root_base(w_ref, prior_ref, base_ref)


def send_up(level, raw_ref, w_ref, send_ref):
    @pl.when(is_lower(level))
    def _():
        raw_msg, sums = upward(scaled(raw_ref[...]), w_ref[0])
        send_ref[...] = (raw_msg * (1.0 / sums)).astype(BF16)


def first_body(u_ref, w_ref, send_ref):
    send_up(0, u_ref, w_ref, send_ref)


def lift_body(level, u_ref, recv_ref, w_ref, u_out, send_ref):
    @pl.when(is_upper(level))
    def _():
        u_out[...] = u_ref[...] * recv_ref[...].astype(F32)

    send_up(level + 1, u_out, w_ref, send_ref)


def root_body(level, u_ref, recv_ref, base_ref, *refs):
    lam_ref, ratio_ref, post_ref = refs[-4:-1] if len(refs) > 3 else refs
    lam = scaled(u_ref[...] * jnp.where(is_upper(level), recv_ref[...].astype(F32), 1.0))
    lam_ref[...] = lam
    if len(refs) > 3:
        for c, block in enumerate([item[...] for item in refs[:-4]] + [lam]):
            refs[-1][c * lam.shape[0] : (c + 1) * lam.shape[0], :] = block

    @pl.when(lax.axis_index("leaf") == 0)
    def _():
        terms = lam.astype(F32) * base_ref[0:1, :]
        inverse = 1.0 / jnp.sum(terms, axis=1, keepdims=True)
        ratio_ref[...] = (base_ref[1:2, :] * inverse).astype(BF16)
        post_ref[...] = (terms * inverse).astype(BF16)


def top_body(lam_ref, w_ref, msg_ref):
    @pl.when(lax.axis_index("leaf") > 0)
    def _():
        msg_ref[...] = lax.dot_general(lam_ref[...], w_ref[0], (((1,), (1,)), ((), ())), preferred_element_type=F32)


def settle_body(level, recv_ref, lam_ref, msg_ref, w_ref, ratio_in, post_in, ratio_ref, post_ref):
    got = is_lower(level)

    @pl.when(got)
    def _():
        ratio, post = downward(recv_ref[...].astype(F32), msg_ref[...], lam_ref[...], w_ref[0])
        ratio_ref[...] = ratio
        post_ref[...] = post

    @pl.when(jnp.logical_not(got))
    def _():
        ratio_ref[...] = ratio_in[...]
        post_ref[...] = post_in[...]


def last_body(nodes, groups, chunk, parent_ref, recv_ref, lam_ref, msg_ref, w_ref, ratio_in, post_in, lams_ref, msgs_ref, *refs):
    packs, posts = refs[:groups], refs[groups]
    rows, part = msgs_ref.shape[1], lam_ref.shape[0]
    share = lam_ref.shape[1] // groups
    got = is_lower(0)

    @pl.when(got)
    def _():
        ratio, post = downward(recv_ref[...].astype(F32), msg_ref[...], lam_ref[...], w_ref[0])
        posts[nodes] = ratio
        posts[0] = post

    @pl.when(jnp.logical_not(got))
    def _():
        posts[nodes] = ratio_in[...]
        posts[0] = post_in[...]

    for n in range(1, nodes):
        q_par = posts[local_slot(parent_ref, n, nodes)].astype(F32)
        low = (n - 1) * rows + chunk * part
        raw_msg = msgs_ref[n - 1, chunk * part : (chunk + 1) * part, :]
        _, posts[n] = downward(q_par, raw_msg, lams_ref[low : low + part, :], w_ref[n])
    own = lax.axis_index("rows")
    for mask in range(groups):
        start = pl.multiple_of(jnp.bitwise_xor(own, mask) * share, share)
        packs[mask][...] = posts[:, :, pl.ds(start, share)]


def ready_body(nodes, groups, w_ref, *refs):
    lams, (raw_ref, hot_ref) = refs[:groups], refs[groups:]
    chunks, merged, share = raw_ref.shape[1:]
    part = merged // groups
    rows = part * chunks
    values = hot_ref.shape[2]
    base = (nodes - 1) * rows
    start = pl.multiple_of(lax.axis_index("rows") * share, share)
    for n in range(nodes):
        observed = [lam[base : base + PAD, :rows].astype(F32).astype(jnp.int32)[n : n + 1] for lam in lams]
        for c in range(chunks):
            row = jnp.concatenate([item[:, c * part : (c + 1) * part] for item in observed], axis=1)
            hot_ref[n, c] = one_hot(row, values)
        if n > 0:
            weight = w_ref[n, pl.ds(start, share), :]
            for c in range(chunks):
                low = (n - 1) * rows + c * part
                lam = jnp.concatenate([item[low : low + part, :] for item in lams], axis=0)
                raw_ref[n - 1, c] = lax.dot_general(lam, weight, (((1,), (1,)), ((), ())), preferred_element_type=F32)


def counts_body(nodes, groups, chunk, parent_ref, raw_ref, hot_ref, *refs):
    lams, tops, posts = refs[:groups], refs[groups : 2 * groups], refs[2 * groups : 3 * groups]
    refs = refs[3 * groups :]
    chunks = raw_ref.shape[1]
    part = raw_ref.shape[2] // groups
    rows = part * chunks
    before = refs[:2] if chunk > 0 else None
    refs = refs[2:] if chunk > 0 else refs
    final = chunk == chunks - 1
    copies = []
    if final:
        w_ref, homes, refs, sems = refs[0], refs[1:3], refs[3:5], refs[5]
        share = refs[0].shape[1]
        samples = rows * groups
        start = pl.multiple_of(lax.axis_index("rows") * share, share)
    for n in range(nodes):
        low = (n - 1) * rows + chunk * part if n > 0 else chunk * part
        lam = jnp.concatenate([item[low : low + part, :] for item in (lams if n > 0 else tops)], axis=0)
        if n == 0:
            ratio = jnp.concatenate([item[nodes] for item in posts], axis=0)
        else:
            slot = local_slot(parent_ref, n, nodes)
            q_par = jnp.concatenate([item[slot] for item in posts], axis=0)
            ratio = (q_par.astype(F32) / raw_ref[n - 1, chunk]).astype(BF16)
        flow = lax.dot_general(ratio, lam, (((0,), (0,)), ((), ())), preferred_element_type=F32)
        post = jnp.concatenate([item[n] for item in posts], axis=0)
        tally = jnp.dot(hot_ref[n, chunk], post, preferred_element_type=F32)
        if before is not None:
            flow += before[0][n]
            tally += before[1][n]
        if final:
            states, values = flow.shape[1], tally.shape[0]
            weight = w_ref[n, pl.ds(start, share), :].astype(F32)
            flow = weight * flow * (states * states / samples)
            tally = tally * (values * states / samples)
        for k, value in enumerate((flow, tally)):
            refs[k][n] = value.astype(refs[k].dtype)
            if final:
                copies.append(pltpu.make_async_copy(refs[k].at[n], homes[k].at[n], sems.at[k, n]))
                copies[-1].start()
    for copy in copies:
        copy.wait()


def swap(value, mask):
    return lax.ppermute(value, "rows", [(s, s ^ mask) for s in range(lax.axis_size("rows"))])


def hold(value, after):
    shape = pltpu.VMEM(value.shape, value.dtype)
    return run(lambda *refs: None, "hold", (value,), (shape,), same={0: 0}, after=after)[0]


def gather(blocks, after=()):
    for bit in reversed(range(lax.axis_size("rows").bit_length() - 1)):
        if 1 << bit in blocks:
            continue
        for place, block in list(blocks.items()):
            blocks[place | (1 << bit)] = swap(hold(block, after) if place and after else block, 1 << bit)
    return [blocks[place] for place in range(len(blocks))]


def far(value):
    half = lax.axis_size("rows") // 2
    return {0: value, half: swap(value, half)} if half else {0: value}


def per_device(mixing, emission, prior, parent, observed):
    nodes, states = mixing.shape[:2]
    rows = observed.shape[1]
    values = emission.shape[1]
    leaves = lax.axis_size("leaf")
    groups = lax.axis_size("rows")
    levels = leaves.bit_length() - 1
    share = states // groups
    part = rows // CHUNKS
    every = range(CHUNKS)
    half = functools.partial(pltpu.VMEM, (part, states))

    outs = run(
        functools.partial(prep_body, nodes),
        "prep",
        tuple(pltpu.with_memory_space_constraint(x, pltpu.HBM) for x in (parent, observed, emission, mixing, prior.reshape(1, states))),
        (
            pltpu.VMEM(mixing.shape, BF16),
            pltpu.VMEM(((nodes - 1) * rows + PAD, states), BF16),
            pltpu.VMEM((nodes - 1, rows, states), F32),
            pltpu.VMEM((8, states), F32),
        )
        + (half(F32),) * CHUNKS,
        (
            pltpu.VMEM((nodes - 1, rows, states), F32),
            pltpu.VMEM(emission.shape, BF16),
            pltpu.VMEM(observed.shape, jnp.int32),
            pltpu.SMEM(parent.shape, jnp.int32),
            pltpu.VMEM((1, states), F32),
            pltpu.SemaphoreType.DMA((4, max(nodes, 2))),
        ),
        [ANY] * 5,
    )
    weights, lams, msgs, base = outs[:4]
    raw, send = list(outs[4:]), []
    for c in every:
        (block,) = run(first_body, "first", (raw[c], weights), (half(BF16),), after=[lams] if c > 0 else ())
        send.append(block)
        if c == 0:
            lams = hold(lams, (block,))

    def up_pairs(level):
        step = 1 << level
        return [(s, s - step) for s in range(leaves) if s % (2 * step) == step]

    def down_pairs(level):
        return [(b, a) for a, b in up_pairs(level)]

    for level in range(levels - 1):
        for c in every:
            recv = lax.ppermute(send[c], "leaf", up_pairs(level))
            raw[c], send[c] = run(
                functools.partial(lift_body, level),
                "lift",
                (raw[c], recv, weights),
                (half(F32), half(BF16)),
                same={0: 0},
                after=send[:c][-1:],
            )
        if level == 0:
            near = far(lams)
    top_lam, top_msg, ratio, post = ([None] * CHUNKS for _ in range(4))
    for c in every:
        recv = lax.ppermute(send[c], "leaf", up_pairs(levels - 1))
        final = c == CHUNKS - 1
        top_lam[c], ratio[c], post[c], *merged = run(
            functools.partial(root_body, levels - 1),
            "root",
            (raw[c], recv, base) + (tuple(top_lam[:c]) if final else ()),
            (half(BF16), half(BF16), half(BF16)) + ((pltpu.VMEM((rows, states), BF16),) if final else ()),
        )
        (top_msg[c],) = run(top_body, "top", (top_lam[c], weights), (half(F32),), work=2.0)
    all_tops = gather(far(merged[0]))
    all_lams = gather(near, send[-1:])
    for level in reversed(range(1, levels)):
        for c in every:
            recv = lax.ppermute(post[c], "leaf", down_pairs(level))
            ratio[c], post[c] = run(
                functools.partial(settle_body, level),
                "settle",
                (recv, top_lam[c], top_msg[c], weights, ratio[c], post[c]),
                (half(BF16), half(BF16)),
                after=post[:c][-1:] + (all_lams if level == 1 and c == CHUNKS - 1 else []),
            )
    own_posts = []
    for c in every:
        recv = lax.ppermute(post[c], "leaf", down_pairs(0))
        packs = run(
            functools.partial(last_body, nodes, groups, c),
            "last",
            (parent, recv, top_lam[c], top_msg[c], weights, ratio[c], post[c], lams, msgs),
            (pltpu.VMEM((nodes + 1, part, share), BF16),) * groups,
            (pltpu.VMEM((nodes + 1, part, states), BF16),),
            [SM] + [VM] * 8,
            after=[own_posts[-1][0], *all_tops] if c > 0 else [],
        )
        order = sorted(range(1, groups), reverse=c < CHUNKS - 1)
        moved = {mask: swap(packs[mask], mask) for mask in order}
        own_posts.append([packs[0]] + [moved[mask] for mask in range(1, groups)])
    raw_own, hots = run(
        functools.partial(ready_body, nodes, groups),
        "ready",
        (weights, *all_lams),
        (
            pltpu.VMEM((nodes - 1, CHUNKS, groups * part, share), F32),
            pltpu.VMEM((nodes, CHUNKS, values, groups * part), BF16),
        ),
        after=own_posts[0][-1:],
        work=0.1,
    )
    sums = ()
    for c in every:
        final = c == CHUNKS - 1
        ins = (parent, raw_own, hots, *all_lams, *all_tops, *own_posts[c], *sums) + ((weights,) if final else ())
        shapes = ((nodes, share, states), (nodes, values, share))
        sums = run(
            functools.partial(counts_body, nodes, groups, c),
            "counts",
            ins,
            tuple(jax.ShapeDtypeStruct(x, BF16) if final else pltpu.VMEM(x, F32) for x in shapes),
            tuple(pltpu.VMEM(x, BF16) for x in shapes) + (pltpu.SemaphoreType.DMA((2, nodes)),) if final else (),
            [SM] + [VM] * (len(ins) - 1),
            (ANY, ANY) if final else None,
        )
    return tuple(sums)


def solution(mesh):
    placed = (P("leaf", None, None), P("leaf", None, None), P(), P("leaf"), P("leaf", "rows"))
    return jax.shard_map(
        per_device,
        mesh=mesh,
        in_specs=placed,
        out_specs=(P("leaf", "rows", None), P("leaf", None, "rows")),
        check_vma=False,
    )
```

```python
import functools
import jax
import jax.numpy as jnp
from jax import lax
from jax.experimental import pallas as pl
from jax.experimental.pallas import tpu as pltpu
from jax.sharding import PartitionSpec as P

F32 = jnp.float32
BF16 = jnp.bfloat16
PAD = 16
CHUNKS = 2
WORK = 10*10**8
LIMIT = 24 * 2**20
VM = pl.BlockSpec(memory_space=pltpu.VMEM)
SM = pl.BlockSpec(memory_space=pltpu.SMEM)
ANY = pl.BlockSpec(memory_space=pl.ANY)


def run(body, name, ins, outs, scratch=(), specs=None, out_specs=None, same=None, after=(), work=1.0):
    count, idle = len(ins), len(ins) + len(after)
    return pl.pallas_call(
        lambda *refs: body(*refs[:count], *refs[idle:]),
        name=name,
        in_specs=(specs or [VM] * count) + [VM] * len(after),
        out_specs=out_specs or tuple(VM for _ in outs),
        out_shape=tuple(outs),
        input_output_aliases=same or {},
        scratch_shapes=list(scratch),
        compiler_params=pltpu.CompilerParams(vmem_limit_bytes=LIMIT),
        cost_estimate=pl.CostEstimate(flops=int(work * WORK), bytes_accessed=2**21, transcendentals=0),
    )(*ins, *after)


def scaled(raw):
    return (raw * (1.0 / jnp.mean(raw, axis=1, keepdims=True))).astype(BF16)


def upward(lam, weight):
    rows = lam.shape[0]
    stacked = jnp.concatenate([lam, jnp.ones((PAD, lam.shape[1]), BF16)], axis=0)
    both = lax.dot_general(stacked, weight, (((1,), (1,)), ((), ())), preferred_element_type=F32)
    return both[:rows], both[rows : rows + 1]


def downward(q_par, raw_msg, lam, weight):
    ratio = (q_par / raw_msg).astype(BF16)
    post = lam.astype(F32) * jnp.dot(ratio, weight, preferred_element_type=F32)
    return ratio, post.astype(BF16)


def one_hot(row, values):
    return (lax.broadcasted_iota(jnp.int32, (values, row.shape[1]), 0) == row).astype(F32).astype(BF16)


def local_slot(parent_ref, node, nodes):
    return jnp.clip(parent_ref[node] - lax.axis_index("leaf") * nodes, 0, node - 1)


def is_upper(level):
    return jnp.bitwise_and(lax.axis_index("leaf"), (2 << level) - 1) == 0


def is_lower(level):
    return jnp.bitwise_and(lax.axis_index("leaf"), (2 << level) - 1) == (1 << level)


def root_base(w_ref, prior_ref, base_ref):
    states = base_ref.shape[1]
    sums = lax.dot_general(jnp.ones((PAD, states), BF16), w_ref[0], (((1,), (1,)), ((), ())), preferred_element_type=F32)
    prior = prior_ref[...]
    odds = (prior / jnp.sum(prior)) / sums[:1]
    high = odds.astype(BF16).astype(F32)
    index = lax.broadcasted_iota(jnp.int32, (PAD, states), 0)
    stacked = jnp.where(index == 0, high, jnp.where(index == 1, odds - high, 0.0)).astype(BF16)
    both = jnp.dot(stacked, w_ref[0], preferred_element_type=F32)
    base_ref[0:1, :] = both[0:1] + both[1:2]
    base_ref[1:2, :] = odds


def prep_body(nodes, parent_hbm, obs_hbm, emission_hbm, mixing_hbm, prior_hbm, *refs):
    w_ref, lam_ref, msg_ref, base_ref = refs[:4]
    u_refs = refs[4 : 4 + CHUNKS]
    prods, tables, obs, parent_ref, prior_ref, sems = refs[4 + CHUNKS :]
    copy_prior = pltpu.make_async_copy(prior_hbm, prior_ref, sems.at[3, 0])
    copy_obs = pltpu.make_async_copy(obs_hbm, obs, sems.at[2, 0])
    copy_parent = pltpu.make_async_copy(parent_hbm, parent_ref, sems.at[2, 1])
    copies_w = [pltpu.make_async_copy(mixing_hbm.at[n], w_ref.at[n], sems.at[0, n]) for n in range(nodes)]
    copies_e = [pltpu.make_async_copy(emission_hbm.at[n], tables.at[n], sems.at[1, n]) for n in range(nodes)]
    copy_obs.start()
    copy_parent.start()
    for n in reversed(range(nodes)):
        copies_e[n].start()
        copies_w[n].start()
    copy_prior.start()
    values = tables.shape[1]
    rows = obs.shape[1]
    part = rows // CHUNKS
    for n in range(nodes - 1):
        prods[n] = jnp.ones(prods.shape[1:], F32)
    copy_obs.wait()
    index = lax.broadcasted_iota(jnp.int32, (PAD, rows), 0)
    listed = jnp.zeros((PAD, rows), jnp.int32)
    for n in range(nodes):
        listed = jnp.where(index == n, obs[n : n + 1, :], listed)
    base = (nodes - 1) * rows
    lam_ref[base : base + PAD, :] = jnp.zeros((PAD, lam_ref.shape[1]), BF16)
    lam_ref[base : base + PAD, :rows] = listed.astype(F32).astype(BF16)
    copy_parent.wait()
    for n in reversed(range(nodes)):
        copies_e[n].wait()
        hot = one_hot(obs[n : n + 1, :], values)
        table = tables[n]
        picked = lax.dot_general(hot, table, (((0,), (0,)), ((), ())), preferred_element_type=F32)
        total = jnp.dot(jnp.ones((PAD, values), BF16), table, preferred_element_type=F32)[:1]
        raw = (picked * (1.0 / total)).astype(BF16).astype(F32)
        if n < nodes - 1:
            raw = raw * prods[n]
        if n > 0:
            lam = scaled(raw)
            copies_w[n].wait()
            raw_msg, sums = upward(lam, w_ref[n])
            lam_ref[(n - 1) * rows : n * rows, :] = lam
            msg_ref[n - 1] = raw_msg
            slot = local_slot(parent_ref, n, nodes)
            prods[slot] = prods[slot] * (raw_msg * (1.0 / sums))
        else:
            for c in range(CHUNKS):
                u_refs[c][...] = raw[c * part : (c + 1) * part]
    copies_w[0].wait()
    copy_prior.wait()

    @pl.when(lax.axis_index("leaf") == 0)
    def _():
        root_base(w_ref, prior_ref, base_ref)


def send_up(level, raw_ref, w_ref, send_ref):
    @pl.when(is_lower(level))
    def _():
        raw_msg, sums = upward(scaled(raw_ref[...]), w_ref[0])
        send_ref[...] = (raw_msg * (1.0 / sums)).astype(BF16)


def first_body(u_ref, w_ref, send_ref):
    send_up(0, u_ref, w_ref, send_ref)


def lift_body(level, u_ref, recv_ref, w_ref, u_out, send_ref):
    @pl.when(is_upper(level))
    def _():
        u_out[...] = u_ref[...] * recv_ref[...].astype(F32)

    send_up(level + 1, u_out, w_ref, send_ref)


def root_body(level, u_ref, recv_ref, base_ref, *refs):
    lam_ref, ratio_ref, post_ref = refs[-4:-1] if len(refs) > 3 else refs
    lam = scaled(u_ref[...] * jnp.where(is_upper(level), recv_ref[...].astype(F32), 1.0))
    lam_ref[...] = lam
    if len(refs) > 3:
        for c, block in enumerate([item[...] for item in refs[:-4]] + [lam]):
            refs[-1][c * lam.shape[0] : (c + 1) * lam.shape[0], :] = block

    @pl.when(lax.axis_index("leaf") == 0)
    def _():
        terms = lam.astype(F32) * base_ref[0:1, :]
        inverse = 1.0 / jnp.sum(terms, axis=1, keepdims=True)
        ratio_ref[...] = (base_ref[1:2, :] * inverse).astype(BF16)
        post_ref[...] = (terms * inverse).astype(BF16)


def top_body(lam_ref, w_ref, msg_ref):
    @pl.when(lax.axis_index("leaf") > 0)
    def _():
        msg_ref[...] = lax.dot_general(lam_ref[...], w_ref[0], (((1,), (1,)), ((), ())), preferred_element_type=F32)


def settle_body(level, recv_ref, lam_ref, msg_ref, w_ref, ratio_in, post_in, ratio_ref, post_ref):
    got = is_lower(level)

    @pl.when(got)
    def _():
        ratio, post = downward(recv_ref[...].astype(F32), msg_ref[...], lam_ref[...], w_ref[0])
        ratio_ref[...] = ratio
        post_ref[...] = post

    @pl.when(jnp.logical_not(got))
    def _():
        ratio_ref[...] = ratio_in[...]
        post_ref[...] = post_in[...]


def last_body(nodes, groups, chunk, parent_ref, recv_ref, lam_ref, msg_ref, w_ref, ratio_in, post_in, lams_ref, msgs_ref, *refs):
    packs, posts = refs[:groups], refs[groups]
    rows, part = msgs_ref.shape[1], lam_ref.shape[0]
    share = lam_ref.shape[1] // groups
    got = is_lower(0)

    @pl.when(got)
    def _():
        ratio, post = downward(recv_ref[...].astype(F32), msg_ref[...], lam_ref[...], w_ref[0])
        posts[nodes] = ratio
        posts[0] = post

    @pl.when(jnp.logical_not(got))
    def _():
        posts[nodes] = ratio_in[...]
        posts[0] = post_in[...]

    for n in range(1, nodes):
        q_par = posts[local_slot(parent_ref, n, nodes)].astype(F32)
        low = (n - 1) * rows + chunk * part
        raw_msg = msgs_ref[n - 1, chunk * part : (chunk + 1) * part, :]
        _, posts[n] = downward(q_par, raw_msg, lams_ref[low : low + part, :], w_ref[n])
    own = lax.axis_index("rows")
    for mask in range(groups):
        start = pl.multiple_of(jnp.bitwise_xor(own, mask) * share, share)
        packs[mask][...] = posts[:, :, pl.ds(start, share)]


def ready_body(nodes, groups, w_ref, *refs):
    lams, (raw_ref, hot_ref) = refs[:groups], refs[groups:]
    chunks, merged, share = raw_ref.shape[1:]
    part = merged // groups
    rows = part * chunks
    values = hot_ref.shape[2]
    base = (nodes - 1) * rows
    start = pl.multiple_of(lax.axis_index("rows") * share, share)
    for n in range(nodes):
        observed = [lam[base : base + PAD, :rows].astype(F32).astype(jnp.int32)[n : n + 1] for lam in lams]
        for c in range(chunks):
            row = jnp.concatenate([item[:, c * part : (c + 1) * part] for item in observed], axis=1)
            hot_ref[n, c] = one_hot(row, values)
        if n > 0:
            weight = w_ref[n, pl.ds(start, share), :]
            for c in range(chunks):
                low = (n - 1) * rows + c * part
                lam = jnp.concatenate([item[low : low + part, :] for item in lams], axis=0)
                raw_ref[n - 1, c] = lax.dot_general(lam, weight, (((1,), (1,)), ((), ())), preferred_element_type=F32)


def counts_body(nodes, groups, chunk, parent_ref, raw_ref, hot_ref, *refs):
    lams, tops, posts = refs[:groups], refs[groups : 2 * groups], refs[2 * groups : 3 * groups]
    refs = refs[3 * groups :]
    chunks = raw_ref.shape[1]
    part = raw_ref.shape[2] // groups
    rows = part * chunks
    before = refs[:2] if chunk > 0 else None
    refs = refs[2:] if chunk > 0 else refs
    final = chunk == chunks - 1
    copies = []
    if final:
        w_ref, homes, refs, sems = refs[0], refs[1:3], refs[3:5], refs[5]
        share = refs[0].shape[1]
        samples = rows * groups
        start = pl.multiple_of(lax.axis_index("rows") * share, share)
    for n in range(nodes):
        low = (n - 1) * rows + chunk * part if n > 0 else chunk * part
        lam = jnp.concatenate([item[low : low + part, :] for item in (lams if n > 0 else tops)], axis=0)
        if n == 0:
            ratio = jnp.concatenate([item[nodes] for item in posts], axis=0)
        else:
            slot = local_slot(parent_ref, n, nodes)
            q_par = jnp.concatenate([item[slot] for item in posts], axis=0)
            ratio = (q_par.astype(F32) / raw_ref[n - 1, chunk]).astype(BF16)
        flow = lax.dot_general(ratio, lam, (((0,), (0,)), ((), ())), preferred_element_type=F32)
        post = jnp.concatenate([item[n] for item in posts], axis=0)
        tally = jnp.dot(hot_ref[n, chunk], post, preferred_element_type=F32)
        if before is not None:
            flow += before[0][n]
            tally += before[1][n]
        if final:
            states, values = flow.shape[1], tally.shape[0]
            weight = w_ref[n, pl.ds(start, share), :].astype(F32)
            flow = weight * flow * (states * states / samples)
            tally = tally * (values * states / samples)
        for k, value in enumerate((flow, tally)):
            refs[k][n] = value.astype(refs[k].dtype)
            if final:
                copies.append(pltpu.make_async_copy(refs[k].at[n], homes[k].at[n], sems.at[k, n]))
                copies[-1].start()
    for copy in copies:
        copy.wait()


def swap(value, mask):
    return lax.ppermute(value, "rows", [(s, s ^ mask) for s in range(lax.axis_size("rows"))])


def hold(value, after):
    shape = pltpu.VMEM(value.shape, value.dtype)
    return run(lambda *refs: None, "hold", (value,), (shape,), same={0: 0}, after=after)[0]


def gather(blocks, after=()):
    for bit in reversed(range(lax.axis_size("rows").bit_length() - 1)):
        if 1 << bit in blocks:
            continue
        for place, block in list(blocks.items()):
            blocks[place | (1 << bit)] = swap(hold(block, after) if place and after else block, 1 << bit)
    return [blocks[place] for place in range(len(blocks))]


def far(value):
    half = lax.axis_size("rows") // 2
    return {0: value, half: swap(value, half)} if half else {0: value}


def per_device(mixing, emission, prior, parent, observed):
    nodes, states = mixing.shape[:2]
    rows = observed.shape[1]
    values = emission.shape[1]
    leaves = lax.axis_size("leaf")
    groups = lax.axis_size("rows")
    levels = leaves.bit_length() - 1
    share = states // groups
    part = rows // CHUNKS
    every = range(CHUNKS)
    half = functools.partial(pltpu.VMEM, (part, states))

    outs = run(
        functools.partial(prep_body, nodes),
        "prep",
        tuple(pltpu.with_memory_space_constraint(x, pltpu.HBM) for x in (parent, observed, emission, mixing, prior.reshape(1, states))),
        (
            pltpu.VMEM(mixing.shape, BF16),
            pltpu.VMEM(((nodes - 1) * rows + PAD, states), BF16),
            pltpu.VMEM((nodes - 1, rows, states), F32),
            pltpu.VMEM((8, states), F32),
        )
        + (half(F32),) * CHUNKS,
        (
            pltpu.VMEM((nodes - 1, rows, states), F32),
            pltpu.VMEM(emission.shape, BF16),
            pltpu.VMEM(observed.shape, jnp.int32),
            pltpu.SMEM(parent.shape, jnp.int32),
            pltpu.VMEM((1, states), F32),
            pltpu.SemaphoreType.DMA((4, max(nodes, 2))),
        ),
        [ANY] * 5,
    )
    weights, lams, msgs, base = outs[:4]
    raw, send = list(outs[4:]), []
    for c in every:
        (block,) = run(first_body, "first", (raw[c], weights), (half(BF16),), after=[lams] if c > 0 else ())
        send.append(block)
        if c == 0:
            lams = hold(lams, (block,))

    def up_pairs(level):
        step = 1 << level
        return [(s, s - step) for s in range(leaves) if s % (2 * step) == step]

    def down_pairs(level):
        return [(b, a) for a, b in up_pairs(level)]

    for level in range(levels - 1):
        for c in every:
            recv = lax.ppermute(send[c], "leaf", up_pairs(level))
            raw[c], send[c] = run(
                functools.partial(lift_body, level),
                "lift",
                (raw[c], recv, weights),
                (half(F32), half(BF16)),
                same={0: 0},
                after=send[:c][-1:],
            )
        if level == 0:
            near = far(lams)
    top_lam, top_msg, ratio, post = ([None] * CHUNKS for _ in range(4))
    for c in every:
        recv = lax.ppermute(send[c], "leaf", up_pairs(levels - 1))
        final = c == CHUNKS - 1
        top_lam[c], ratio[c], post[c], *merged = run(
            functools.partial(root_body, levels - 1),
            "root",
            (raw[c], recv, base) + (tuple(top_lam[:c]) if final else ()),
            (half(BF16), half(BF16), half(BF16)) + ((pltpu.VMEM((rows, states), BF16),) if final else ()),
        )
        (top_msg[c],) = run(top_body, "top", (top_lam[c], weights), (half(F32),), work=1.0)
    all_tops = gather(far(merged[0]))
    all_lams = gather(near, send[-1:])
    raw_own, hots = run(
        functools.partial(ready_body, nodes, groups),
        "ready",
        (weights, *all_lams),
        (
            pltpu.VMEM((nodes - 1, CHUNKS, groups * part, share), F32),
            pltpu.VMEM((nodes, CHUNKS, values, groups * part), BF16),
        ),
        after=(),
        work=0.1,
    )
    for level in reversed(range(1, levels)):
        for c in every:
            recv = lax.ppermute(post[c], "leaf", down_pairs(level))
            ratio[c], post[c] = run(
                functools.partial(settle_body, level),
                "settle",
                (recv, top_lam[c], top_msg[c], weights, ratio[c], post[c]),
                (half(BF16), half(BF16)),
                after=post[:c][-1:] + ([raw_own] if level == 1 and c == CHUNKS - 1 else []),
            )
    own_posts = []
    for c in every:
        recv = lax.ppermute(post[c], "leaf", down_pairs(0))
        packs = run(
            functools.partial(last_body, nodes, groups, c),
            "last",
            (parent, recv, top_lam[c], top_msg[c], weights, ratio[c], post[c], lams, msgs),
            (pltpu.VMEM((nodes + 1, part, share), BF16),) * groups,
            (pltpu.VMEM((nodes + 1, part, states), BF16),),
            [SM] + [VM] * 8,
            after=[own_posts[-1][0], *all_tops] if c > 0 else [],
        )
        order = sorted(range(1, groups), reverse=c < CHUNKS - 1)
        moved = {mask: swap(packs[mask], mask) for mask in order}
        own_posts.append([packs[0]] + [moved[mask] for mask in range(1, groups)])
    sums = ()
    for c in every:
        final = c == CHUNKS - 1
        ins = (parent, raw_own, hots, *all_lams, *all_tops, *own_posts[c], *sums) + ((weights,) if final else ())
        shapes = ((nodes, share, states), (nodes, values, share))
        sums = run(
            functools.partial(counts_body, nodes, groups, c),
            "counts",
            ins,
            tuple(jax.ShapeDtypeStruct(x, BF16) if final else pltpu.VMEM(x, F32) for x in shapes),
            tuple(pltpu.VMEM(x, BF16) for x in shapes) + (pltpu.SemaphoreType.DMA((2, nodes)),) if final else (),
            [SM] + [VM] * (len(ins) - 1),
            (ANY, ANY) if final else None,
        )
    return tuple(sums)


def solution(mesh):
    placed = (P("leaf", None, None), P("leaf", None, None), P(), P("leaf"), P("leaf", "rows"))
    return jax.shard_map(
        per_device,
        mesh=mesh,
        in_specs=placed,
        out_specs=(P("leaf", "rows", None), P("leaf", None, "rows")),
        check_vma=False,
    )
```

```python
import functools
import jax
import jax.numpy as jnp
from jax import lax
from jax.experimental import pallas as pl
from jax.experimental.pallas import tpu as pltpu
from jax.sharding import PartitionSpec as P

F32 = jnp.float32
BF16 = jnp.bfloat16
PAD = 16
CHUNKS = 2
WORK = 10**9
LIMIT = 24 * 2**20
VM = pl.BlockSpec(memory_space=pltpu.VMEM)
SM = pl.BlockSpec(memory_space=pltpu.SMEM)
ANY = pl.BlockSpec(memory_space=pl.ANY)


def run(body, name, ins, outs, scratch=(), specs=None, out_specs=None, same=None, after=(), work=1.0):
    count, idle = len(ins), len(ins) + len(after)
    return pl.pallas_call(
        lambda *refs: body(*refs[:count], *refs[idle:]),
        name=name,
        in_specs=(specs or [VM] * count) + [VM] * len(after),
        out_specs=out_specs or tuple(VM for _ in outs),
        out_shape=tuple(outs),
        input_output_aliases=same or {},
        scratch_shapes=list(scratch),
        compiler_params=pltpu.CompilerParams(vmem_limit_bytes=LIMIT),
        cost_estimate=pl.CostEstimate(flops=int(work * WORK), bytes_accessed=2**21, transcendentals=0),
    )(*ins, *after)


def scaled(raw):
    return (raw * (1.0 / jnp.mean(raw, axis=1, keepdims=True))).astype(BF16)


def upward(lam, weight):
    rows = lam.shape[0]
    stacked = jnp.concatenate([lam, jnp.ones((PAD, lam.shape[1]), BF16)], axis=0)
    both = lax.dot_general(stacked, weight, (((1,), (1,)), ((), ())), preferred_element_type=F32)
    return both[:rows], both[rows : rows + 1]


def downward(q_par, raw_msg, lam, weight):
    ratio = (q_par / raw_msg).astype(BF16)
    post = lam.astype(F32) * jnp.dot(ratio, weight, preferred_element_type=F32)
    return ratio, post.astype(BF16)


def one_hot(row, values):
    return (lax.broadcasted_iota(jnp.int32, (values, row.shape[1]), 0) == row).astype(F32).astype(BF16)


def local_slot(parent_ref, node, nodes):
    return jnp.clip(parent_ref[node] - lax.axis_index("leaf") * nodes, 0, node - 1)


def is_upper(level):
    return jnp.bitwise_and(lax.axis_index("leaf"), (2 << level) - 1) == 0


def is_lower(level):
    return jnp.bitwise_and(lax.axis_index("leaf"), (2 << level) - 1) == (1 << level)


def root_base(w_ref, prior_ref, base_ref):
    states = base_ref.shape[1]
    sums = lax.dot_general(jnp.ones((PAD, states), BF16), w_ref[0], (((1,), (1,)), ((), ())), preferred_element_type=F32)
    prior = prior_ref[...]
    odds = (prior / jnp.sum(prior)) / sums[:1]
    high = odds.astype(BF16).astype(F32)
    index = lax.broadcasted_iota(jnp.int32, (PAD, states), 0)
    stacked = jnp.where(index == 0, high, jnp.where(index == 1, odds - high, 0.0)).astype(BF16)
    both = jnp.dot(stacked, w_ref[0], preferred_element_type=F32)
    base_ref[0:1, :] = both[0:1] + both[1:2]
    base_ref[1:2, :] = odds


def prep_body(nodes, parent_hbm, obs_hbm, emission_hbm, mixing_hbm, prior_hbm, *refs):
    w_ref, lam_ref, msg_ref, base_ref = refs[:4]
    u_refs = refs[4 : 4 + CHUNKS]
    prods, tables, obs, parent_ref, prior_ref, sems = refs[4 + CHUNKS :]
    copy_prior = pltpu.make_async_copy(prior_hbm, prior_ref, sems.at[3, 0])
    copy_obs = pltpu.make_async_copy(obs_hbm, obs, sems.at[2, 0])
    copy_parent = pltpu.make_async_copy(parent_hbm, parent_ref, sems.at[2, 1])
    copies_w = [pltpu.make_async_copy(mixing_hbm.at[n], w_ref.at[n], sems.at[0, n]) for n in range(nodes)]
    copies_e = [pltpu.make_async_copy(emission_hbm.at[n], tables.at[n], sems.at[1, n]) for n in range(nodes)]
    copy_obs.start()
    copy_parent.start()
    for n in reversed(range(nodes)):
        copies_e[n].start()
        copies_w[n].start()
    copy_prior.start()
    values = tables.shape[1]
    rows = obs.shape[1]
    part = rows // CHUNKS
    for n in range(nodes - 1):
        prods[n] = jnp.ones(prods.shape[1:], F32)
    copy_obs.wait()
    index = lax.broadcasted_iota(jnp.int32, (PAD, rows), 0)
    listed = jnp.zeros((PAD, rows), jnp.int32)
    for n in range(nodes):
        listed = jnp.where(index == n, obs[n : n + 1, :], listed)
    base = (nodes - 1) * rows
    lam_ref[base : base + PAD, :] = jnp.zeros((PAD, lam_ref.shape[1]), BF16)
    lam_ref[base : base + PAD, :rows] = listed.astype(F32).astype(BF16)
    copy_parent.wait()
    for n in reversed(range(nodes)):
        copies_e[n].wait()
        hot = one_hot(obs[n : n + 1, :], values)
        table = tables[n]
        picked = lax.dot_general(hot, table, (((0,), (0,)), ((), ())), preferred_element_type=F32)
        total = jnp.dot(jnp.ones((PAD, values), BF16), table, preferred_element_type=F32)[:1]
        raw = (picked * (1.0 / total)).astype(BF16).astype(F32)
        if n < nodes - 1:
            raw = raw * prods[n]
        if n > 0:
            lam = scaled(raw)
            copies_w[n].wait()
            raw_msg, sums = upward(lam, w_ref[n])
            lam_ref[(n - 1) * rows : n * rows, :] = lam
            msg_ref[n - 1] = raw_msg
            slot = local_slot(parent_ref, n, nodes)
            prods[slot] = prods[slot] * (raw_msg * (1.0 / sums))
        else:
            for c in range(CHUNKS):
                u_refs[c][...] = raw[c * part : (c + 1) * part]
    copies_w[0].wait()
    copy_prior.wait()

    @pl.when(lax.axis_index("leaf") == 0)
    def _():
        root_base(w_ref, prior_ref, base_ref)


def send_up(level, raw_ref, w_ref, send_ref):
    @pl.when(is_lower(level))
    def _():
        raw_msg, sums = upward(scaled(raw_ref[...]), w_ref[0])
        send_ref[...] = (raw_msg * (1.0 / sums)).astype(BF16)


def first_body(u_ref, w_ref, send_ref):
    send_up(0, u_ref, w_ref, send_ref)


def lift_body(level, u_ref, recv_ref, w_ref, u_out, send_ref):
    @pl.when(is_upper(level))
    def _():
        u_out[...] = u_ref[...] * recv_ref[...].astype(F32)

    send_up(level + 1, u_out, w_ref, send_ref)


def root_body(level, u_ref, recv_ref, base_ref, *refs):
    lam_ref, ratio_ref, post_ref = refs[-4:-1] if len(refs) > 3 else refs
    lam = scaled(u_ref[...] * jnp.where(is_upper(level), recv_ref[...].astype(F32), 1.0))
    lam_ref[...] = lam
    if len(refs) > 3:
        for c, block in enumerate([item[...] for item in refs[:-4]] + [lam]):
            refs[-1][c * lam.shape[0] : (c + 1) * lam.shape[0], :] = block

    @pl.when(lax.axis_index("leaf") == 0)
    def _():
        terms = lam.astype(F32) * base_ref[0:1, :]
        inverse = 1.0 / jnp.sum(terms, axis=1, keepdims=True)
        ratio_ref[...] = (base_ref[1:2, :] * inverse).astype(BF16)
        post_ref[...] = (terms * inverse).astype(BF16)


def top_body(lam_ref, w_ref, msg_ref):
    @pl.when(lax.axis_index("leaf") > 0)
    def _():
        msg_ref[...] = lax.dot_general(lam_ref[...], w_ref[0], (((1,), (1,)), ((), ())), preferred_element_type=F32)


def settle_body(level, recv_ref, lam_ref, msg_ref, w_ref, ratio_in, post_in, ratio_ref, post_ref):
    got = is_lower(level)

    @pl.when(got)
    def _():
        ratio, post = downward(recv_ref[...].astype(F32), msg_ref[...], lam_ref[...], w_ref[0])
        ratio_ref[...] = ratio
        post_ref[...] = post

    @pl.when(jnp.logical_not(got))
    def _():
        ratio_ref[...] = ratio_in[...]
        post_ref[...] = post_in[...]


def last_body(nodes, groups, chunk, parent_ref, recv_ref, lam_ref, msg_ref, w_ref, ratio_in, post_in, lams_ref, msgs_ref, *refs):
    packs, posts = refs[:groups], refs[groups]
    rows, part = msgs_ref.shape[1], lam_ref.shape[0]
    share = lam_ref.shape[1] // groups
    got = is_lower(0)

    @pl.when(got)
    def _():
        ratio, post = downward(recv_ref[...].astype(F32), msg_ref[...], lam_ref[...], w_ref[0])
        posts[nodes] = ratio
        posts[0] = post

    @pl.when(jnp.logical_not(got))
    def _():
        posts[nodes] = ratio_in[...]
        posts[0] = post_in[...]

    for n in range(1, nodes):
        q_par = posts[local_slot(parent_ref, n, nodes)].astype(F32)
        low = (n - 1) * rows + chunk * part
        raw_msg = msgs_ref[n - 1, chunk * part : (chunk + 1) * part, :]
        _, posts[n] = downward(q_par, raw_msg, lams_ref[low : low + part, :], w_ref[n])
    own = lax.axis_index("rows")
    for mask in range(groups):
        start = pl.multiple_of(jnp.bitwise_xor(own, mask) * share, share)
        packs[mask][...] = posts[:, :, pl.ds(start, share)]


def ready_body(nodes, groups, w_ref, *refs):
    lams, (raw_ref, hot_ref) = refs[:groups], refs[groups:]
    chunks, merged, share = raw_ref.shape[1:]
    part = merged // groups
    rows = part * chunks
    values = hot_ref.shape[2]
    base = (nodes - 1) * rows
    start = pl.multiple_of(lax.axis_index("rows") * share, share)
    for n in range(nodes):
        observed = [lam[base : base + PAD, :rows].astype(F32).astype(jnp.int32)[n : n + 1] for lam in lams]
        for c in range(chunks):
            row = jnp.concatenate([item[:, c * part : (c + 1) * part] for item in observed], axis=1)
            hot_ref[n, c] = one_hot(row, values)
        if n > 0:
            weight = w_ref[n, pl.ds(start, share), :]
            for c in range(chunks):
                low = (n - 1) * rows + c * part
                lam = jnp.concatenate([item[low : low + part, :] for item in lams], axis=0)
                raw_ref[n - 1, c] = lax.dot_general(lam, weight, (((1,), (1,)), ((), ())), preferred_element_type=F32)


def counts_body(nodes, groups, chunk, parent_ref, raw_ref, hot_ref, *refs):
    lams, tops, posts = refs[:groups], refs[groups : 2 * groups], refs[2 * groups : 3 * groups]
    refs = refs[3 * groups :]
    chunks = raw_ref.shape[1]
    part = raw_ref.shape[2] // groups
    rows = part * chunks
    before = refs[:2] if chunk > 0 else None
    refs = refs[2:] if chunk > 0 else refs
    final = chunk == chunks - 1
    copies = []
    if final:
        w_ref, homes, refs, sems = refs[0], refs[1:3], refs[3:5], refs[5]
        share = refs[0].shape[1]
        samples = rows * groups
        start = pl.multiple_of(lax.axis_index("rows") * share, share)
    for n in range(nodes):
        low = (n - 1) * rows + chunk * part if n > 0 else chunk * part
        lam = jnp.concatenate([item[low : low + part, :] for item in (lams if n > 0 else tops)], axis=0)
        if n == 0:
            ratio = jnp.concatenate([item[nodes] for item in posts], axis=0)
        else:
            slot = local_slot(parent_ref, n, nodes)
            q_par = jnp.concatenate([item[slot] for item in posts], axis=0)
            ratio = (q_par.astype(F32) / raw_ref[n - 1, chunk]).astype(BF16)
        flow = lax.dot_general(ratio, lam, (((0,), (0,)), ((), ())), preferred_element_type=F32)
        post = jnp.concatenate([item[n] for item in posts], axis=0)
        tally = jnp.dot(hot_ref[n, chunk], post, preferred_element_type=F32)
        if before is not None:
            flow += before[0][n]
            tally += before[1][n]
        if final:
            states, values = flow.shape[1], tally.shape[0]
            weight = w_ref[n, pl.ds(start, share), :].astype(F32)
            flow = weight * flow * (states * states / samples)
            tally = tally * (values * states / samples)
        for k, value in enumerate((flow, tally)):
            refs[k][n] = value.astype(refs[k].dtype)
            if final:
                copies.append(pltpu.make_async_copy(refs[k].at[n], homes[k].at[n], sems.at[k, n]))
                copies[-1].start()
    for copy in copies:
        copy.wait()


def swap(value, mask):
    return lax.ppermute(value, "rows", [(s, s ^ mask) for s in range(lax.axis_size("rows"))])


def hold(value, after):
    shape = pltpu.VMEM(value.shape, value.dtype)
    return run(lambda *refs: None, "hold", (value,), (shape,), same={0: 0}, after=after)[0]


def gather(blocks, after=()):
    for bit in reversed(range(lax.axis_size("rows").bit_length() - 1)):
        if 1 << bit in blocks:
            continue
        for place, block in list(blocks.items()):
            blocks[place | (1 << bit)] = swap(hold(block, after) if place and after else block, 1 << bit)
    return [blocks[place] for place in range(len(blocks))]


def far(value):
    half = lax.axis_size("rows") // 2
    return {0: value, half: swap(value, half)} if half else {0: value}


def per_device(mixing, emission, prior, parent, observed):
    nodes, states = mixing.shape[:2]
    rows = observed.shape[1]
    values = emission.shape[1]
    leaves = lax.axis_size("leaf")
    groups = lax.axis_size("rows")
    levels = leaves.bit_length() - 1
    share = states // groups
    part = rows // CHUNKS
    every = range(CHUNKS)
    half = functools.partial(pltpu.VMEM, (part, states))

    outs = run(
        functools.partial(prep_body, nodes),
        "prep",
        tuple(pltpu.with_memory_space_constraint(x, pltpu.HBM) for x in (parent, observed, emission, mixing, prior.reshape(1, states))),
        (
            pltpu.VMEM(mixing.shape, BF16),
            pltpu.VMEM(((nodes - 1) * rows + PAD, states), BF16),
            pltpu.VMEM((nodes - 1, rows, states), F32),
            pltpu.VMEM((8, states), F32),
        )
        + (half(F32),) * CHUNKS,
        (
            pltpu.VMEM((nodes - 1, rows, states), F32),
            pltpu.VMEM(emission.shape, BF16),
            pltpu.VMEM(observed.shape, jnp.int32),
            pltpu.SMEM(parent.shape, jnp.int32),
            pltpu.VMEM((1, states), F32),
            pltpu.SemaphoreType.DMA((4, max(nodes, 2))),
        ),
        [ANY] * 5,
    )
    weights, lams, msgs, base = outs[:4]
    raw, send = list(outs[4:]), []
    for c in every:
        (block,) = run(first_body, "first", (raw[c], weights), (half(BF16),), after=[lams] if c > 0 else ())
        send.append(block)
        if c == 0:
            lams = hold(lams, (block,))

    def up_pairs(level):
        step = 1 << level
        return [(s, s - step) for s in range(leaves) if s % (2 * step) == step]

    def down_pairs(level):
        return [(b, a) for a, b in up_pairs(level)]

    for level in range(levels - 1):
        for c in every:
            recv = lax.ppermute(send[c], "leaf", up_pairs(level))
            raw[c], send[c] = run(
                functools.partial(lift_body, level),
                "lift",
                (raw[c], recv, weights),
                (half(F32), half(BF16)),
                same={0: 0},
                after=send[:c][-1:],
            )
        if level == 0:
            near = far(lams)
    top_lam, top_msg, ratio, post = ([None] * CHUNKS for _ in range(4))
    for c in every:
        recv = lax.ppermute(send[c], "leaf", up_pairs(levels - 1))
        final = c == CHUNKS - 1
        top_lam[c], ratio[c], post[c], *merged = run(
            functools.partial(root_body, levels - 1),
            "root",
            (raw[c], recv, base) + (tuple(top_lam[:c]) if final else ()),
            (half(BF16), half(BF16), half(BF16)) + ((pltpu.VMEM((rows, states), BF16),) if final else ()),
        )
        (top_msg[c],) = run(top_body, "top", (top_lam[c], weights), (half(F32),), work=1.0)
    all_tops = gather(far(merged[0]))
    all_lams = gather(near, send[-1:])
    raw_own, hots = run(
        functools.partial(ready_body, nodes, groups),
        "ready",
        (weights, *all_lams),
        (
            pltpu.VMEM((nodes - 1, CHUNKS, groups * part, share), F32),
            pltpu.VMEM((nodes, CHUNKS, values, groups * part), BF16),
        ),
        after=(),
        work=1.0,
    )
    for level in reversed(range(1, levels)):
        for c in every:
            recv = lax.ppermute(post[c], "leaf", down_pairs(level))
            ratio[c], post[c] = run(
                functools.partial(settle_body, level),
                "settle",
                (recv, top_lam[c], top_msg[c], weights, ratio[c], post[c]),
                (half(BF16), half(BF16)),
                after=post[:c][-1:] + (all_lams if level == 1 and c == CHUNKS - 1 else []),
            )
    own_posts = []
    for c in every:
        recv = lax.ppermute(post[c], "leaf", down_pairs(0))
        packs = run(
            functools.partial(last_body, nodes, groups, c),
            "last",
            (parent, recv, top_lam[c], top_msg[c], weights, ratio[c], post[c], lams, msgs),
            (pltpu.VMEM((nodes + 1, part, share), BF16),) * groups,
            (pltpu.VMEM((nodes + 1, part, states), BF16),),
            [SM] + [VM] * 8,
            after=[own_posts[-1][0], *all_tops, raw_own] if c > 0 else [],
        )
        order = sorted(range(1, groups), reverse=True)
        moved = {mask: swap(packs[mask], mask) for mask in order}
        own_posts.append([packs[0]] + [moved[mask] for mask in range(1, groups)])
    sums = ()
    for c in every:
        final = c == CHUNKS - 1
        ins = (parent, raw_own, hots, *all_lams, *all_tops, *own_posts[c], *sums) + ((weights,) if final else ())
        shapes = ((nodes, share, states), (nodes, values, share))
        sums = run(
            functools.partial(counts_body, nodes, groups, c),
            "counts",
            ins,
            tuple(jax.ShapeDtypeStruct(x, BF16) if final else pltpu.VMEM(x, F32) for x in shapes),
            tuple(pltpu.VMEM(x, BF16) for x in shapes) + (pltpu.SemaphoreType.DMA((2, nodes)),) if final else (),
            [SM] + [VM] * (len(ins) - 1),
            (ANY, ANY) if final else None,
        )
    return tuple(sums)


def solution(mesh):
    placed = (P("leaf", None, None), P("leaf", None, None), P(), P("leaf"), P("leaf", "rows"))
    return jax.shard_map(
        per_device,
        mesh=mesh,
        in_specs=placed,
        out_specs=(P("leaf", "rows", None), P("leaf", None, "rows")),
        check_vma=False,
    )
```

```python
import functools
import jax
import jax.numpy as jnp
from jax import lax
from jax.experimental import pallas as pl
from jax.experimental.pallas import tpu as pltpu
from jax.sharding import PartitionSpec as P

F32 = jnp.float32
BF16 = jnp.bfloat16
PAD = 16
CHUNKS = 2
WORK = 10**9
LIMIT = 24 * 2**20
VM = pl.BlockSpec(memory_space=pltpu.VMEM)
SM = pl.BlockSpec(memory_space=pltpu.SMEM)
ANY = pl.BlockSpec(memory_space=pl.ANY)


def run(body, name, ins, outs, scratch=(), specs=None, out_specs=None, same=None, after=(), work=1.0):
    count, idle = len(ins), len(ins) + len(after)
    return pl.pallas_call(
        lambda *refs: body(*refs[:count], *refs[idle:]),
        name=name,
        in_specs=(specs or [VM] * count) + [VM] * len(after),
        out_specs=out_specs or tuple(VM for _ in outs),
        out_shape=tuple(outs),
        input_output_aliases=same or {},
        scratch_shapes=list(scratch),
        compiler_params=pltpu.CompilerParams(vmem_limit_bytes=LIMIT),
        cost_estimate=pl.CostEstimate(flops=int(work * WORK), bytes_accessed=2**21, transcendentals=0),
    )(*ins, *after)


def scaled(raw):
    return (raw * (1.0 / jnp.mean(raw, axis=1, keepdims=True))).astype(BF16)


def upward(lam, weight):
    rows = lam.shape[0]
    stacked = jnp.concatenate([lam, jnp.ones((PAD, lam.shape[1]), BF16)], axis=0)
    both = lax.dot_general(stacked, weight, (((1,), (1,)), ((), ())), preferred_element_type=F32)
    return both[:rows], both[rows : rows + 1]


def downward(q_par, raw_msg, lam, weight):
    ratio = (q_par / raw_msg).astype(BF16)
    post = lam.astype(F32) * jnp.dot(ratio, weight, preferred_element_type=F32)
    return ratio, post.astype(BF16)


def one_hot(row, values):
    return (lax.broadcasted_iota(jnp.int32, (values, row.shape[1]), 0) == row).astype(F32).astype(BF16)


def local_slot(parent_ref, node, nodes):
    return jnp.clip(parent_ref[node] - lax.axis_index("leaf") * nodes, 0, node - 1)


def is_upper(level):
    return jnp.bitwise_and(lax.axis_index("leaf"), (2 << level) - 1) == 0


def is_lower(level):
    return jnp.bitwise_and(lax.axis_index("leaf"), (2 << level) - 1) == (1 << level)


def root_base(w_ref, prior_ref, base_ref):
    states = base_ref.shape[1]
    sums = lax.dot_general(jnp.ones((PAD, states), BF16), w_ref[0], (((1,), (1,)), ((), ())), preferred_element_type=F32)
    prior = prior_ref[...]
    odds = (prior / jnp.sum(prior)) / sums[:1]
    high = odds.astype(BF16).astype(F32)
    index = lax.broadcasted_iota(jnp.int32, (PAD, states), 0)
    stacked = jnp.where(index == 0, high, jnp.where(index == 1, odds - high, 0.0)).astype(BF16)
    both = jnp.dot(stacked, w_ref[0], preferred_element_type=F32)
    base_ref[0:1, :] = both[0:1] + both[1:2]
    base_ref[1:2, :] = odds


def prep_body(nodes, parent_hbm, obs_hbm, emission_hbm, mixing_hbm, prior_hbm, *refs):
    w_ref, lam_ref, msg_ref, base_ref = refs[:4]
    u_refs = refs[4 : 4 + CHUNKS]
    prods, tables, obs, parent_ref, prior_ref, sems = refs[4 + CHUNKS :]
    copy_prior = pltpu.make_async_copy(prior_hbm, prior_ref, sems.at[3, 0])
    copy_obs = pltpu.make_async_copy(obs_hbm, obs, sems.at[2, 0])
    copy_parent = pltpu.make_async_copy(parent_hbm, parent_ref, sems.at[2, 1])
    copies_w = [pltpu.make_async_copy(mixing_hbm.at[n], w_ref.at[n], sems.at[0, n]) for n in range(nodes)]
    copies_e = [pltpu.make_async_copy(emission_hbm.at[n], tables.at[n], sems.at[1, n]) for n in range(nodes)]
    copy_obs.start()
    copy_parent.start()
    for n in reversed(range(nodes)):
        copies_e[n].start()
        copies_w[n].start()
    copy_prior.start()
    values = tables.shape[1]
    rows = obs.shape[1]
    part = rows // CHUNKS
    for n in range(nodes - 1):
        prods[n] = jnp.ones(prods.shape[1:], F32)
    copy_obs.wait()
    index = lax.broadcasted_iota(jnp.int32, (PAD, rows), 0)
    listed = jnp.zeros((PAD, rows), jnp.int32)
    for n in range(nodes):
        listed = jnp.where(index == n, obs[n : n + 1, :], listed)
    base = (nodes - 1) * rows
    lam_ref[base : base + PAD, :] = jnp.zeros((PAD, lam_ref.shape[1]), BF16)
    lam_ref[base : base + PAD, :rows] = listed.astype(F32).astype(BF16)
    copy_parent.wait()
    for n in reversed(range(nodes)):
        copies_e[n].wait()
        hot = one_hot(obs[n : n + 1, :], values)
        table = tables[n]
        picked = lax.dot_general(hot, table, (((0,), (0,)), ((), ())), preferred_element_type=F32)
        total = jnp.dot(jnp.ones((PAD, values), BF16), table, preferred_element_type=F32)[:1]
        raw = (picked * (1.0 / total)).astype(BF16).astype(F32)
        if n < nodes - 1:
            raw = raw * prods[n]
        if n > 0:
            lam = scaled(raw)
            copies_w[n].wait()
            raw_msg, sums = upward(lam, w_ref[n])
            lam_ref[(n - 1) * rows : n * rows, :] = lam
            msg_ref[n - 1] = raw_msg
            slot = local_slot(parent_ref, n, nodes)
            prods[slot] = prods[slot] * (raw_msg * (1.0 / sums))
        else:
            for c in range(CHUNKS):
                u_refs[c][...] = raw[c * part : (c + 1) * part]
    copies_w[0].wait()
    copy_prior.wait()

    @pl.when(lax.axis_index("leaf") == 0)
    def _():
        root_base(w_ref, prior_ref, base_ref)


def send_up(level, raw_ref, w_ref, send_ref):
    @pl.when(is_lower(level))
    def _():
        raw_msg, sums = upward(scaled(raw_ref[...]), w_ref[0])
        send_ref[...] = (raw_msg * (1.0 / sums)).astype(BF16)


def first_body(u_ref, w_ref, send_ref):
    send_up(0, u_ref, w_ref, send_ref)


def lift_body(level, u_ref, recv_ref, w_ref, u_out, send_ref):
    @pl.when(is_upper(level))
    def _():
        u_out[...] = u_ref[...] * recv_ref[...].astype(F32)

    send_up(level + 1, u_out, w_ref, send_ref)


def root_body(level, u_ref, recv_ref, base_ref, *refs):
    lam_ref, ratio_ref, post_ref = refs[-4:-1] if len(refs) > 3 else refs
    lam = scaled(u_ref[...] * jnp.where(is_upper(level), recv_ref[...].astype(F32), 1.0))
    lam_ref[...] = lam
    if len(refs) > 3:
        for c, block in enumerate([item[...] for item in refs[:-4]] + [lam]):
            refs[-1][c * lam.shape[0] : (c + 1) * lam.shape[0], :] = block

    @pl.when(lax.axis_index("leaf") == 0)
    def _():
        terms = lam.astype(F32) * base_ref[0:1, :]
        inverse = 1.0 / jnp.sum(terms, axis=1, keepdims=True)
        ratio_ref[...] = (base_ref[1:2, :] * inverse).astype(BF16)
        post_ref[...] = (terms * inverse).astype(BF16)


def top_body(lam_ref, w_ref, msg_ref):
    @pl.when(lax.axis_index("leaf") > 0)
    def _():
        msg_ref[...] = lax.dot_general(lam_ref[...], w_ref[0], (((1,), (1,)), ((), ())), preferred_element_type=F32)


def settle_body(level, recv_ref, lam_ref, msg_ref, w_ref, ratio_in, post_in, ratio_ref, post_ref):
    got = is_lower(level)

    @pl.when(got)
    def _():
        ratio, post = downward(recv_ref[...].astype(F32), msg_ref[...], lam_ref[...], w_ref[0])
        ratio_ref[...] = ratio
        post_ref[...] = post

    @pl.when(jnp.logical_not(got))
    def _():
        ratio_ref[...] = ratio_in[...]
        post_ref[...] = post_in[...]


def last_body(nodes, groups, chunk, parent_ref, recv_ref, lam_ref, msg_ref, w_ref, ratio_in, post_in, lams_ref, msgs_ref, *refs):
    packs, posts = refs[:groups], refs[groups]
    rows, part = msgs_ref.shape[1], lam_ref.shape[0]
    share = lam_ref.shape[1] // groups
    got = is_lower(0)

    @pl.when(got)
    def _():
        ratio, post = downward(recv_ref[...].astype(F32), msg_ref[...], lam_ref[...], w_ref[0])
        posts[nodes] = ratio
        posts[0] = post

    @pl.when(jnp.logical_not(got))
    def _():
        posts[nodes] = ratio_in[...]
        posts[0] = post_in[...]

    for n in range(1, nodes):
        q_par = posts[local_slot(parent_ref, n, nodes)].astype(F32)
        low = (n - 1) * rows + chunk * part
        raw_msg = msgs_ref[n - 1, chunk * part : (chunk + 1) * part, :]
        _, posts[n] = downward(q_par, raw_msg, lams_ref[low : low + part, :], w_ref[n])
    own = lax.axis_index("rows")
    for mask in range(groups):
        start = pl.multiple_of(jnp.bitwise_xor(own, mask) * share, share)
        packs[mask][...] = posts[:, :, pl.ds(start, share)]


def ready_body(nodes, groups, *refs):
    lams, hot_ref = refs[:groups], refs[groups]
    chunks, _, merged = hot_ref.shape[1:]
    part = merged // groups
    rows = part * chunks
    values = hot_ref.shape[2]
    base = (nodes - 1) * rows
    for n in range(nodes):
        observed = [lam[base : base + PAD, :rows].astype(F32).astype(jnp.int32)[n : n + 1] for lam in lams]
        for c in range(chunks):
            row = jnp.concatenate([item[:, c * part : (c + 1) * part] for item in observed], axis=1)
            hot_ref[n, c] = one_hot(row, values)


def counts_body(nodes, groups, chunk, parent_ref, w_ref, hot_ref, *refs):
    lams, tops, posts = refs[:groups], refs[groups : 2 * groups], refs[2 * groups : 3 * groups]
    refs = refs[3 * groups :]
    chunks = hot_ref.shape[1]
    part = hot_ref.shape[3] // groups
    rows = part * chunks
    before = refs[:3] if chunk > 0 else None
    refs = refs[3:] if chunk > 0 else refs
    final = chunk == chunks - 1
    copies = []
    if final:
        homes, refs, sems = refs[:2], refs[2:4], refs[4]
        samples = rows * groups
    share = refs[0].shape[1]
    start = pl.multiple_of(lax.axis_index("rows") * share, share)

    def own_message(n, c):
        low = (n - 1) * rows + c * part
        lam = jnp.concatenate([item[low : low + part, :] for item in lams], axis=0)
        weight = w_ref[n, pl.ds(start, share), :]
        return lax.dot_general(lam, weight, (((1,), (1,)), ((), ())), preferred_element_type=F32)

    for n in range(nodes):
        low = (n - 1) * rows + chunk * part if n > 0 else chunk * part
        lam = jnp.concatenate([item[low : low + part, :] for item in (lams if n > 0 else tops)], axis=0)
        if n == 0:
            ratio = jnp.concatenate([item[nodes] for item in posts], axis=0)
        else:
            slot = local_slot(parent_ref, n, nodes)
            q_par = jnp.concatenate([item[slot] for item in posts], axis=0)
            ratio = (q_par.astype(F32) / (own_message(n, chunk) if before is None else before[2][n - 1, chunk - 1])).astype(BF16)
        flow = lax.dot_general(ratio, lam, (((0,), (0,)), ((), ())), preferred_element_type=F32)
        post = jnp.concatenate([item[n] for item in posts], axis=0)
        tally = jnp.dot(hot_ref[n, chunk], post, preferred_element_type=F32)
        if before is not None:
            flow += before[0][n]
            tally += before[1][n]
        if final:
            states, values = flow.shape[1], tally.shape[0]
            weight = w_ref[n, pl.ds(start, share), :].astype(F32)
            flow = weight * flow * (states * states / samples)
            tally = tally * (values * states / samples)
        for k, value in enumerate((flow, tally)):
            refs[k][n] = value.astype(refs[k].dtype)
            if final:
                copies.append(pltpu.make_async_copy(refs[k].at[n], homes[k].at[n], sems.at[k, n]))
                copies[-1].start()
    if before is None:
        for n in range(1, nodes):
            for c in range(1, chunks):
                refs[2][n - 1, c - 1] = own_message(n, c)
    for copy in copies:
        copy.wait()


def swap(value, mask):
    return lax.ppermute(value, "rows", [(s, s ^ mask) for s in range(lax.axis_size("rows"))])


def hold(value, after):
    shape = pltpu.VMEM(value.shape, value.dtype)
    return run(lambda *refs: None, "hold", (value,), (shape,), same={0: 0}, after=after)[0]


def gather(blocks, after=()):
    for bit in reversed(range(lax.axis_size("rows").bit_length() - 1)):
        if 1 << bit in blocks:
            continue
        for place, block in list(blocks.items()):
            blocks[place | (1 << bit)] = swap(hold(block, after) if place and after else block, 1 << bit)
    return [blocks[place] for place in range(len(blocks))]


def far(value):
    half = lax.axis_size("rows") // 2
    return {0: value, half: swap(value, half)} if half else {0: value}


def per_device(mixing, emission, prior, parent, observed):
    nodes, states = mixing.shape[:2]
    rows = observed.shape[1]
    values = emission.shape[1]
    leaves = lax.axis_size("leaf")
    groups = lax.axis_size("rows")
    levels = leaves.bit_length() - 1
    share = states // groups
    part = rows // CHUNKS
    every = range(CHUNKS)
    half = functools.partial(pltpu.VMEM, (part, states))

    outs = run(
        functools.partial(prep_body, nodes),
        "prep",
        tuple(pltpu.with_memory_space_constraint(x, pltpu.HBM) for x in (parent, observed, emission, mixing, prior.reshape(1, states))),
        (
            pltpu.VMEM(mixing.shape, BF16),
            pltpu.VMEM(((nodes - 1) * rows + PAD, states), BF16),
            pltpu.VMEM((nodes - 1, rows, states), F32),
            pltpu.VMEM((8, states), F32),
        )
        + (half(F32),) * CHUNKS,
        (
            pltpu.VMEM((nodes - 1, rows, states), F32),
            pltpu.VMEM(emission.shape, BF16),
            pltpu.VMEM(observed.shape, jnp.int32),
            pltpu.SMEM(parent.shape, jnp.int32),
            pltpu.VMEM((1, states), F32),
            pltpu.SemaphoreType.DMA((4, max(nodes, 2))),
        ),
        [ANY] * 5,
    )
    weights, lams, msgs, base = outs[:4]
    raw, send = list(outs[4:]), []
    for c in every:
        (block,) = run(first_body, "first", (raw[c], weights), (half(BF16),), after=[lams] if c > 0 else ())
        send.append(block)
        if c == 0:
            lams = hold(lams, (block,))

    def up_pairs(level):
        step = 1 << level
        return [(s, s - step) for s in range(leaves) if s % (2 * step) == step]

    def down_pairs(level):
        return [(b, a) for a, b in up_pairs(level)]

    for level in range(levels - 1):
        for c in every:
            recv = lax.ppermute(send[c], "leaf", up_pairs(level))
            raw[c], send[c] = run(
                functools.partial(lift_body, level),
                "lift",
                (raw[c], recv, weights),
                (half(F32), half(BF16)),
                same={0: 0},
                after=send[:c][-1:],
            )
        if level == 0:
            near = far(lams)
    top_lam, top_msg, ratio, post = ([None] * CHUNKS for _ in range(4))
    for c in every:
        recv = lax.ppermute(send[c], "leaf", up_pairs(levels - 1))
        final = c == CHUNKS - 1
        top_lam[c], ratio[c], post[c], *merged = run(
            functools.partial(root_body, levels - 1),
            "root",
            (raw[c], recv, base) + (tuple(top_lam[:c]) if final else ()),
            (half(BF16), half(BF16), half(BF16)) + ((pltpu.VMEM((rows, states), BF16),) if final else ()),
        )
        (top_msg[c],) = run(top_body, "top", (top_lam[c], weights), (half(F32),), work=1.0)
    all_tops = gather(far(merged[0]))
    all_lams = gather(near, send[-1:])
    (hots,) = run(
        functools.partial(ready_body, nodes, groups),
        "ready",
        (*all_lams,),
        (
            pltpu.VMEM((nodes, CHUNKS, values, groups * part), BF16),
        ),
        after=(),
        work=1.0,
    )
    for level in reversed(range(1, levels)):
        for c in every:
            recv = lax.ppermute(post[c], "leaf", down_pairs(level))
            ratio[c], post[c] = run(
                functools.partial(settle_body, level),
                "settle",
                (recv, top_lam[c], top_msg[c], weights, ratio[c], post[c]),
                (half(BF16), half(BF16)),
                after=post[:c][-1:] + (all_lams if level == 1 and c == CHUNKS - 1 else []),
            )
    own_posts = []
    for c in every:
        recv = lax.ppermute(post[c], "leaf", down_pairs(0))
        packs = run(
            functools.partial(last_body, nodes, groups, c),
            "last",
            (parent, recv, top_lam[c], top_msg[c], weights, ratio[c], post[c], lams, msgs),
            (pltpu.VMEM((nodes + 1, part, share), BF16),) * groups,
            (pltpu.VMEM((nodes + 1, part, states), BF16),),
            [SM] + [VM] * 8,
            after=[own_posts[-1][0], *all_tops, hots] if c > 0 else [],
        )
        order = sorted(range(1, groups), reverse=True)
        moved = {mask: swap(packs[mask], mask) for mask in order}
        own_posts.append([packs[0]] + [moved[mask] for mask in range(1, groups)])
    sums = ()
    for c in every:
        final = c == CHUNKS - 1
        ins = (parent, weights, hots, *all_lams, *all_tops, *own_posts[c], *sums)
        shapes = ((nodes, share, states), (nodes, values, share))
        sums = run(
            functools.partial(counts_body, nodes, groups, c),
            "counts",
            ins,
            tuple(jax.ShapeDtypeStruct(x, BF16) if final else pltpu.VMEM(x, F32) for x in shapes)
            + (() if final else (pltpu.VMEM((nodes - 1, CHUNKS - 1, groups * part, share), F32),)),
            tuple(pltpu.VMEM(x, BF16) for x in shapes) + (pltpu.SemaphoreType.DMA((2, nodes)),) if final else (),
            [SM] + [VM] * (len(ins) - 1),
            (ANY, ANY) if final else None,
        )
    return tuple(sums)


def solution(mesh):
    placed = (P("leaf", None, None), P("leaf", None, None), P(), P("leaf"), P("leaf", "rows"))
    return jax.shard_map(
        per_device,
        mesh=mesh,
        in_specs=placed,
        out_specs=(P("leaf", "rows", None), P("leaf", None, "rows")),
        check_vma=False,
    )
```

```python
import functools
import jax
import jax.numpy as jnp
from jax import lax
from jax.experimental import pallas as pl
from jax.experimental.pallas import tpu as pltpu
from jax.sharding import PartitionSpec as P

F32 = jnp.float32
BF16 = jnp.bfloat16
PAD = 16
CHUNKS = 2
WORK = 10**9
LIMIT = 24 * 2**20
VM = pl.BlockSpec(memory_space=pltpu.VMEM)
SM = pl.BlockSpec(memory_space=pltpu.SMEM)
ANY = pl.BlockSpec(memory_space=pl.ANY)


def run(body, name, ins, outs, scratch=(), specs=None, out_specs=None, same=None, after=(), work=1.0):
    count, idle = len(ins), len(ins) + len(after)
    return pl.pallas_call(
        lambda *refs: body(*refs[:count], *refs[idle:]),
        name=name,
        in_specs=(specs or [VM] * count) + [VM] * len(after),
        out_specs=out_specs or tuple(VM for _ in outs),
        out_shape=tuple(outs),
        input_output_aliases=same or {},
        scratch_shapes=list(scratch),
        compiler_params=pltpu.CompilerParams(vmem_limit_bytes=LIMIT),
        cost_estimate=pl.CostEstimate(flops=int(work * WORK), bytes_accessed=2**21, transcendentals=0),
    )(*ins, *after)


def scaled(raw):
    return (raw * (1.0 / jnp.mean(raw, axis=1, keepdims=True))).astype(BF16)


def upward(lam, weight):
    rows = lam.shape[0]
    stacked = jnp.concatenate([lam, jnp.ones((PAD, lam.shape[1]), BF16)], axis=0)
    both = lax.dot_general(stacked, weight, (((1,), (1,)), ((), ())), preferred_element_type=F32)
    return both[:rows], both[rows : rows + 1]


def downward(q_par, raw_msg, lam, weight):
    ratio = (q_par / raw_msg).astype(BF16)
    post = lam.astype(F32) * jnp.dot(ratio, weight, preferred_element_type=F32)
    return ratio, post.astype(BF16)


def one_hot(row, values):
    return (lax.broadcasted_iota(jnp.int32, (values, row.shape[1]), 0) == row).astype(F32).astype(BF16)


def local_slot(parent_ref, node, nodes):
    return jnp.clip(parent_ref[node] - lax.axis_index("leaf") * nodes, 0, node - 1)


def is_upper(level):
    return jnp.bitwise_and(lax.axis_index("leaf"), (2 << level) - 1) == 0


def is_lower(level):
    return jnp.bitwise_and(lax.axis_index("leaf"), (2 << level) - 1) == (1 << level)


def root_base(w_ref, prior_ref, base_ref):
    states = base_ref.shape[1]
    sums = lax.dot_general(jnp.ones((PAD, states), BF16), w_ref[0], (((1,), (1,)), ((), ())), preferred_element_type=F32)
    prior = prior_ref[...]
    odds = (prior / jnp.sum(prior)) / sums[:1]
    high = odds.astype(BF16).astype(F32)
    index = lax.broadcasted_iota(jnp.int32, (PAD, states), 0)
    stacked = jnp.where(index == 0, high, jnp.where(index == 1, odds - high, 0.0)).astype(BF16)
    both = jnp.dot(stacked, w_ref[0], preferred_element_type=F32)
    base_ref[0:1, :] = both[0:1] + both[1:2]
    base_ref[1:2, :] = odds


def prep_body(nodes, parent_hbm, obs_hbm, emission_hbm, mixing_hbm, prior_hbm, *refs):
    w_ref, lam_ref, msg_ref, base_ref = refs[:4]
    u_refs = refs[4 : 4 + CHUNKS]
    prods, tables, obs, parent_ref, prior_ref, sems = refs[4 + CHUNKS :]
    copy_prior = pltpu.make_async_copy(prior_hbm, prior_ref, sems.at[3, 0])
    copy_obs = pltpu.make_async_copy(obs_hbm, obs, sems.at[2, 0])
    copy_parent = pltpu.make_async_copy(parent_hbm, parent_ref, sems.at[2, 1])
    copies_w = [pltpu.make_async_copy(mixing_hbm.at[n], w_ref.at[n], sems.at[0, n]) for n in range(nodes)]
    copies_e = [pltpu.make_async_copy(emission_hbm.at[n], tables.at[n], sems.at[1, n]) for n in range(nodes)]
    copy_obs.start()
    copy_parent.start()
    for n in reversed(range(nodes)):
        copies_e[n].start()
        copies_w[n].start()
    copy_prior.start()
    values = tables.shape[1]
    rows = obs.shape[1]
    part = rows // CHUNKS
    for n in range(nodes - 1):
        prods[n] = jnp.ones(prods.shape[1:], F32)
    copy_obs.wait()
    index = lax.broadcasted_iota(jnp.int32, (PAD, rows), 0)
    listed = jnp.zeros((PAD, rows), jnp.int32)
    for n in range(nodes):
        listed = jnp.where(index == n, obs[n : n + 1, :], listed)
    base = (nodes - 1) * rows
    lam_ref[base : base + PAD, :] = jnp.zeros((PAD, lam_ref.shape[1]), BF16)
    lam_ref[base : base + PAD, :rows] = listed.astype(F32).astype(BF16)
    copy_parent.wait()
    for n in reversed(range(nodes)):
        copies_e[n].wait()
        hot = one_hot(obs[n : n + 1, :], values)
        table = tables[n]
        picked = lax.dot_general(hot, table, (((0,), (0,)), ((), ())), preferred_element_type=F32)
        total = jnp.dot(jnp.ones((PAD, values), BF16), table, preferred_element_type=F32)[:1]
        raw = (picked * (1.0 / total)).astype(BF16).astype(F32)
        if n < nodes - 1:
            raw = raw * prods[n]
        if n > 0:
            lam = scaled(raw)
            copies_w[n].wait()
            raw_msg, sums = upward(lam, w_ref[n])
            lam_ref[(n - 1) * rows : n * rows, :] = lam
            msg_ref[n - 1] = raw_msg
            slot = local_slot(parent_ref, n, nodes)
            prods[slot] = prods[slot] * (raw_msg * (1.0 / sums))
        else:
            for c in range(CHUNKS):
                u_refs[c][...] = raw[c * part : (c + 1) * part]
    copies_w[0].wait()
    copy_prior.wait()

    @pl.when(lax.axis_index("leaf") == 0)
    def _():
        root_base(w_ref, prior_ref, base_ref)


def send_up(level, raw_ref, w_ref, send_ref):
    @pl.when(is_lower(level))
    def _():
        raw_msg, sums = upward(scaled(raw_ref[...]), w_ref[0])
        send_ref[...] = (raw_msg * (1.0 / sums)).astype(BF16)


def first_body(u_ref, w_ref, send_ref):
    send_up(0, u_ref, w_ref, send_ref)


def lift_body(level, u_ref, recv_ref, w_ref, u_out, send_ref):
    @pl.when(is_upper(level))
    def _():
        u_out[...] = u_ref[...] * recv_ref[...].astype(F32)

    send_up(level + 1, u_out, w_ref, send_ref)


def root_body(level, u_ref, recv_ref, base_ref, *refs):
    lam_ref, ratio_ref, post_ref = refs[-4:-1] if len(refs) > 3 else refs
    lam = scaled(u_ref[...] * jnp.where(is_upper(level), recv_ref[...].astype(F32), 1.0))
    lam_ref[...] = lam
    if len(refs) > 3:
        for c, block in enumerate([item[...] for item in refs[:-4]] + [lam]):
            refs[-1][c * lam.shape[0] : (c + 1) * lam.shape[0], :] = block

    @pl.when(lax.axis_index("leaf") == 0)
    def _():
        terms = lam.astype(F32) * base_ref[0:1, :]
        inverse = 1.0 / jnp.sum(terms, axis=1, keepdims=True)
        ratio_ref[...] = (base_ref[1:2, :] * inverse).astype(BF16)
        post_ref[...] = (terms * inverse).astype(BF16)


def top_body(lam_ref, w_ref, msg_ref):
    @pl.when(lax.axis_index("leaf") > 0)
    def _():
        msg_ref[...] = lax.dot_general(lam_ref[...], w_ref[0], (((1,), (1,)), ((), ())), preferred_element_type=F32)


def settle_body(level, recv_ref, lam_ref, msg_ref, w_ref, ratio_in, post_in, ratio_ref, post_ref):
    got = is_lower(level)

    @pl.when(got)
    def _():
        ratio, post = downward(recv_ref[...].astype(F32), msg_ref[...], lam_ref[...], w_ref[0])
        ratio_ref[...] = ratio
        post_ref[...] = post

    @pl.when(jnp.logical_not(got))
    def _():
        ratio_ref[...] = ratio_in[...]
        post_ref[...] = post_in[...]


def last_body(nodes, groups, chunk, parent_ref, recv_ref, lam_ref, msg_ref, w_ref, ratio_in, post_in, lams_ref, msgs_ref, *refs):
    packs, posts = refs[:groups], refs[groups]
    rows, part = msgs_ref.shape[1], lam_ref.shape[0]
    share = lam_ref.shape[1] // groups
    got = is_lower(0)

    @pl.when(got)
    def _():
        ratio, post = downward(recv_ref[...].astype(F32), msg_ref[...], lam_ref[...], w_ref[0])
        posts[nodes] = ratio
        posts[0] = post

    @pl.when(jnp.logical_not(got))
    def _():
        posts[nodes] = ratio_in[...]
        posts[0] = post_in[...]

    for n in range(1, nodes):
        q_par = posts[local_slot(parent_ref, n, nodes)].astype(F32)
        low = (n - 1) * rows + chunk * part
        raw_msg = msgs_ref[n - 1, chunk * part : (chunk + 1) * part, :]
        _, posts[n] = downward(q_par, raw_msg, lams_ref[low : low + part, :], w_ref[n])
    own = lax.axis_index("rows")
    for mask in range(groups):
        start = pl.multiple_of(jnp.bitwise_xor(own, mask) * share, share)
        packs[mask][...] = posts[:, :, pl.ds(start, share)]


def ready_body(nodes, groups, *refs):
    lams, hot_ref = refs[:groups], refs[groups]
    chunks, _, merged = hot_ref.shape[1:]
    part = merged // groups
    rows = part * chunks
    values = hot_ref.shape[2]
    base = (nodes - 1) * rows
    for n in range(nodes):
        observed = [lam[base : base + PAD, :rows].astype(F32).astype(jnp.int32)[n : n + 1] for lam in lams]
        for c in range(chunks):
            row = jnp.concatenate([item[:, c * part : (c + 1) * part] for item in observed], axis=1)
            hot_ref[n, c] = one_hot(row, values)


def counts_body(nodes, groups, chunk, parent_ref, w_ref, hot_ref, *refs):
    lams, tops, posts = refs[:groups], refs[groups : 2 * groups], refs[2 * groups : 3 * groups]
    refs = refs[3 * groups :]
    chunks = hot_ref.shape[1]
    part = hot_ref.shape[3] // groups
    rows = part * chunks
    before = refs[:3] if chunk > 0 else None
    refs = refs[3:] if chunk > 0 else refs
    final = chunk == chunks - 1
    copies = []
    if final:
        homes, refs, sems = refs[:2], refs[2:4], refs[4]
        samples = rows * groups
    share = refs[0].shape[1]
    start = pl.multiple_of(lax.axis_index("rows") * share, share)

    def own_message(n, c):
        low = (n - 1) * rows + c * part
        lam = jnp.concatenate([item[low : low + part, :] for item in lams], axis=0)
        weight = w_ref[n, pl.ds(start, share), :]
        return lax.dot_general(lam, weight, (((1,), (1,)), ((), ())), preferred_element_type=F32)

    for n in range(nodes):
        low = (n - 1) * rows + chunk * part if n > 0 else chunk * part
        lam = jnp.concatenate([item[low : low + part, :] for item in (lams if n > 0 else tops)], axis=0)
        if n == 0:
            ratio = jnp.concatenate([item[nodes] for item in posts], axis=0)
        else:
            slot = local_slot(parent_ref, n, nodes)
            q_par = jnp.concatenate([item[slot] for item in posts], axis=0)
            ratio = (q_par.astype(F32) / (own_message(n, chunk) if before is None else before[2][n - 1, chunk - 1])).astype(BF16)
        flow = lax.dot_general(ratio, lam, (((0,), (0,)), ((), ())), preferred_element_type=F32)
        post = jnp.concatenate([item[n] for item in posts], axis=0)
        tally = jnp.dot(hot_ref[n, chunk], post, preferred_element_type=F32)
        if before is not None:
            flow += before[0][n]
            tally += before[1][n]
        if final:
            states, values = flow.shape[1], tally.shape[0]
            weight = w_ref[n, pl.ds(start, share), :].astype(F32)
            flow = weight * flow * (states * states / samples)
            tally = tally * (values * states / samples)
        for k, value in enumerate((flow, tally)):
            refs[k][n] = value.astype(refs[k].dtype)
            if final:
                copies.append(pltpu.make_async_copy(refs[k].at[n], homes[k].at[n], sems.at[k, n]))
                copies[-1].start()
    if before is None:
        for n in range(1, nodes):
            for c in range(1, chunks):
                refs[2][n - 1, c - 1] = own_message(n, c)
    for copy in copies:
        copy.wait()


def swap(value, mask):
    return lax.ppermute(value, "rows", [(s, s ^ mask) for s in range(lax.axis_size("rows"))])


def hold(value, after):
    shape = pltpu.VMEM(value.shape, value.dtype)
    return run(lambda *refs: None, "hold", (value,), (shape,), same={0: 0}, after=after)[0]


def gather(blocks, after=()):
    for bit in reversed(range(lax.axis_size("rows").bit_length() - 1)):
        if 1 << bit in blocks:
            continue
        for place, block in list(blocks.items()):
            blocks[place | (1 << bit)] = swap(hold(block, after) if place and after else block, 1 << bit)
    return [blocks[place] for place in range(len(blocks))]


def far(value):
    half = lax.axis_size("rows") // 2
    return {0: value, half: swap(value, half)} if half else {0: value}


def per_device(mixing, emission, prior, parent, observed):
    nodes, states = mixing.shape[:2]
    rows = observed.shape[1]
    values = emission.shape[1]
    leaves = lax.axis_size("leaf")
    groups = lax.axis_size("rows")
    levels = leaves.bit_length() - 1
    share = states // groups
    part = rows // CHUNKS
    every = range(CHUNKS)
    half = functools.partial(pltpu.VMEM, (part, states))

    outs = run(
        functools.partial(prep_body, nodes),
        "prep",
        tuple(pltpu.with_memory_space_constraint(x, pltpu.HBM) for x in (parent, observed, emission, mixing, prior.reshape(1, states))),
        (
            pltpu.VMEM(mixing.shape, BF16),
            pltpu.VMEM(((nodes - 1) * rows + PAD, states), BF16),
            pltpu.VMEM((nodes - 1, rows, states), F32),
            pltpu.VMEM((8, states), F32),
        )
        + (half(F32),) * CHUNKS,
        (
            pltpu.VMEM((nodes - 1, rows, states), F32),
            pltpu.VMEM(emission.shape, BF16),
            pltpu.VMEM(observed.shape, jnp.int32),
            pltpu.SMEM(parent.shape, jnp.int32),
            pltpu.VMEM((1, states), F32),
            pltpu.SemaphoreType.DMA((4, max(nodes, 2))),
        ),
        [ANY] * 5,
    )
    weights, lams, msgs, base = outs[:4]
    raw, send = list(outs[4:]), []
    for c in every:
        (block,) = run(first_body, "first", (raw[c], weights), (half(BF16),), after=[lams] if c > 0 else ())
        send.append(block)
        if c == 0:
            lams = hold(lams, (block,))

    def up_pairs(level):
        step = 1 << level
        return [(s, s - step) for s in range(leaves) if s % (2 * step) == step]

    def down_pairs(level):
        return [(b, a) for a, b in up_pairs(level)]

    for level in range(levels - 1):
        for c in every:
            recv = lax.ppermute(send[c], "leaf", up_pairs(level))
            raw[c], send[c] = run(
                functools.partial(lift_body, level),
                "lift",
                (raw[c], recv, weights),
                (half(F32), half(BF16)),
                same={0: 0},
                after=send[:c][-1:],
            )
        if level == 0:
            near = far(lams)
    top_lam, top_msg, ratio, post = ([None] * CHUNKS for _ in range(4))
    for c in every:
        recv = lax.ppermute(send[c], "leaf", up_pairs(levels - 1))
        final = c == CHUNKS - 1
        top_lam[c], ratio[c], post[c], *merged = run(
            functools.partial(root_body, levels - 1),
            "root",
            (raw[c], recv, base) + (tuple(top_lam[:c]) if final else ()),
            (half(BF16), half(BF16), half(BF16)) + ((pltpu.VMEM((rows, states), BF16),) if final else ()),
        )
        (top_msg[c],) = run(top_body, "top", (top_lam[c], weights), (half(F32),), work=1.0)
    all_tops = gather(far(merged[0]))
    all_lams = gather(near, send[-1:])
    (hots,) = run(
        functools.partial(ready_body, nodes, groups),
        "ready",
        (*all_lams,),
        (
            pltpu.VMEM((nodes, CHUNKS, values, groups * part), BF16),
        ),
        after=(),
        work=1.0,
    )
    for level in reversed(range(1, levels)):
        for c in every:
            recv = lax.ppermute(post[c], "leaf", down_pairs(level))
            ratio[c], post[c] = run(
                functools.partial(settle_body, level),
                "settle",
                (recv, top_lam[c], top_msg[c], weights, ratio[c], post[c]),
                (half(BF16), half(BF16)),
                after=post[:c][-1:] + (all_lams if level == 1 and c == CHUNKS - 1 else []),
            )
    own_posts = []
    for c in every:
        recv = lax.ppermute(post[c], "leaf", down_pairs(0))
        packs = run(
            functools.partial(last_body, nodes, groups, c),
            "last",
            (parent, recv, top_lam[c], top_msg[c], weights, ratio[c], post[c], lams, msgs),
            (pltpu.VMEM((nodes + 1, part, share), BF16),) * groups,
            (pltpu.VMEM((nodes + 1, part, states), BF16),),
            [SM] + [VM] * 8,
            after=[own_posts[-1][0], *all_tops, hots] if c > 0 else [],
        )
        order = sorted(range(1, groups), reverse=c == CHUNKS - 1)
        moved = {mask: swap(packs[mask], mask) for mask in order}
        own_posts.append([packs[0]] + [moved[mask] for mask in range(1, groups)])
    sums = ()
    for c in every:
        final = c == CHUNKS - 1
        ins = (parent, weights, hots, *all_lams, *all_tops, *own_posts[c], *sums)
        shapes = ((nodes, share, states), (nodes, values, share))
        sums = run(
            functools.partial(counts_body, nodes, groups, c),
            "counts",
            ins,
            tuple(jax.ShapeDtypeStruct(x, BF16) if final else pltpu.VMEM(x, F32) for x in shapes)
            + (() if final else (pltpu.VMEM((nodes - 1, CHUNKS - 1, groups * part, share), F32),)),
            tuple(pltpu.VMEM(x, BF16) for x in shapes) + (pltpu.SemaphoreType.DMA((2, nodes)),) if final else (),
            [SM] + [VM] * (len(ins) - 1),
            (ANY, ANY) if final else None,
        )
    return tuple(sums)


def solution(mesh):
    placed = (P("leaf", None, None), P("leaf", None, None), P(), P("leaf"), P("leaf", "rows"))
    return jax.shard_map(
        per_device,
        mesh=mesh,
        in_specs=placed,
        out_specs=(P("leaf", "rows", None), P("leaf", None, "rows")),
        check_vma=False,
    )
```
